32 devices in a mesh: seq: 4 (over x, core), vocab: 8 (over z, y).
Axes of the slice: x: 2, y: 2, z: 4, core: 2. Of those that a mesh axis runs over, the one named last changes fastest.
Arguments:
- hidden: bfloat16 [512, 8192], P('seq'), may hold values from -6 to 6
- steer: float32 [8192], replicated, may hold values from -4 to 4
- tangent: float32 [8192], replicated, may hold values from -6 to 6
- gain: float32 [8192], replicated, may hold values from 0.5 to 1.5
- head: bfloat16 [8192, 19456], P('seq', 'vocab'), may hold values from -0.198873782 to 0.198873782
- target: bfloat16 [512, 19456], P('seq', 'vocab'), may hold values from 0.099609375 to 10
Outputs:
- gradient: float32 [512, 8192], P('vocab', 'seq')
- curvature: float32 [512, 8192], P('vocab', 'seq')
The draws below stay inside these ranges and needn't reach their ends.
All inputs are finite; a program needn't handle non-finite values.
Results may differ from the reference program's by a relative error of at most 0.0082.
Values may be sent and summed in bfloat16 or wider, within the bound.
No kernel may reach another device: no remote copies, remote signals or barrier semaphores. Data moves between devices by JAX's collectives and lax.ppermute only.
A program may use at most 128 MiB of HBM per device.

```python
import math
import jax
import jax.numpy as jnp
from jax import lax

D = 8192
VOCAB = 19456
TOKENS = 512


def draw_hidden(key, part):
    values = jnp.clip(jax.random.normal(key, (TOKENS, D), jnp.float32), -6.0, 6.0)
    return values.astype(jnp.bfloat16)


def draw_head(key, part):
    spread = 3.0 / math.sqrt(D)
    values = jnp.clip(jax.random.normal(jax.random.fold_in(key, 5), (D, VOCAB), jnp.float32), -6.0, 6.0) * spread
    return values.astype(jnp.bfloat16)


def steps_of(stream_key, extent, split, least, high):
    factor_of, own = 1.0, jax.random.fold_in(stream_key, 6)
    for position, blocks in split:
        draws = jnp.exp(jax.random.uniform(jax.random.fold_in(own, position), (blocks,), jnp.float32, least / len(split), high / len(split)))
        factor_of = factor_of * jnp.repeat(draws, extent[position] // blocks).reshape([-1 if axis == position else 1 for axis in range(len(extent))])
    return factor_of


def gaussian(stream_key, shape, deviation, bound, kind=jnp.bfloat16):
    return jnp.clip(deviation * jax.random.normal(stream_key, shape, jnp.float32), -bound, bound).astype(kind)


def setup_inputs(seed: int = 0) -> dict:
    splits = jax.random.split(jax.random.key(seed), 7)
    return {
        "hidden": draw_hidden(jax.random.fold_in(splits[6], 71), 0),
        "steer": gaussian(splits[1], (D,), 0.3, 4.0, jnp.float32),
        "tangent": gaussian(splits[2], (D,), 1.0, 6.0, jnp.float32),
        "gain": jnp.clip(1.0 + 0.1 * jax.random.normal(splits[3], (D,), jnp.float32), 0.5, 1.5),
        "head": draw_head(jax.random.fold_in(splits[6], 71), 0),
        "target": jnp.clip(jnp.exp(math.log(10.0) - 4.609084 * jax.random.uniform(splits[5], (TOKENS, VOCAB), jnp.float32) ** steps_of(splits[5], (TOKENS, VOCAB), ((0, 4), (1, 8)), -0.2, 0.2)), 0.099609375, 10.0).astype(jnp.bfloat16),
    }


EPSILON = 1e-06

def reference(hidden, steer, tangent, gain, head, target):
    inputs = hidden.astype(jnp.float32) + steer
    feature_count = inputs.shape[1]
    meansq = lax.optimization_barrier(jnp.sum(inputs * inputs, axis=1)) / feature_count
    denominator = meansq + EPSILON
    radius = jnp.sqrt(denominator)
    tangent_dot = lax.optimization_barrier(jnp.sum(inputs * tangent, axis=1)) / feature_count
    normed = (gain * inputs / radius[:, None]).astype(jnp.bfloat16)
    tangent_normed = (gain * (tangent - inputs * (tangent_dot / denominator)[:, None]) / radius[:, None]).astype(jnp.bfloat16)
    logits = jnp.dot(normed, head, preferred_element_type=jnp.float32)
    dlogits = jnp.dot(tangent_normed, head, preferred_element_type=jnp.float32)
    row_peak = lax.optimization_barrier(jnp.max(logits, axis=1, keepdims=True))
    exponent = jnp.exp(logits - row_peak)
    row_total = lax.optimization_barrier(jnp.sum(exponent, axis=1))
    softmax_probs = exponent / row_total[:, None]
    mean_shift = lax.optimization_barrier(jnp.sum(exponent * dlogits, axis=1)) / row_total
    weights = target.astype(jnp.float32)
    target_probs = weights / lax.optimization_barrier(jnp.sum(weights, axis=1))[:, None]
    cot_grad = (softmax_probs - target_probs).astype(jnp.bfloat16)
    cot_ggn = (softmax_probs * (dlogits - mean_shift[:, None])).astype(jnp.bfloat16)
    dims = (((1,), (1,)), ((), ()))
    back_grad = lax.dot_general(cot_grad, head, dims, preferred_element_type=jnp.float32)
    back_ggn = lax.dot_general(cot_ggn, head, dims, preferred_element_type=jnp.float32)

    def norm_back(upstream):
        scaled = gain * upstream
        dotted = lax.optimization_barrier(jnp.sum(inputs * scaled, axis=1)) / feature_count
        return (scaled - inputs * (dotted / denominator)[:, None]) / radius[:, None]
    return (norm_back(back_grad), norm_back(back_ggn))
```

```python
import jax
import jax.numpy as jnp
from jax import lax
from jax.sharding import PartitionSpec as P

EPSILON = 1e-06
ROWS_BY_ROWS = (((1,), (1,)), ((), ()))


def swap(value, axis, bit, size):
    return lax.ppermute(value, axis, [(i, i ^ bit) for i in range(size)])


def shift(value, axis, pairs):
    return lax.ppermute(value, axis, pairs)


def chain_scatter(parts, place, length, pair):
    def right(step):
        return [
            (z * pair + y, (z + 1) * pair + y)
            for z in range(length - 1)
            for y in range(pair)
            if z < step
        ]

    def left(step):
        return [
            ((length - 1 - z) * pair + y, (length - 2 - z) * pair + y)
            for z in range(length - 1)
            for y in range(pair)
            if z < step
        ]

    going_up = going_down = None
    for step in range(1, length):
        up = lax.dynamic_index_in_dim(parts, length - step + place, 0, False)
        down = lax.dynamic_index_in_dim(parts, step - length + place, 0, False)
        if step > 1:
            up = up + going_up.astype(jnp.float32)
            down = down + going_down.astype(jnp.float32)
        going_up = shift(up.astype(jnp.bfloat16), "vocab", right(step))
        going_down = shift(down.astype(jnp.bfloat16), "vocab", left(step))
    own = lax.dynamic_index_in_dim(parts, place, 0, False)
    return own + going_up.astype(jnp.float32) + going_down.astype(jnp.float32)


def vocab_scatter(partial, seq_index, vocab_index, vocab_size):
    blocks, rows, features = partial.shape
    pair = 2
    length = vocab_size // pair
    share = blocks * rows // vocab_size
    cut = partial.reshape(blocks, length // blocks, pair, share, features)
    mine_y = vocab_index % pair
    theirs = lax.dynamic_index_in_dim(cut, 1 - mine_y, 2, False).astype(jnp.bfloat16)
    got = swap(theirs, "vocab", 1, vocab_size)
    kept = lax.dynamic_index_in_dim(cut, mine_y, 2, False) + got.astype(jnp.float32)
    order = jnp.bitwise_xor(jnp.arange(blocks), seq_index)
    kept = jnp.take(kept, order, axis=0).reshape(length, share, features)
    return chain_scatter(kept, vocab_index // pair, length, pair)


def body(hidden, steer, tangent, gain, head, target):
    seq_size = lax.axis_size("seq")
    vocab_size = lax.axis_size("vocab")
    seq_index = lax.axis_index("seq")
    vocab_index = lax.axis_index("vocab")
    tokens, feature_count = hidden.shape
    width = head.shape[0]
    float32, bfloat16 = jnp.float32, jnp.bfloat16

    blocks = []
    for bit in range(seq_size):
        cut = lax.dynamic_slice_in_dim(hidden, (seq_index ^ bit) * width, width, 1)
        blocks.append(cut if bit == 0 else swap(cut, "seq", bit, seq_size))

    inputs = hidden.astype(float32) + steer
    sums = jnp.stack([jnp.sum(inputs * inputs, axis=1), jnp.sum(inputs * tangent, axis=1)])
    all_sums = jnp.stack(
        [sums if bit == 0 else swap(sums, "seq", bit, seq_size) for bit in range(seq_size)], axis=1
    )
    denominator = all_sums[0] / feature_count + EPSILON
    radius = jnp.sqrt(denominator)
    slope = all_sums[1] / feature_count / denominator

    offset = seq_index * width
    steer_part = lax.dynamic_slice_in_dim(steer, offset, width)
    tangent_part = lax.dynamic_slice_in_dim(tangent, offset, width)
    gain_part = lax.dynamic_slice_in_dim(gain, offset, width)

    line = gain_part * tangent_part
    high = line.astype(bfloat16)
    low = (line - high.astype(float32)).astype(bfloat16)
    two = jnp.concatenate(
        [high[None], low[None], jnp.zeros((14, width), bfloat16)], axis=0
    )
    row = jnp.sum(jnp.dot(two, head, preferred_element_type=float32), axis=0)
    tangent_row = row
    for bit in range(1, seq_size):
        tangent_row = tangent_row + swap(row, "seq", bit, seq_size)

    def partial_logits(bit):
        values = blocks[bit].astype(float32) + steer_part
        normed = (gain_part * values / radius[bit][:, None]).astype(bfloat16)
        return jnp.dot(normed, head, preferred_element_type=float32)

    logits = [None] * 4
    sums_of = {}
    got_of = {}
    for base in (0, 2):
        kept = partial_logits(base)
        given = partial_logits(base + 1)
        whole = kept + swap(given, "seq", 1, seq_size)
        sums_of[base] = whole
        got_of[base ^ 2] = swap(whole.astype(jnp.float16), "seq", 2, seq_size)
    for base in (2, 0):
        full = sums_of[base] + got_of[base].astype(float32)
        logits[base] = full
        logits[base + 1] = swap(full, "seq", 1, seq_size)
    logits = jnp.stack(logits)

    target_1 = swap(target, "seq", 1, seq_size)
    target_2 = swap(target, "seq", 2, seq_size)
    target_3 = swap(target_2, "seq", 1, seq_size)
    weights = jnp.stack([target, target_1, target_2, target_3])

    peak = jnp.max(logits, axis=2)
    below = logits - peak[..., None]
    exponent = jnp.exp(below)
    dlogits = tangent_row / radius[..., None] - logits * slope[..., None]
    total = jnp.sum(exponent, axis=2)
    shift_mean = jnp.sum(exponent * dlogits, axis=2) / total
    tilted = exponent * (dlogits - shift_mean[..., None])
    total_below = jnp.sum(exponent * below, axis=2)
    tilted_below = jnp.sum(tilted * below, axis=2)
    wide = weights.astype(float32)
    weight_sum = jnp.sum(wide, axis=2)
    weight_logits = jnp.sum(wide * logits, axis=2)

    stats = lax.all_gather(
        jnp.stack([peak, total, shift_mean, total_below, tilted_below, weight_sum, weight_logits]),
        "vocab",
    )
    peaks, totals, means, belows, tilts, weight_sums, weight_lines = (
        stats[:, i] for i in range(7)
    )
    row_peak = jnp.max(peaks, axis=0)
    factor = jnp.exp(peaks - row_peak)
    row_total = jnp.sum(factor * totals, axis=0)
    mean_shift = jnp.sum(factor * totals * means, axis=0) / row_total
    first = belows + peaks * totals
    weight_total = jnp.sum(weight_sums, axis=0)
    dot_grad = (
        jnp.sum(factor * first, axis=0) / row_total - jnp.sum(weight_lines, axis=0) / weight_total
    )
    dot_ggn = jnp.sum(factor * (tilts + (means - mean_shift) * first), axis=0) / row_total
    scale = jnp.exp(peak - row_peak) / row_total
    lean = scale * (shift_mean - mean_shift)

    rows = seq_size * tokens

    def back(cotangent):
        flat = cotangent.astype(bfloat16).reshape(rows, -1)
        out = lax.dot_general(flat, head, ROWS_BY_ROWS, preferred_element_type=float32)
        return out.reshape(seq_size, tokens, width)

    back_plain = back(exponent)
    back_tilted = back(tilted)
    back_weights = back(weights)
    ggn = scale[..., None] * back_tilted + lean[..., None] * back_plain
    ggn_mine = vocab_scatter(ggn, seq_index, vocab_index, vocab_size)
    grad = scale[..., None] * back_plain - back_weights / weight_total[..., None]
    grad_mine = vocab_scatter(grad, seq_index, vocab_index, vocab_size)

    share = rows // vocab_size
    owner = vocab_index * share // tokens
    inner = vocab_index * share - owner * tokens
    block = jnp.bitwise_xor(owner, seq_index)

    def mine(values):
        return lax.dynamic_slice(values, (block, inner), (1, share))[0]

    my_hidden = lax.dynamic_slice(jnp.stack(blocks), (block, inner, 0), (1, share, width))[0]
    my_inputs = my_hidden.astype(float32) + steer_part
    my_radius, my_denominator = mine(radius), mine(denominator)

    def norm_back(upstream, dotted):
        along = dotted * my_radius / feature_count / my_denominator
        return (gain_part * upstream - my_inputs * along[:, None]) / my_radius[:, None]

    return norm_back(grad_mine, mine(dot_grad)), norm_back(ggn_mine, mine(dot_ggn))


def solution(mesh):
    return jax.shard_map(
        body,
        mesh=mesh,
        in_specs=(P("seq", None), P(), P(), P(), P("seq", "vocab"), P("seq", "vocab")),
        out_specs=(P("vocab", "seq"), P("vocab", "seq")),
        check_vma=False,
    )
```

```python
import functools

import jax
import jax.numpy as jnp
from jax import lax
from jax.experimental import pallas as pl
from jax.experimental.pallas import tpu as pltpu
from jax.sharding import PartitionSpec as P

EPSILON = 1e-06
NT = (((1,), (1,)), ((), ()))
QUARTERS = 4
PAIR = 2
F32, BF16 = jnp.float32, jnp.bfloat16
VMEM_BYTES = 48 * 1024 * 1024


def params():
    return pltpu.CompilerParams(vmem_limit_bytes=VMEM_BYTES)


def whole_spec():
    return pl.BlockSpec(memory_space=pltpu.VMEM)


def smem_spec():
    return pl.BlockSpec(memory_space=pltpu.SMEM)


def swap(value, axis, bit, size):
    return lax.ppermute(value, axis, [(i, i ^ bit) for i in range(size)])


def lanes(columns, rows):
    lane = lax.broadcasted_iota(jnp.int32, (rows, 128), 1)
    tile = jnp.zeros((rows, 128), F32)
    for index, column in enumerate(columns):
        tile = jnp.where(lane == index, column, tile)
    return tile


def turn(rows8):
    return jnp.concatenate([rows8, jnp.zeros((120, 128), F32)], axis=0).T


def cut_kernel(width, seq_size, at, hidden, vectors, *outs):
    own, mate, near_2, near_3, far_2, far_3, sums, parts, two = outs
    seq_index, group = at[0], at[1]
    rows = hidden.shape[0]
    size = rows // QUARTERS

    def quarter(place):
        return pl.ds(pl.multiple_of((place ^ group) * size, size), size)

    def features(bit):
        return pl.ds(pl.multiple_of((seq_index ^ bit) * width, width), width)

    near_2[...] = hidden[quarter(0), features(2)]
    near_3[...] = hidden[quarter(0), features(3)]
    far_2[...] = hidden[quarter(3), features(2)]
    far_3[...] = hidden[quarter(3), features(3)]
    steer, tangent = vectors[0:1, :], vectors[1:2, :]
    columns = []
    for place in range(QUARTERS):
        spot = pl.ds(place * size, size)
        own[spot, :] = hidden[quarter(place), features(0)]
        mate[spot, :] = hidden[quarter(place), features(1)]
        inputs = hidden[quarter(place), :].astype(F32) + steer
        columns.append(
            lanes(
                [
                    jnp.sum(inputs * inputs, axis=1, keepdims=True),
                    jnp.sum(inputs * tangent, axis=1, keepdims=True),
                ],
                size,
            )
        )
    sums[...] = jnp.concatenate(columns, axis=0).T[:8]
    mine = vectors[:, features(0)]
    parts[...] = mine
    line = mine[1:2] * mine[2:3]
    high = line.astype(BF16).astype(F32)
    two[...] = jnp.concatenate(
        [high, line - high, jnp.zeros((14, width), F32)], axis=0
    ).astype(BF16)


def cut(at, hidden, vectors, width, seq_size):
    rows = hidden.shape[0]
    piece = jax.ShapeDtypeStruct((rows // QUARTERS, width), BF16)
    block = jax.ShapeDtypeStruct((rows, width), BF16)
    return pl.pallas_call(
        functools.partial(cut_kernel, width, seq_size),
        in_specs=[smem_spec(), whole_spec(), whole_spec()],
        out_specs=[whole_spec()] * 9,
        out_shape=[
            block,
            block,
            piece,
            piece,
            piece,
            piece,
            jax.ShapeDtypeStruct((8, rows), F32),
            jax.ShapeDtypeStruct((vectors.shape[0], width), F32),
            jax.ShapeDtypeStruct((16, width), BF16),
        ],
        compiler_params=params(),
    )(at, hidden, vectors)


def soften_kernel(feature_count, at, first, second, row, sums_a, sums_b, *outs):
    exponent_out, tilted_out, logits_out, stats, tile = outs
    tokens = first.shape[0]
    count = at.shape[0]
    size = 2 * tokens // count
    line = row[0:1, :]
    for block, (source, sums) in enumerate(((first, sums_a), (second, sums_b))):
        turned = turn(sums[...])
        denominator = turned[:, 0:1] / feature_count + EPSILON
        inverse = 1.0 / jnp.sqrt(denominator)
        slope = turned[:, 1:2] / feature_count / denominator
        for piece in range(count // 2):
            begin = piece * size
            logits = source[begin : begin + size, :]
            spot = pl.ds(pl.multiple_of(at[block * (count // 2) + piece], size), size)
            logits_out[spot, :] = logits
            peak = jnp.max(logits, axis=1, keepdims=True)
            below = logits - peak
            exponent = jnp.exp(below)
            dlogits = line * inverse[begin : begin + size] - logits * slope[begin : begin + size]
            total = jnp.sum(exponent, axis=1, keepdims=True)
            mean = jnp.sum(exponent * dlogits, axis=1, keepdims=True) / total
            tilted = exponent * (dlogits - mean)
            under = jnp.sum(exponent * below, axis=1, keepdims=True)
            tilted_under = jnp.sum(tilted * below, axis=1, keepdims=True)
            exponent_out[spot, :] = exponent.astype(BF16)
            tilted_out[spot, :] = tilted.astype(BF16)
            tile[spot, :] = lanes(
                [peak, total, mean, under + peak * total, tilted_under], size
            )
    for begin in range(0, 2 * tokens, 128):
        stats[:, begin : begin + 128] = tile[begin : begin + 128, :].T[:8]


def soften(at, first, second, row, sums_a, sums_b, feature_count):
    tokens, width = first.shape
    rows = 2 * tokens
    return pl.pallas_call(
        functools.partial(soften_kernel, feature_count),
        in_specs=[smem_spec()] + [whole_spec()] * 5,
        out_specs=[whole_spec()] * 4,
        out_shape=[
            jax.ShapeDtypeStruct((rows, width), BF16),
            jax.ShapeDtypeStruct((rows, width), BF16),
            jax.ShapeDtypeStruct((rows, width), F32),
            jax.ShapeDtypeStruct((8, rows), F32),
        ],
        scratch_shapes=[pltpu.VMEM((rows, 128), F32)],
        compiler_params=params(),
        cost_estimate=pl.CostEstimate(
            flops=30 * rows * width, bytes_accessed=12 * rows * width, transcendentals=rows * width
        ),
    )(at, first, second, row, sums_a, sums_b)


def weigh_kernel(at, *refs):
    blocks, (logits_own, logits_other), (ordered_own, ordered_other, stats, tile) = (
        refs[:4],
        refs[4:6],
        refs[6:],
    )
    tokens = blocks[0].shape[0]
    count = at.shape[0]
    size = 4 * tokens // count
    half = 2 * tokens
    for block in range(4):
        logits, ordered = (
            (logits_own, ordered_own) if block < 2 else (logits_other, ordered_other)
        )
        for piece in range(count // 4):
            begin = piece * size
            value = blocks[block][begin : begin + size, :]
            place = pl.multiple_of(at[block * (count // 4) + piece], size)
            spot = pl.ds(place, size)
            ordered[spot, :] = value
            wide = value.astype(F32)
            tile[pl.ds(place + half * (block // 2), size), :] = lanes(
                [
                    jnp.sum(wide, axis=1, keepdims=True),
                    jnp.sum(wide * logits[spot, :], axis=1, keepdims=True),
                ],
                size,
            )
    for begin in range(0, 2 * half, 128):
        stats[:, begin : begin + 128] = tile[begin : begin + 128, :].T[:8]


def weigh(at, blocks, logits_own, logits_other):
    tokens, width = blocks[0].shape
    rows = 2 * tokens
    return pl.pallas_call(
        weigh_kernel,
        in_specs=[smem_spec()] + [whole_spec()] * 6,
        out_specs=[whole_spec()] * 3,
        out_shape=[
            jax.ShapeDtypeStruct((rows, width), BF16),
            jax.ShapeDtypeStruct((rows, width), BF16),
            jax.ShapeDtypeStruct((8, 2 * rows), F32),
        ],
        scratch_shapes=[pltpu.VMEM((2 * rows, 128), F32)],
        compiler_params=params(),
        cost_estimate=pl.CostEstimate(
            flops=8 * rows * width, bytes_accessed=16 * rows * width, transcendentals=0
        ),
    )(at, *blocks, logits_own, logits_other)


def matmul_cost(rows, width, features, extra):
    return pl.CostEstimate(
        flops=2 * rows * width * features,
        bytes_accessed=2 * width * (rows + features) + extra,
        transcendentals=0,
    )


def plain_kernel(cotangent, head, out):
    out[...] = lax.dot_general(cotangent[...], head[...], NT, preferred_element_type=F32)


def tile_of(features):
    return 256 if features % 256 == 0 else features


def back_plain(cotangent, head):
    rows, width = cotangent.shape
    features = head.shape[0]
    tile = tile_of(features)
    return pl.pallas_call(
        plain_kernel,
        grid=(features // tile,),
        in_specs=[
            pl.BlockSpec((rows, width), lambda i: (0, 0)),
            pl.BlockSpec((tile, width), lambda i: (i, 0)),
        ],
        out_specs=pl.BlockSpec((rows, tile), lambda i: (0, i)),
        out_shape=jax.ShapeDtypeStruct((rows, features), F32),
        compiler_params=params(),
        cost_estimate=matmul_cost(rows, width, features, 4 * rows * features),
    )(cotangent, head)


def aligned(value, bit):
    if bit % 2 == 0:
        return value
    half = value.shape[1] // 2
    return jnp.concatenate([value[:, half:], value[:, :half]], axis=1)


def columns_of(rows8, out):
    for begin in range(0, rows8.shape[1], 128):
        out[begin : begin + 128, :] = turn(rows8[:, begin : begin + 128])


def stack8(rows):
    pad = jnp.zeros((8 - len(rows), rows[0].shape[1]), F32)
    return jnp.concatenate(rows + [pad], axis=0)


def tilted_kernel(count, cotangent, head, plain, *refs):
    stats, (theirs, kept, joint, columns) = refs[:count], refs[count:]

    @pl.when(pl.program_id(0) == 0)
    def _():
        values = [aligned(stats[bit][...], bit) for bit in range(count)]
        own = values[0]
        row_peak = functools.reduce(jnp.maximum, [value[0:1] for value in values])
        factors = [jnp.exp(value[0:1] - row_peak) for value in values]
        total = sum(f * value[1:2] for f, value in zip(factors, values))
        mean = sum(f * value[1:2] * value[2:3] for f, value in zip(factors, values)) / total
        line = sum(f * value[3:4] for f, value in zip(factors, values)) / total
        tilt = (
            sum(
                f * (value[4:5] + (value[2:3] - mean) * value[3:4])
                for f, value in zip(factors, values)
            )
            / total
        )
        scale = factors[0] / total
        found = stack8([scale, scale * (own[2:3] - mean), line, tilt])
        joint[...] = found
        columns_of(found, columns)

    product = lax.dot_general(cotangent[...], head[...], NT, preferred_element_type=F32)
    result = columns[:, 0:1] * product + columns[:, 1:2] * plain[...]
    half = result.shape[0] // 2
    kept[...] = result[:half]
    theirs[...] = result[half:].astype(BF16)


def weights_kernel(count, cotangent, head, plain, joint, *refs):
    stats, (theirs, kept, sums, columns) = refs[:count], refs[count:]

    @pl.when(pl.program_id(0) == 0)
    def _():
        values = [aligned(stats[bit][...], bit) for bit in range(count)]
        total = sum(value[0:1] for value in values)
        line = sum(value[1:2] for value in values)
        found = stack8([joint[0:1, :], 1.0 / total, line / total])
        sums[...] = found
        columns_of(found, columns)

    product = lax.dot_general(cotangent[...], head[...], NT, preferred_element_type=F32)
    result = columns[:, 0:1] * plain[...] - columns[:, 1:2] * product
    half = result.shape[0] // 2
    kept[...] = result[:half]
    theirs[...] = result[half:].astype(BF16)


def back_scaled(kernel, cotangent, head, plain, first, stats):
    rows, width = cotangent.shape
    features = head.shape[0]
    tile = tile_of(features)
    small = pl.BlockSpec((8, rows), lambda i: (0, 0))
    return pl.pallas_call(
        functools.partial(kernel, len(stats)),
        grid=(features // tile,),
        in_specs=[
            pl.BlockSpec((rows, width), lambda i: (0, 0)),
            pl.BlockSpec((tile, width), lambda i: (i, 0)),
            pl.BlockSpec((rows, tile), lambda i: (0, i)),
        ]
        + [small] * (len(first) + len(stats)),
        out_specs=[
            pl.BlockSpec((rows // 2, tile), lambda i: (0, i)),
            pl.BlockSpec((rows // 2, tile), lambda i: (0, i)),
            small,
        ],
        out_shape=[
            jax.ShapeDtypeStruct((rows // 2, features), BF16),
            jax.ShapeDtypeStruct((rows // 2, features), F32),
            jax.ShapeDtypeStruct((8, rows), F32),
        ],
        scratch_shapes=[pltpu.VMEM((rows, 128), F32)],
        compiler_params=params(),
        cost_estimate=matmul_cost(rows, width, features, 7 * rows * features),
    )(cotangent, head, plain, *first, *stats)


def chain_scatter(part, place, length):
    def right(step):
        return [
            (z * PAIR + y, (z + 1) * PAIR + y)
            for z in range(length - 1)
            for y in range(PAIR)
            if z < step
        ]

    def left(step):
        return [
            ((length - 1 - z) * PAIR + y, (length - 2 - z) * PAIR + y)
            for z in range(length - 1)
            for y in range(PAIR)
            if z < step
        ]

    going_up = going_down = None
    for step in range(1, length):
        up = part(jnp.minimum(length - step + place, length - 1))
        down = part(jnp.maximum(step - length + place, 0))
        if step > 1:
            up = up + going_up.astype(F32)
            down = down + going_down.astype(F32)
        going_up = lax.ppermute(up.astype(BF16), "vocab", right(step))
        going_down = lax.ppermute(down.astype(BF16), "vocab", left(step))
    return part(place) + going_up.astype(F32) + going_down.astype(F32)


def body(hidden, steer, tangent, gain, head, target):
    seq_size = lax.axis_size("seq")
    vocab_size = lax.axis_size("vocab")
    seq_index = lax.axis_index("seq")
    vocab_index = lax.axis_index("vocab")
    tokens, feature_count = hidden.shape
    width = head.shape[0]
    rows = seq_size * tokens
    share = rows // vocab_size
    quarter = tokens // QUARTERS
    size = min(share, quarter)
    y, z = vocab_index % PAIR, vocab_index // PAIR
    length = vocab_size // PAIR
    chip = seq_index // 2
    group = 2 * y + z % 2

    def destination(block, begin):
        row = (block % 2) * tokens + begin
        owner, inside = row // share, row % share
        return ((owner % PAIR) ^ y) * tokens + owner // PAIR * share + inside

    starts = jnp.arange(tokens // size) * size
    turned = ((starts // quarter) ^ group) * quarter + starts % quarter

    def places(bits, begins):
        return jnp.concatenate(
            [destination(seq_index ^ bit, begins) for bit in bits]
        ).astype(jnp.int32)

    own_places, other_places = places((0, 1), turned), places((2, 3), turned)
    target_places = places((0, 1, 2, 3), starts)

    at = jnp.stack([seq_index, group]).astype(jnp.int32)
    vectors = jnp.stack([steer, tangent, gain])
    own, mate, near_2, near_3, far_2, far_3, sums_0, parts, two = cut(
        at, hidden, vectors, width, seq_size
    )
    near = jnp.stack([swap(near_2, "seq", 2, seq_size), swap(near_3, "seq", 3, seq_size)])
    mate = swap(mate, "seq", 1, seq_size)
    sums = [sums_0] + [swap(sums_0, "seq", bit, seq_size) for bit in range(1, seq_size)]
    by_y = swap(near, "vocab", 2, vocab_size)
    by_z = swap(near, "vocab", 1, vocab_size)
    far = [swap(far_2, "seq", 2, seq_size), swap(far_3, "seq", 3, seq_size)]
    blocks = [own, mate] + [
        jnp.concatenate([near[i], by_y[i], by_z[i], far[i]], axis=0) for i in range(2)
    ]
    steer_part, gain_part = parts[0], parts[2]

    row = jnp.sum(jnp.dot(two, head, preferred_element_type=F32), axis=0, keepdims=True)
    tangent_row = row
    for bit in range(1, seq_size):
        tangent_row = tangent_row + swap(row, "seq", bit, seq_size)

    denominators = [s[0] / feature_count + EPSILON for s in sums]
    radii = [jnp.sqrt(d) for d in denominators]

    def partial_logits(bit):
        values = blocks[bit].astype(F32) + steer_part
        normed = (gain_part * values / radii[bit][:, None]).astype(BF16)
        return jnp.dot(normed, head, preferred_element_type=F32)

    summed, got = {}, {}
    for base in (0, 2):
        given = swap(partial_logits(base + 1), "seq", 1, seq_size)
        summed[base] = partial_logits(base) + given
        got[base ^ 2] = swap(summed[base].astype(jnp.float16), "seq", 2, seq_size)

    halves = {}
    for base, where in ((2, other_places), (0, own_places)):
        full = summed[base] + got[base].astype(F32)
        mates = swap(full, "seq", 1, seq_size)
        exponent, tilted, logits, stats = soften(
            where, full, mates, tangent_row, sums[base], sums[base + 1], feature_count
        )
        all_stats = [stats] + [
            swap(stats, "vocab", bit, vocab_size) for bit in range(1, vocab_size)
        ]
        plain = back_plain(exponent, head)
        theirs, kept, joint = back_scaled(tilted_kernel, tilted, head, plain, [], all_stats)
        halves[base] = (logits, plain, theirs, kept, joint)

    target_1 = swap(target, "seq", 1, seq_size)
    target_2 = swap(target, "seq", 2, seq_size)
    target_3 = swap(target_2, "seq", 1, seq_size)
    weights_own, weights_other, target_stats = weigh(
        target_places, [target, target_1, target_2, target_3], halves[0][0], halves[2][0]
    )
    target_all = [target_stats] + [
        swap(target_stats, "vocab", bit, vocab_size) for bit in range(1, vocab_size)
    ]
    weighed = {}
    half = rows // 2
    for base, weights in ((2, weights_other), (0, weights_own)):
        begin = 0 if base == 0 else half
        stats = [value[:, begin : begin + half] for value in target_all]
        _, plain, _, _, joint = halves[base]
        weighed[base] = back_scaled(weights_kernel, weights, head, plain, [joint], stats)

    def over_vocab(pairs):
        met = []
        for theirs, kept in pairs:
            met.append(kept + swap(theirs, "vocab", 1, vocab_size).astype(F32))
        joined = jnp.stack(met).reshape(length, share, -1)

        def part(index):
            other = (index // (length // 2)) ^ chip
            place = other * (length // 2) + index % (length // 2)
            return lax.dynamic_index_in_dim(joined, place, 0, False)

        return chain_scatter(part, z, length)

    ggn_mine = over_vocab([halves[base][2:4] for base in (0, 2)])
    grad_mine = over_vocab([weighed[base][0:2] for base in (0, 2)])

    first_row = vocab_index * share
    owner = first_row // tokens
    block = owner ^ seq_index

    def choose(options):
        result = options[0]
        for index in range(1, len(options)):
            result = jnp.where(block == index, options[index], result)
        return result

    def gather_rows(options):
        pieces = []
        for begin in range(0, share, size):
            inside = first_row % tokens + begin
            place = ((inside // quarter) ^ group) * quarter + inside % quarter
            pieces.append(
                choose([lax.dynamic_slice_in_dim(o, place, size, 0) for o in options])
            )
        return jnp.concatenate(pieces, axis=0)

    my_inputs = gather_rows(blocks).astype(F32) + steer_part
    my_denominator = gather_rows(denominators)
    my_radius = jnp.sqrt(my_denominator)
    in_half = z % (length // 2) * share
    other = (z // (length // 2)) ^ chip

    def mine(own_value, other_value):
        value = jnp.where(other == 0, own_value, other_value)
        return lax.dynamic_slice_in_dim(value, in_half, share)

    dot_ggn = mine(halves[0][4][3], halves[2][4][3])
    dot_grad = mine(
        halves[0][4][2] - weighed[0][2][2], halves[2][4][2] - weighed[2][2][2]
    )

    def norm_back(upstream, dotted):
        along = dotted * my_radius / feature_count / my_denominator
        return (gain_part * upstream - my_inputs * along[:, None]) / my_radius[:, None]

    return norm_back(grad_mine, dot_grad), norm_back(ggn_mine, dot_ggn)


def solution(mesh):
    return jax.shard_map(
        body,
        mesh=mesh,
        in_specs=(P("seq", None), P(), P(), P(), P("seq", "vocab"), P("seq", "vocab")),
        out_specs=(P("vocab", "seq"), P("vocab", "seq")),
        check_vma=False,
    )
```

```python
import functools

import jax
import jax.numpy as jnp
from jax import lax
from jax.experimental import pallas as pl
from jax.experimental.pallas import tpu as pltpu
from jax.sharding import PartitionSpec as P

EPSILON = 1e-06
QUARTERS = 4
PAIR = 2
F32, BF16 = jnp.float32, jnp.bfloat16
VMEM_BYTES = 48 * 1024 * 1024


def params():
    return pltpu.CompilerParams(vmem_limit_bytes=VMEM_BYTES)


def whole_spec():
    return pl.BlockSpec(memory_space=pltpu.VMEM)


def smem_spec():
    return pl.BlockSpec(memory_space=pltpu.SMEM)


def swap(value, axis, bit, size):
    return lax.ppermute(value, axis, [(i, i ^ bit) for i in range(size)])


def lanes(columns, rows):
    lane = lax.broadcasted_iota(jnp.int32, (rows, 128), 1)
    tile = jnp.zeros((rows, 128), F32)
    for index, column in enumerate(columns):
        tile = jnp.where(lane == index, column, tile)
    return tile


def turn(rows8):
    return jnp.concatenate([rows8, jnp.zeros((120, 128), F32)], axis=0).T


def cut_kernel(width, seq_size, at, hidden, vectors, *outs):
    own, mate, near_2, near_3, far_2, far_3, sums, parts, two = outs
    seq_index, group = at[0], at[1]
    rows = hidden.shape[0]
    size = rows // QUARTERS

    def quarter(place):
        return pl.ds(pl.multiple_of((place ^ group) * size, size), size)

    def features(bit):
        return pl.ds(pl.multiple_of((seq_index ^ bit) * width, width), width)

    near_2[...] = hidden[quarter(0), features(2)]
    near_3[...] = hidden[quarter(0), features(3)]
    far_2[...] = hidden[quarter(3), features(2)]
    far_3[...] = hidden[quarter(3), features(3)]
    steer, tangent = vectors[0:1, :], vectors[1:2, :]
    columns = []
    for place in range(QUARTERS):
        spot = pl.ds(place * size, size)
        own[spot, :] = hidden[quarter(place), features(0)]
        mate[spot, :] = hidden[quarter(place), features(1)]
        inputs = hidden[quarter(place), :].astype(F32) + steer
        columns.append(
            lanes(
                [
                    jnp.sum(inputs * inputs, axis=1, keepdims=True),
                    jnp.sum(inputs * tangent, axis=1, keepdims=True),
                ],
                size,
            )
        )
    sums[...] = jnp.concatenate(columns, axis=0).T[:8]
    mine = vectors[:, features(0)]
    parts[...] = mine
    line = mine[1:2] * mine[2:3]
    high = line.astype(BF16).astype(F32)
    two[...] = jnp.concatenate(
        [high, line - high, jnp.zeros((14, width), F32)], axis=0
    ).astype(BF16)


def cut(at, hidden, vectors, width, seq_size):
    rows = hidden.shape[0]
    piece = jax.ShapeDtypeStruct((rows // QUARTERS, width), BF16)
    block = jax.ShapeDtypeStruct((rows, width), BF16)
    return pl.pallas_call(
        functools.partial(cut_kernel, width, seq_size),
        in_specs=[smem_spec(), whole_spec(), whole_spec()],
        out_specs=[whole_spec()] * 9,
        out_shape=[
            block,
            block,
            piece,
            piece,
            piece,
            piece,
            jax.ShapeDtypeStruct((8, rows), F32),
            jax.ShapeDtypeStruct((vectors.shape[0], width), F32),
            jax.ShapeDtypeStruct((16, width), BF16),
        ],
        compiler_params=params(),
    )(at, hidden, vectors)


def soften_kernel(feature_count, at, first, second, row, sums_a, sums_b, *outs):
    exponent_out, tilted_out, stats, tile = outs
    tokens = first.shape[0]
    count = at.shape[0]
    size = 2 * tokens // count
    line = row[0:1, :]
    for block, (source, sums) in enumerate(((first, sums_a), (second, sums_b))):
        turned = turn(sums[...])
        denominator = turned[:, 0:1] / feature_count + EPSILON
        inverse = 1.0 / jnp.sqrt(denominator)
        slope = turned[:, 1:2] / feature_count / denominator
        for piece in range(count // 2):
            begin = piece * size
            logits = source[begin : begin + size, :]
            spot = pl.ds(pl.multiple_of(at[block * (count // 2) + piece], size), size)
            peak = jnp.max(logits, axis=1, keepdims=True)
            exponent = jnp.exp(logits - peak)
            dlogits = line * inverse[begin : begin + size] - logits * slope[begin : begin + size]
            total = jnp.sum(exponent, axis=1, keepdims=True)
            mean = jnp.sum(exponent * dlogits, axis=1, keepdims=True) / total
            tilted = exponent * (dlogits - mean)
            exponent_out[spot, :] = exponent.astype(BF16)
            tilted_out[spot, :] = tilted.astype(BF16)
            tile[spot, :] = lanes([peak, total, mean], size)
    for begin in range(0, 2 * tokens, 128):
        stats[:, begin : begin + 128] = tile[begin : begin + 128, :].T[:8]


def soften(at, first, second, row, sums_a, sums_b, feature_count):
    tokens, width = first.shape
    rows = 2 * tokens
    return pl.pallas_call(
        functools.partial(soften_kernel, feature_count),
        in_specs=[smem_spec()] + [whole_spec()] * 5,
        out_specs=[whole_spec()] * 3,
        out_shape=[
            jax.ShapeDtypeStruct((rows, width), BF16),
            jax.ShapeDtypeStruct((rows, width), BF16),
            jax.ShapeDtypeStruct((8, rows), F32),
        ],
        scratch_shapes=[pltpu.VMEM((rows, 128), F32)],
        compiler_params=params(),
        cost_estimate=pl.CostEstimate(
            flops=30 * rows * width, bytes_accessed=12 * rows * width, transcendentals=rows * width
        ),
    )(at, first, second, row, sums_a, sums_b)


def tile_of(features):
    return 256 if features % 256 == 0 else features


def flip_kernel(head, out):
    out[0] = head[...].T


def flip(head):
    features, width = head.shape
    tile = tile_of(features)
    return pl.pallas_call(
        flip_kernel,
        grid=(features // tile,),
        in_specs=[pl.BlockSpec((tile, width), lambda i: (i, 0))],
        out_specs=pl.BlockSpec((1, width, tile), lambda i: (i, 0, 0)),
        out_shape=jax.ShapeDtypeStruct((features // tile, width, tile), BF16),
        compiler_params=params(),
        cost_estimate=pl.CostEstimate(
            flops=8 * features * width, bytes_accessed=4 * features * width, transcendentals=0
        ),
    )(head)


def matmul_cost(rows, width, features, extra):
    return pl.CostEstimate(
        flops=2 * rows * width * features,
        bytes_accessed=2 * width * (rows + features) + extra,
        transcendentals=0,
    )


def plain_kernel(cotangent, head, out):
    out[...] = jnp.dot(cotangent[...], head[0], preferred_element_type=F32)


def back_plain(cotangent, flipped):
    rows, width = cotangent.shape
    tiles, _, tile = flipped.shape
    features = tiles * tile
    return pl.pallas_call(
        plain_kernel,
        grid=(tiles,),
        in_specs=[
            pl.BlockSpec((rows, width), lambda i: (0, 0)),
            pl.BlockSpec((1, width, tile), lambda i: (i, 0, 0)),
        ],
        out_specs=pl.BlockSpec((rows, tile), lambda i: (0, i)),
        out_shape=jax.ShapeDtypeStruct((rows, features), F32),
        compiler_params=params(),
        cost_estimate=matmul_cost(rows, width, features, 4 * rows * features),
    )(cotangent, flipped)


def weights_kernel(at, *refs):
    blocks, totals = refs[:4], refs[4:8]
    scales, head, plain_own, plain_other, theirs, kept, ordered, columns = refs[8:]
    tokens = blocks[0].shape[0]
    count = at.shape[0]
    size = 4 * tokens // count
    half = 2 * tokens

    @pl.when(pl.program_id(0) == 0)
    def _():
        for begin in range(0, 2 * half, 128):
            columns[begin : begin + 128, :] = turn(scales[:, begin : begin + 128])
        for block in range(4):
            inverse = 1.0 / turn(totals[block][...])[:, 0:1]
            for piece in range(count // 4):
                begin = piece * size
                place = at[block * (count // 4) + piece] + half * (block // 2)
                spot = pl.ds(pl.multiple_of(place, size), size)
                ordered[spot, :] = blocks[block][begin : begin + size, :]
                columns[spot, 1:2] = inverse[begin : begin + size]

    product = jnp.dot(ordered[...], head[0], preferred_element_type=F32)
    for index, plain in enumerate((plain_own, plain_other)):
        begin = index * half
        result = (
            columns[begin : begin + half, 0:1] * plain[...]
            - columns[begin : begin + half, 1:2] * product[begin : begin + half]
        )
        kept[index * tokens : (index + 1) * tokens, :] = result[:tokens]
        theirs[index * tokens : (index + 1) * tokens, :] = result[tokens:].astype(BF16)


def back_weights(at, blocks, totals, scales, flipped, plain_own, plain_other, begin, count):
    tokens, width = blocks[0].shape
    tile = flipped.shape[2]
    rows = 4 * tokens
    plain = pl.BlockSpec((2 * tokens, tile), lambda i: (0, i + begin))
    out = pl.BlockSpec((2 * tokens, tile), lambda i: (0, i))
    fixed = [pl.BlockSpec(value.shape, lambda i: (0, 0)) for value in (*blocks, *totals, scales)]
    return pl.pallas_call(
        weights_kernel,
        grid=(count,),
        in_specs=[smem_spec()]
        + fixed
        + [pl.BlockSpec((1, width, tile), lambda i: (i + begin, 0, 0)), plain, plain],
        out_specs=[out, out],
        out_shape=[
            jax.ShapeDtypeStruct((2 * tokens, count * tile), BF16),
            jax.ShapeDtypeStruct((2 * tokens, count * tile), F32),
        ],
        scratch_shapes=[pltpu.VMEM((rows, width), BF16), pltpu.VMEM((rows, 128), F32)],
        compiler_params=params(),
        cost_estimate=matmul_cost(rows, width, count * tile, 7 * rows * count * tile),
    )(at, *blocks, *totals, scales, flipped, plain_own, plain_other)


def merge(first, second):
    peak = jnp.maximum(first[0], second[0])
    one = jnp.exp(first[0] - peak) * first[1]
    two = jnp.exp(second[0] - peak) * second[1]
    total = one + two
    return jnp.stack([peak, total, (one * first[2] + two * second[2]) / total])


def exchange(value, size):
    half = value.shape[1] // 2
    other = swap(value, "vocab", 1, size)
    value = merge(value, jnp.concatenate([other[:, half:], other[:, :half]], axis=1))
    bit = PAIR
    while bit < size:
        value = merge(value, swap(value, "vocab", bit, size))
        bit *= 2
    return value


def body(hidden, steer, tangent, gain, head, target):
    seq_size = lax.axis_size("seq")
    vocab_size = lax.axis_size("vocab")
    seq_index = lax.axis_index("seq")
    vocab_index = lax.axis_index("vocab")
    tokens, feature_count = hidden.shape
    width = head.shape[0]
    rows = seq_size * tokens
    share = rows // vocab_size
    quarter = tokens // QUARTERS
    size = min(share, quarter)
    y, z = vocab_index % PAIR, vocab_index // PAIR
    length = vocab_size // PAIR
    chip = seq_index // 2
    group = 2 * y + z % 2

    def destination(block, begin):
        row = (block % 2) * tokens + begin
        owner, inside = row // share, row % share
        return ((owner % PAIR) ^ y) * tokens + owner // PAIR * share + inside

    starts = jnp.arange(tokens // size) * size
    turned = ((starts // quarter) ^ group) * quarter + starts % quarter

    def places(bits, begins):
        return jnp.concatenate(
            [destination(seq_index ^ bit, begins) for bit in bits]
        ).astype(jnp.int32)

    own_places, other_places = places((0, 1), turned), places((2, 3), turned)
    target_places = places((0, 1, 2, 3), starts)

    at = jnp.stack([seq_index, group]).astype(jnp.int32)
    vectors = jnp.stack([steer, tangent, gain])
    own, mate, near_2, near_3, far_2, far_3, sums_0, parts, two = cut(
        at, hidden, vectors, width, seq_size
    )
    near = jnp.stack([swap(near_2, "seq", 2, seq_size), swap(near_3, "seq", 3, seq_size)])
    mate = swap(mate, "seq", 1, seq_size)
    far = [swap(far_2, "seq", 2, seq_size), swap(far_3, "seq", 3, seq_size)]
    sums_1 = swap(sums_0, "seq", 1, seq_size)
    both = swap(jnp.stack([sums_0, sums_1]), "seq", 2, seq_size)
    sums = [sums_0, sums_1, both[0], both[1]]
    by_y = swap(near, "vocab", 2, vocab_size)
    by_z = swap(near, "vocab", 1, vocab_size)
    blocks = [own, mate] + [
        jnp.concatenate([near[i], by_y[i], by_z[i], far[i]], axis=0) for i in range(2)
    ]
    steer_part, gain_part = parts[0], parts[2]

    row = jnp.sum(jnp.dot(two, head, preferred_element_type=F32), axis=0, keepdims=True)

    denominators = [s[0] / feature_count + EPSILON for s in sums]
    radii = [jnp.sqrt(d) for d in denominators]

    def partial_logits(bit, block):
        values = block.astype(F32) + steer_part
        normed = (gain_part * values / radii[bit][:, None]).astype(BF16)
        return jnp.dot(normed, head, preferred_element_type=F32)

    given = swap(partial_logits(1, mate), "seq", 1, seq_size)
    later_own, _, row = lax.optimization_barrier((own, far, row))
    summed_0 = partial_logits(0, later_own) + given
    send_0 = summed_0.astype(jnp.float16)
    got_2 = swap(send_0, "seq", 2, seq_size)

    row, target_early, _ = lax.optimization_barrier((row, target, send_0))
    row = row + swap(row, "seq", 1, seq_size)
    tangent_row = row + swap(row, "seq", 2, seq_size)

    given = swap(partial_logits(3, blocks[3]), "seq", 1, seq_size)
    summed_2 = partial_logits(2, blocks[2]) + given
    send_2 = summed_2.astype(jnp.float16)
    send_2, got_2 = lax.optimization_barrier((send_2, got_2))
    got_0 = swap(send_2, "seq", 2, seq_size)

    early_head, _ = lax.optimization_barrier((head, send_2))
    flipped = flip(early_head)

    total_0 = jnp.sum(target_early.astype(F32), axis=1)
    total_0 = jnp.broadcast_to(total_0, (8, tokens))
    bit = 1
    while bit < vocab_size:
        total_0 = total_0 + swap(total_0, "vocab", bit, vocab_size)
        bit *= 2
    total_1 = swap(total_0, "seq", 1, seq_size)
    both = swap(jnp.stack([total_0, total_1]), "seq", 2, seq_size)
    totals = [total_0, total_1, both[0], both[1]]

    half = rows // 2

    def half_of(base, summed, got, where):
        full = summed + got.astype(F32)
        mates = swap(full, "seq", 1, seq_size)
        exponent, tilted, stats = soften(
            where, full, mates, tangent_row, sums[base], sums[base + 1], feature_count
        )
        stats = stats[:3]
        joint = exchange(stats, vocab_size)
        plain = back_plain(exponent, flipped)
        raw = back_plain(tilted, flipped)
        scale = jnp.exp(stats[0] - joint[0]) / joint[1]
        lean = scale * (stats[2] - joint[2])
        ggn = scale[:, None] * raw + lean[:, None] * plain
        return plain, scale, ggn[half // 2 :].astype(BF16), ggn[: half // 2]

    plain_other, scale_other, theirs_other, kept_other = half_of(2, summed_2, got_2, other_places)
    plain_own, scale_own, theirs_own, kept_own = half_of(0, summed_0, got_0, own_places)

    late_target, _ = lax.optimization_barrier((target, got_0))
    target_2 = swap(late_target, "seq", 2, seq_size)
    target_1 = swap(late_target, "seq", 1, seq_size)
    target_3 = swap(target_2, "seq", 1, seq_size)
    scales = jnp.broadcast_to(jnp.concatenate([scale_own, scale_other]), (8, rows))

    def gradient_of(begin, count):
        return back_weights(
            target_places,
            [target, target_1, target_2, target_3],
            totals,
            scales,
            flipped,
            plain_own,
            plain_other,
            begin,
            count,
        )

    def meet(theirs, kept):
        return kept + swap(theirs, "vocab", 1, vocab_size).astype(F32)

    def over_chain(joined):
        joined = joined.reshape(length, share, -1)

        def part(index):
            other = (index // (length // 2)) ^ chip
            place = other * (length // 2) + index % (length // 2)
            return lax.dynamic_index_in_dim(joined, place, 0, False)

        total = part(z)
        for bit in range(1, length):
            sent = part(z ^ bit).astype(BF16)
            total = total + swap(sent, "vocab", bit * PAIR, vocab_size).astype(F32)
        return total

    ggn_mine = over_chain(
        jnp.concatenate([meet(theirs_own, kept_own), meet(theirs_other, kept_other)], axis=0)
    )
    tiles = flipped.shape[0]
    cuts = [(0, tiles)] if tiles < 2 else [(0, tiles // 2), (tiles // 2, tiles - tiles // 2)]
    grad_mine = jnp.concatenate(
        [over_chain(meet(*gradient_of(*piece))) for piece in cuts], axis=1
    )

    first_row = vocab_index * share
    owner = first_row // tokens
    block = owner ^ seq_index

    def choose(options):
        result = options[0]
        for index in range(1, len(options)):
            result = jnp.where(block == index, options[index], result)
        return result

    def gather_rows(options):
        pieces = []
        for begin in range(0, share, size):
            inside = first_row % tokens + begin
            place = ((inside // quarter) ^ group) * quarter + inside % quarter
            pieces.append(
                choose([lax.dynamic_slice_in_dim(o, place, size, 0) for o in options])
            )
        return jnp.concatenate(pieces, axis=0)

    my_inputs = gather_rows(blocks).astype(F32) + steer_part
    my_denominator = gather_rows(denominators)
    my_radius = jnp.sqrt(my_denominator)

    def norm_back(upstream):
        scaled = gain_part * upstream
        dotted = jnp.sum(my_inputs * scaled, axis=1)[None]
        dotted = dotted + swap(dotted, "seq", 1, seq_size)
        dotted = (dotted + swap(dotted, "seq", 2, seq_size))[0]
        along = dotted / feature_count / my_denominator
        return (scaled - my_inputs * along[:, None]) / my_radius[:, None]

    return norm_back(grad_mine), norm_back(ggn_mine)


def solution(mesh):
    return jax.shard_map(
        body,
        mesh=mesh,
        in_specs=(P("seq", None), P(), P(), P(), P("seq", "vocab"), P("seq", "vocab")),
        out_specs=(P("vocab", "seq"), P("vocab", "seq")),
        check_vma=False,
    )
```

```python
import functools

import jax
import jax.numpy as jnp
from jax import lax
from jax.experimental import pallas as pl
from jax.experimental.pallas import tpu as pltpu
from jax.sharding import PartitionSpec as P

EPSILON = 1e-06
NT = (((1,), (1,)), ((), ()))
QUARTERS = 4
PAIR = 2
F32, BF16 = jnp.float32, jnp.bfloat16


def params(mebibytes):
    return pltpu.CompilerParams(vmem_limit_bytes=mebibytes * 1024 * 1024)


def whole_spec():
    return pl.BlockSpec(memory_space=pltpu.VMEM)


def smem_spec():
    return pl.BlockSpec(memory_space=pltpu.SMEM)


def swap(value, axis, bit, size):
    return lax.ppermute(value, axis, [(i, i ^ bit) for i in range(size)])


def lanes(columns, rows):
    lane = lax.broadcasted_iota(jnp.int32, (rows, 128), 1)
    tile = jnp.zeros((rows, 128), F32)
    for index, column in enumerate(columns):
        tile = jnp.where(lane == index, column, tile)
    return tile


def turn(rows8):
    return jnp.concatenate([rows8, jnp.zeros((120, 128), F32)], axis=0).T


def cut_kernel(width, seq_size, at, hidden, vectors, *outs):
    own, mate, over_2, over_3, sums, parts, two = outs
    seq_index, group = at[0], at[1]
    rows = hidden.shape[0]
    size = rows // QUARTERS

    def quarter(place):
        return pl.ds(pl.multiple_of((place ^ group) * size, size), size)

    def features(bit):
        return pl.ds(pl.multiple_of((seq_index ^ bit) * width, width), width)

    for out, bit in ((over_2, 2), (over_3, 3)):
        out[0:size, :] = hidden[quarter(0), features(bit)]
        out[size:, :] = hidden[quarter(3), features(bit)]
    steer, tangent = vectors[0:1, :], vectors[1:2, :]
    columns = []
    for place in range(QUARTERS):
        spot = pl.ds(place * size, size)
        own[spot, :] = hidden[quarter(place), features(0)]
        mate[spot, :] = hidden[quarter(place), features(1)]
        inputs = hidden[quarter(place), :].astype(F32) + steer
        columns.append(
            lanes(
                [
                    jnp.sum(inputs * inputs, axis=1, keepdims=True),
                    jnp.sum(inputs * tangent, axis=1, keepdims=True),
                ],
                size,
            )
        )
    sums[...] = jnp.concatenate(columns, axis=0).T[:8]
    mine = vectors[:, features(0)]
    parts[...] = mine
    line = mine[1:2] * mine[2:3]
    high = line.astype(BF16).astype(F32)
    two[...] = jnp.concatenate(
        [high, line - high, jnp.zeros((14, width), F32)], axis=0
    ).astype(BF16)


def cut(at, hidden, vectors, width, seq_size):
    rows = hidden.shape[0]
    piece = jax.ShapeDtypeStruct((2 * (rows // QUARTERS), width), BF16)
    block = jax.ShapeDtypeStruct((rows, width), BF16)
    return pl.pallas_call(
        functools.partial(cut_kernel, width, seq_size),
        in_specs=[smem_spec(), whole_spec(), whole_spec()],
        out_specs=[whole_spec()] * 7,
        out_shape=[
            block,
            block,
            piece,
            piece,
            jax.ShapeDtypeStruct((8, rows), F32),
            jax.ShapeDtypeStruct((vectors.shape[0], width), F32),
            jax.ShapeDtypeStruct((16, width), BF16),
        ],
        compiler_params=params(12),
    )(at, hidden, vectors)


def soften_kernel(feature_count, at, first, second, row, sums_a, sums_b, *outs):
    both_out, stats, tile = outs
    tokens = first.shape[0]
    count = at.shape[0]
    size = 2 * tokens // count
    line = row[0:1, :]
    for block, (source, sums) in enumerate(((first, sums_a), (second, sums_b))):
        turned = turn(sums[...])
        denominator = turned[:, 0:1] / feature_count + EPSILON
        inverse = 1.0 / jnp.sqrt(denominator)
        slope = turned[:, 1:2] / feature_count / denominator
        for piece in range(count // 2):
            begin = piece * size
            logits = source[begin : begin + size, :]
            spot = pl.ds(pl.multiple_of(at[block * (count // 2) + piece], size), size)
            peak = jnp.max(logits, axis=1, keepdims=True)
            exponent = jnp.exp(logits - peak)
            dlogits = line * inverse[begin : begin + size] - logits * slope[begin : begin + size]
            total = jnp.sum(exponent, axis=1, keepdims=True)
            mean = jnp.sum(exponent * dlogits, axis=1, keepdims=True) / total
            tilted = exponent * (dlogits - mean)
            both_out[0, spot, :] = exponent.astype(BF16)
            both_out[1, spot, :] = tilted.astype(BF16)
            tile[spot, :] = lanes([peak, total, mean], size)
    for begin in range(0, 2 * tokens, 128):
        stats[:, begin : begin + 128] = tile[begin : begin + 128, :].T[:8]


def soften(at, first, second, row, sums_a, sums_b, feature_count):
    tokens, width = first.shape
    rows = 2 * tokens
    return pl.pallas_call(
        functools.partial(soften_kernel, feature_count),
        in_specs=[smem_spec()] + [whole_spec()] * 5,
        out_specs=[whole_spec()] * 2,
        out_shape=[
            jax.ShapeDtypeStruct((2, rows, width), BF16),
            jax.ShapeDtypeStruct((8, rows), F32),
        ],
        scratch_shapes=[pltpu.VMEM((rows, 128), F32)],
        compiler_params=params(16),
        cost_estimate=pl.CostEstimate(
            flops=30 * rows * width, bytes_accessed=12 * rows * width, transcendentals=rows * width
        ),
    )(at, first, second, row, sums_a, sums_b)


def order_kernel(at, *refs):
    blocks, totals, (ordered, columns) = refs[:4], refs[4:8], refs[8:]
    tokens = blocks[0].shape[0]
    count = at.shape[0]
    size = 4 * tokens // count
    half = 2 * tokens
    for block in range(4):
        inverse = 1.0 / turn(totals[block][...])
        for piece in range(count // 4):
            begin = piece * size
            place = at[block * (count // 4) + piece] + half * (block // 2)
            spot = pl.ds(pl.multiple_of(place, size), size)
            ordered[spot, :] = blocks[block][begin : begin + size, :]
            columns[spot, :] = inverse[begin : begin + size]


def order(at, blocks, totals):
    tokens, width = blocks[0].shape
    rows = 4 * tokens
    return pl.pallas_call(
        order_kernel,
        in_specs=[smem_spec()] + [whole_spec()] * 8,
        out_specs=[whole_spec()] * 2,
        out_shape=[
            jax.ShapeDtypeStruct((rows, width), BF16),
            jax.ShapeDtypeStruct((rows, 128), F32),
        ],
        compiler_params=params(12),
        cost_estimate=pl.CostEstimate(
            flops=rows * width, bytes_accessed=4 * rows * width, transcendentals=0
        ),
    )(at, *blocks, *totals)


def merge(first, second):
    peak = jnp.maximum(first[0], second[0])
    one = jnp.exp(first[0] - peak) * first[1]
    two = jnp.exp(second[0] - peak) * second[1]
    total = one + two
    mean = (one * first[2] + two * second[2]) / total
    return jnp.stack([peak, total, mean] + [first[i] + second[i] for i in range(3, len(first))])


def exchange(value, size):
    half = value.shape[1] // 2
    other = swap(value, "vocab", 1, size)
    aligned = jnp.concatenate([other[:3, half:], other[:3, :half]], axis=1)
    value = merge(value, jnp.concatenate([aligned, other[3:]], axis=0))
    bit = PAIR
    while bit < size:
        value = merge(value, swap(value, "vocab", bit, size))
        bit *= 2
    return value


def body(hidden, steer, tangent, gain, head, target):
    seq_size = lax.axis_size("seq")
    vocab_size = lax.axis_size("vocab")
    seq_index = lax.axis_index("seq")
    vocab_index = lax.axis_index("vocab")
    tokens, feature_count = hidden.shape
    width = head.shape[0]
    rows = seq_size * tokens
    share = rows // vocab_size
    quarter = tokens // QUARTERS
    size = min(share, quarter)
    y, z = vocab_index % PAIR, vocab_index // PAIR
    length = vocab_size // PAIR
    chip = seq_index // 2
    group = 2 * y + z % 2

    def destination(block, begin):
        row = (block % 2) * tokens + begin
        owner, inside = row // share, row % share
        return ((owner % PAIR) ^ y) * tokens + owner // PAIR * share + inside

    starts = jnp.arange(tokens // size) * size
    turned = ((starts // quarter) ^ group) * quarter + starts % quarter

    def places(bits, begins):
        return jnp.concatenate(
            [destination(seq_index ^ bit, begins) for bit in bits]
        ).astype(jnp.int32)

    own_places, other_places = places((0, 1), turned), places((2, 3), turned)
    target_places = places((0, 1, 2, 3), starts)

    at = jnp.stack([seq_index, group]).astype(jnp.int32)
    vectors = jnp.stack([steer, tangent, gain])
    own, mate, over_2, over_3, sums_0, parts, two = cut(
        at, hidden, vectors, width, seq_size
    )
    mate = swap(mate, "seq", 1, seq_size)
    sums_1 = swap(sums_0, "seq", 1, seq_size)
    over_2, over_3 = swap(over_2, "seq", 2, seq_size), swap(over_3, "seq", 3, seq_size)
    both = swap(jnp.stack([sums_0, sums_1]), "seq", 2, seq_size)
    sums = [sums_0, sums_1, both[0], both[1]]
    near = jnp.stack([over_2[:quarter], over_3[:quarter]])
    by_y = swap(near, "vocab", 2, vocab_size)
    by_z = swap(near, "vocab", 1, vocab_size)
    steer_part, gain_part = parts[0], parts[2]

    denominators = [s[0] / feature_count + EPSILON for s in sums]
    radii = [jnp.sqrt(d) for d in denominators]

    def partial_logits(bit, block):
        values = block.astype(F32) + steer_part
        normed = (gain_part * values / radii[bit][:, None]).astype(BF16)
        return jnp.dot(normed, head, preferred_element_type=F32)

    given = swap(partial_logits(1, mate), "seq", 1, seq_size)
    summed_0 = partial_logits(0, own) + given
    send_0, over_2, over_3 = lax.optimization_barrier(
        (summed_0.astype(jnp.float16), over_2, over_3)
    )
    got_2 = swap(send_0, "seq", 2, seq_size)

    two, by_y, by_z, _ = lax.optimization_barrier((two, by_y, by_z, send_0))
    row = jnp.sum(jnp.dot(two, head, preferred_element_type=F32), axis=0, keepdims=True)
    row = row + swap(row, "seq", 1, seq_size)
    tangent_row = row + swap(row, "seq", 2, seq_size)

    blocks = [own, mate] + [
        jnp.concatenate([over[:quarter], by_y[i], by_z[i], over[quarter:]], axis=0)
        for i, over in enumerate((over_2, over_3))
    ]
    given = swap(partial_logits(3, blocks[3]), "seq", 1, seq_size)
    summed_2 = partial_logits(2, blocks[2]) + given
    send_2, got_2, tangent_row = lax.optimization_barrier(
        (summed_2.astype(jnp.float16), got_2, tangent_row)
    )
    got_0 = swap(send_2, "seq", 2, seq_size)

    half = rows // 2

    def half_of(base, summed, got, where, extra):
        full = summed + got.astype(F32)
        mates = swap(full, "seq", 1, seq_size)
        both, stats = soften(
            where, full, mates, tangent_row, sums[base], sums[base + 1], feature_count
        )
        stats = stats[:3]
        joint = exchange(jnp.concatenate([stats] + extra), vocab_size)
        raw = lax.dot_general(
            both.reshape(2 * half, -1), head, NT, preferred_element_type=F32
        )
        scale = jnp.exp(stats[0] - joint[0]) / joint[1]
        lean = scale * (stats[2] - joint[2])
        plain = scale[:, None] * raw[:half]
        ggn = scale[:, None] * raw[half:] + lean[:, None] * raw[:half]
        return plain, ggn[half // 2 :].astype(BF16), ggn[: half // 2], joint

    plain_other, theirs_other, kept_other, _ = half_of(2, summed_2, got_2, other_places, [])
    own_total = jnp.sum(target.astype(F32), axis=1)
    plain_own, theirs_own, kept_own, joint = half_of(
        0, summed_0, got_0, own_places, [jnp.concatenate([own_total, own_total])[None]]
    )

    late_target, _ = lax.optimization_barrier((target, got_0))
    target_2 = swap(late_target, "seq", 2, seq_size)
    target_1 = swap(late_target, "seq", 1, seq_size)
    target_3 = swap(target_2, "seq", 1, seq_size)
    total_0 = jnp.broadcast_to(joint[3, :tokens], (8, tokens))
    total_1 = swap(total_0, "seq", 1, seq_size)
    both = swap(jnp.stack([total_0, total_1]), "seq", 2, seq_size)
    ordered, columns = order(
        target_places,
        [target, target_1, target_2, target_3],
        [total_0, total_1, both[0], both[1]],
    )
    ordered, theirs_own = lax.optimization_barrier((ordered, theirs_own))
    weighed = lax.dot_general(ordered, head, NT, preferred_element_type=F32)
    inverse = columns[:, 0:1]
    gradients = [
        plain - inverse[begin : begin + half] * weighed[begin : begin + half]
        for plain, begin in ((plain_own, 0), (plain_other, half))
    ]

    def meet(theirs, kept):
        return kept + swap(theirs, "vocab", 1, vocab_size).astype(F32)

    def over_chain(joined):
        joined = joined.reshape(length, share, -1)
        near_half = length // 2
        bit = 1
        while bit < length:
            if bit < near_half:
                cut_up = joined.reshape(-1, 2, share, joined.shape[-1])
                mine_bit = (z // bit) % 2
                sent = lax.dynamic_index_in_dim(cut_up, 1 - mine_bit, 1, False)
                kept = lax.dynamic_index_in_dim(cut_up, mine_bit, 1, False)
            else:
                place = (z // bit) ^ chip
                sent = lax.dynamic_index_in_dim(joined, 1 - place, 0, True)
                kept = lax.dynamic_index_in_dim(joined, place, 0, True)
            got = swap(sent.astype(BF16), "vocab", bit * PAIR, vocab_size)
            joined = kept + got.astype(F32)
            bit *= 2
        return joined[0]

    ggn_mine = over_chain(
        jnp.concatenate([meet(theirs_own, kept_own), meet(theirs_other, kept_other)], axis=0)
    )
    chunks = []
    for begin in (0, width // 2):
        part = [g[:, begin : begin + width // 2] for g in gradients]
        theirs = jnp.concatenate([p[half // 2 :] for p in part]).astype(BF16)
        kept = jnp.concatenate([p[: half // 2] for p in part])
        chunks.append(over_chain(meet(theirs, kept)))
    grad_mine = jnp.concatenate(chunks, axis=1)

    first_row = vocab_index * share
    owner = first_row // tokens
    block = owner ^ seq_index

    def choose(options):
        result = options[0]
        for index in range(1, len(options)):
            result = jnp.where(block == index, options[index], result)
        return result

    def gather_rows(options):
        pieces = []
        for begin in range(0, share, size):
            inside = first_row % tokens + begin
            place = ((inside // quarter) ^ group) * quarter + inside % quarter
            pieces.append(
                choose([lax.dynamic_slice_in_dim(o, place, size, 0) for o in options])
            )
        return jnp.concatenate(pieces, axis=0)

    my_inputs = gather_rows(blocks).astype(F32) + steer_part
    my_denominator = gather_rows(denominators)
    my_radius = jnp.sqrt(my_denominator)

    def norm_back(upstream):
        scaled = gain_part * upstream
        dotted = jnp.sum(my_inputs * scaled, axis=1)[None]
        dotted = dotted + swap(dotted, "seq", 1, seq_size)
        dotted = (dotted + swap(dotted, "seq", 2, seq_size))[0]
        along = dotted / feature_count / my_denominator
        return (scaled - my_inputs * along[:, None]) / my_radius[:, None]

    return norm_back(grad_mine), norm_back(ggn_mine)


def solution(mesh):
    return jax.shard_map(
        body,
        mesh=mesh,
        in_specs=(P("seq", None), P(), P(), P(), P("seq", "vocab"), P("seq", "vocab")),
        out_specs=(P("vocab", "seq"), P("vocab", "seq")),
        check_vma=False,
    )
```

```python
import functools

import jax
import jax.numpy as jnp
from jax import lax
from jax.experimental import pallas as pl
from jax.experimental.pallas import tpu as pltpu
from jax.sharding import PartitionSpec as P

EPSILON = 1e-06
NT = (((1,), (1,)), ((), ()))
QUARTERS = 4
PAIR = 2
LIGHT = pl.CostEstimate(flops=0, bytes_accessed=0, transcendentals=0)
F32, BF16 = jnp.float32, jnp.bfloat16


def params(mebibytes):
    return pltpu.CompilerParams(vmem_limit_bytes=mebibytes * 1024 * 1024)


def whole_spec():
    return pl.BlockSpec(memory_space=pltpu.VMEM)


def smem_spec():
    return pl.BlockSpec(memory_space=pltpu.SMEM)


def swap(value, axis, bit, size):
    return lax.ppermute(value, axis, [(i, i ^ bit) for i in range(size)])


def lanes(columns, rows):
    lane = lax.broadcasted_iota(jnp.int32, (rows, 128), 1)
    tile = jnp.zeros((rows, 128), F32)
    for index, column in enumerate(columns):
        tile = jnp.where(lane == index, column, tile)
    return tile


def turn(rows8):
    return jnp.concatenate([rows8, jnp.zeros((120, 128), F32)], axis=0).T


def cut_kernel(width, seq_size, at, hidden, vectors, *outs):
    own, mate, over_2, over_3, sums, parts, two = outs
    seq_index, group = at[0], at[1]
    rows = hidden.shape[0]
    size = rows // QUARTERS

    def quarter(place):
        return pl.ds(pl.multiple_of((place ^ group) * size, size), size)

    def features(bit):
        return pl.ds(pl.multiple_of((seq_index ^ bit) * width, width), width)

    for out, bit in ((over_2, 2), (over_3, 3)):
        out[0:size, :] = hidden[quarter(0), features(bit)]
        out[size:, :] = hidden[quarter(3), features(bit)]
    steer, tangent = vectors[0:1, :], vectors[1:2, :]
    columns = []
    for place in range(QUARTERS):
        spot = pl.ds(place * size, size)
        own[spot, :] = hidden[quarter(place), features(0)]
        mate[spot, :] = hidden[quarter(place), features(1)]
        inputs = hidden[quarter(place), :].astype(F32) + steer
        columns.append(
            lanes(
                [
                    jnp.sum(inputs * inputs, axis=1, keepdims=True),
                    jnp.sum(inputs * tangent, axis=1, keepdims=True),
                ],
                size,
            )
        )
    sums[...] = jnp.concatenate(columns, axis=0).T[:8]
    mine = vectors[:, features(0)]
    parts[...] = mine
    line = mine[1:2] * mine[2:3]
    high = line.astype(BF16).astype(F32)
    two[...] = jnp.concatenate(
        [high, line - high, jnp.zeros((14, width), F32)], axis=0
    ).astype(BF16)


def cut(at, hidden, vectors, width, seq_size):
    rows = hidden.shape[0]
    piece = jax.ShapeDtypeStruct((2 * (rows // QUARTERS), width), BF16)
    block = jax.ShapeDtypeStruct((rows, width), BF16)
    return pl.pallas_call(
        functools.partial(cut_kernel, width, seq_size),
        in_specs=[smem_spec(), whole_spec(), whole_spec()],
        out_specs=[whole_spec()] * 7,
        out_shape=[
            block,
            block,
            piece,
            piece,
            jax.ShapeDtypeStruct((8, rows), F32),
            jax.ShapeDtypeStruct((vectors.shape[0], width), F32),
            jax.ShapeDtypeStruct((16, width), BF16),
        ],
        compiler_params=params(12),
        cost_estimate=LIGHT,
    )(at, hidden, vectors)


def soften_kernel(feature_count, at, first, second, row, sums_a, sums_b, *outs):
    both_out, stats, tile = outs
    tokens = first.shape[0]
    count = at.shape[0]
    size = 2 * tokens // count
    line = row[0:1, :]
    for block, (source, sums) in enumerate(((first, sums_a), (second, sums_b))):
        turned = turn(sums[...])
        denominator = turned[:, 0:1] / feature_count + EPSILON
        inverse = 1.0 / jnp.sqrt(denominator)
        slope = turned[:, 1:2] / feature_count / denominator
        for piece in range(count // 2):
            begin = piece * size
            logits = source[begin : begin + size, :]
            spot = pl.ds(pl.multiple_of(at[block * (count // 2) + piece], size), size)
            peak = jnp.max(logits, axis=1, keepdims=True)
            exponent = jnp.exp(logits - peak)
            dlogits = line * inverse[begin : begin + size] - logits * slope[begin : begin + size]
            total = jnp.sum(exponent, axis=1, keepdims=True)
            mean = jnp.sum(exponent * dlogits, axis=1, keepdims=True) / total
            tilted = exponent * (dlogits - mean)
            both_out[0, spot, :] = exponent.astype(BF16)
            both_out[1, spot, :] = tilted.astype(BF16)
            tile[spot, :] = lanes([peak, total, mean], size)
    for begin in range(0, 2 * tokens, 128):
        stats[:, begin : begin + 128] = tile[begin : begin + 128, :].T[:8]


def soften(at, first, second, row, sums_a, sums_b, feature_count):
    tokens, width = first.shape
    rows = 2 * tokens
    return pl.pallas_call(
        functools.partial(soften_kernel, feature_count),
        in_specs=[smem_spec()] + [whole_spec()] * 5,
        out_specs=[whole_spec()] * 2,
        out_shape=[
            jax.ShapeDtypeStruct((2, rows, width), BF16),
            jax.ShapeDtypeStruct((8, rows), F32),
        ],
        scratch_shapes=[pltpu.VMEM((rows, 128), F32)],
        compiler_params=params(16),
        cost_estimate=LIGHT,
    )(at, first, second, row, sums_a, sums_b)


def order_kernel(at, *refs):
    blocks, totals, (ordered, columns) = refs[:4], refs[4:8], refs[8:]
    tokens = blocks[0].shape[0]
    count = at.shape[0]
    size = 4 * tokens // count
    half = 2 * tokens
    for block in range(4):
        inverse = 1.0 / turn(totals[block][...])
        for piece in range(count // 4):
            begin = piece * size
            place = at[block * (count // 4) + piece] + half * (block // 2)
            spot = pl.ds(pl.multiple_of(place, size), size)
            ordered[spot, :] = blocks[block][begin : begin + size, :]
            columns[spot, :] = inverse[begin : begin + size]


def order(at, blocks, totals):
    tokens, width = blocks[0].shape
    rows = 4 * tokens
    return pl.pallas_call(
        order_kernel,
        in_specs=[smem_spec()] + [whole_spec()] * 8,
        out_specs=[whole_spec()] * 2,
        out_shape=[
            jax.ShapeDtypeStruct((rows, width), BF16),
            jax.ShapeDtypeStruct((rows, 128), F32),
        ],
        compiler_params=params(12),
        cost_estimate=LIGHT,
    )(at, *blocks, *totals)


def back_kernel(deep, cotangent, head, out):
    width = head.shape[1]
    result = lax.dot_general(
        cotangent[:, :deep], head[:, :deep], NT, preferred_element_type=F32
    )
    if deep < width:
        result += lax.dot_general(
            cotangent[:, deep:], head[:, deep:], NT, preferred_element_type=F32
        )
    out[...] = result


def back(cotangent, head):
    rows, width = cotangent.shape
    features = head.shape[0]
    tile = 256 if features % 256 == 0 else features
    deep = width // 256 * 256 or width
    return pl.pallas_call(
        functools.partial(back_kernel, deep),
        grid=(features // tile,),
        in_specs=[
            pl.BlockSpec((rows, width), lambda i: (0, 0)),
            pl.BlockSpec((tile, width), lambda i: (i, 0)),
        ],
        out_specs=pl.BlockSpec((rows, tile), lambda i: (0, i)),
        out_shape=jax.ShapeDtypeStruct((rows, features), F32),
        compiler_params=params(20),
        cost_estimate=LIGHT,
    )(cotangent, head)


def merge(first, second):
    peak = jnp.maximum(first[0], second[0])
    one = jnp.exp(first[0] - peak) * first[1]
    two = jnp.exp(second[0] - peak) * second[1]
    total = one + two
    mean = (one * first[2] + two * second[2]) / total
    return jnp.stack([peak, total, mean] + [first[i] + second[i] for i in range(3, len(first))])


def exchange(value, size):
    half = value.shape[1] // 2
    other = swap(value, "vocab", 1, size)
    aligned = jnp.concatenate([other[:3, half:], other[:3, :half]], axis=1)
    value = merge(value, jnp.concatenate([aligned, other[3:]], axis=0))
    bit = PAIR
    while bit < size:
        value = merge(value, swap(value, "vocab", bit, size))
        bit *= 2
    return value


def body(hidden, steer, tangent, gain, head, target):
    seq_size = lax.axis_size("seq")
    vocab_size = lax.axis_size("vocab")
    seq_index = lax.axis_index("seq")
    vocab_index = lax.axis_index("vocab")
    tokens, feature_count = hidden.shape
    width = head.shape[0]
    rows = seq_size * tokens
    share = rows // vocab_size
    quarter = tokens // QUARTERS
    size = min(share, quarter)
    y, z = vocab_index % PAIR, vocab_index // PAIR
    length = vocab_size // PAIR
    chip = seq_index // 2
    group = 2 * y + z % 2

    def destination(block, begin):
        row = (block % 2) * tokens + begin
        owner, inside = row // share, row % share
        return ((owner % PAIR) ^ y) * tokens + owner // PAIR * share + inside

    starts = jnp.arange(tokens // size) * size
    turned = ((starts // quarter) ^ group) * quarter + starts % quarter

    def places(bits, begins):
        return jnp.concatenate(
            [destination(seq_index ^ bit, begins) for bit in bits]
        ).astype(jnp.int32)

    own_places, other_places = places((0, 1), turned), places((2, 3), turned)
    target_places = places((0, 1, 2, 3), starts)

    at = jnp.stack([seq_index, group]).astype(jnp.int32)
    vectors = jnp.stack([steer, tangent, gain])
    own, mate, over_2, over_3, sums_0, parts, two = cut(
        at, hidden, vectors, width, seq_size
    )
    mate = swap(mate, "seq", 1, seq_size)
    sums_1 = swap(sums_0, "seq", 1, seq_size)
    over_2, over_3 = swap(over_2, "seq", 2, seq_size), swap(over_3, "seq", 3, seq_size)
    both = swap(jnp.stack([sums_0, sums_1]), "seq", 2, seq_size)
    near = jnp.stack([over_2[:quarter], over_3[:quarter]])
    by_y = swap(near, "vocab", 2, vocab_size)
    by_z = swap(near, "vocab", 1, vocab_size)
    steer_part, gain_part = parts[0], parts[2]

    def partial_logits(block, sums_of):
        radius = jnp.sqrt(sums_of[0] / feature_count + EPSILON)
        values = block.astype(F32) + steer_part
        normed = (gain_part * values / radius[:, None]).astype(BF16)
        return jnp.dot(normed, head, preferred_element_type=F32)

    row = jnp.sum(jnp.dot(two, head, preferred_element_type=F32), axis=0, keepdims=True)
    row = row + swap(row, "seq", 1, seq_size)
    tangent_row = row + swap(row, "seq", 2, seq_size)
    given = swap(partial_logits(mate, sums_1), "seq", 1, seq_size)
    summed_0 = partial_logits(own, sums_0) + given
    send_0, tangent_row = lax.optimization_barrier((summed_0.astype(jnp.float16), tangent_row))
    got_2 = swap(send_0, "seq", 2, seq_size)
    by_y, by_z, over_2, over_3, both, _ = lax.optimization_barrier(
        (by_y, by_z, over_2, over_3, both, send_0)
    )
    sums = [sums_0, sums_1, both[0], both[1]]
    denominators = [s[0] / feature_count + EPSILON for s in sums]

    blocks = [own, mate] + [
        jnp.concatenate([over[:quarter], by_y[i], by_z[i], over[quarter:]], axis=0)
        for i, over in enumerate((over_2, over_3))
    ]
    given = swap(partial_logits(blocks[3], sums[3]), "seq", 1, seq_size)
    summed_2 = partial_logits(blocks[2], sums[2]) + given
    send_2, got_2 = lax.optimization_barrier((summed_2.astype(jnp.float16), got_2))
    got_0 = swap(send_2, "seq", 2, seq_size)

    half = rows // 2

    def half_of(base, summed, got, where, extra):
        full = summed + got.astype(F32)
        mates = swap(full, "seq", 1, seq_size)
        both, stats = soften(
            where, full, mates, tangent_row, sums[base], sums[base + 1], feature_count
        )
        stats = stats[:3]
        joint = exchange(jnp.concatenate([stats] + extra), vocab_size)
        raw = back(both.reshape(2 * half, -1), head)
        scale = jnp.exp(stats[0] - joint[0]) / joint[1]
        lean = scale * (stats[2] - joint[2])
        plain = scale[:, None] * raw[:half]
        ggn = scale[:, None] * raw[half:] + lean[:, None] * raw[:half]
        return plain, ggn[half // 2 :].astype(BF16), ggn[: half // 2], joint

    plain_other, theirs_other, kept_other, _ = half_of(2, summed_2, got_2, other_places, [])
    got_0, target, theirs_other = lax.optimization_barrier((got_0, target, theirs_other))
    got_other = swap(theirs_other, "vocab", 1, vocab_size)
    own_total = jnp.sum(target.astype(F32), axis=1)
    plain_own, theirs_own, kept_own, joint = half_of(
        0, summed_0, got_0, own_places, [jnp.concatenate([own_total, own_total])[None]]
    )

    target_2 = swap(target, "seq", 2, seq_size)
    target_1 = swap(target, "seq", 1, seq_size)
    target_3 = swap(target_2, "seq", 1, seq_size)
    total_0 = jnp.broadcast_to(joint[3, :tokens], (8, tokens))
    total_1 = swap(total_0, "seq", 1, seq_size)
    both = swap(jnp.stack([total_0, total_1]), "seq", 2, seq_size)
    ordered, columns = order(
        target_places,
        [target, target_1, target_2, target_3],
        [total_0, total_1, both[0], both[1]],
    )
    ordered, theirs_own = lax.optimization_barrier((ordered, theirs_own))
    weighed = back(ordered, head)
    inverse = columns[:, 0:1]
    gradients = [
        plain - inverse[begin : begin + half] * weighed[begin : begin + half]
        for plain, begin in ((plain_own, 0), (plain_other, half))
    ]

    def halve(joined, bit):
        if bit < length // 2:
            joined = joined.reshape(-1, 2, share, joined.shape[-1])
            place, axis = (z // bit) % 2, 1
        else:
            joined = joined.reshape(2, -1, share, joined.shape[-1])
            place, axis = (z // bit) ^ chip, 0
        sent = lax.dynamic_index_in_dim(joined, 1 - place, axis, False)
        kept = lax.dynamic_index_in_dim(joined, place, axis, False)
        return sent.astype(BF16), kept

    got_own = swap(theirs_own, "vocab", 1, vocab_size)
    chunks = []
    for begin in (0, width // 2):
        part = [g[:, begin : begin + width // 2] for g in gradients]
        chunks.append(
            (
                jnp.concatenate([p[half // 2 :] for p in part]).astype(BF16),
                jnp.concatenate([p[: half // 2] for p in part]),
            )
        )
    got_own, got_other, *sends = lax.optimization_barrier(
        (got_own, got_other, chunks[0][0], chunks[1][0])
    )
    ggn = jnp.concatenate(
        [kept_own + got_own.astype(F32), kept_other + got_other.astype(F32)], axis=0
    )
    bits = [1]
    bit = 1
    while bit < length:
        bits.append(bit * PAIR)
        bit *= 2
    items = [[1, *halve(ggn, 1)]] + [[0, sent, chunk[1]] for sent, chunk in zip(sends, chunks)]
    tick = 0
    while any(item[0] < len(bits) for item in items):
        active = [
            i for i, item in enumerate(items) if item[0] < len(bits) and i <= tick + 1
        ]
        got = [swap(items[i][1], "vocab", bits[items[i][0]], vocab_size) for i in active]
        waiting = [i for i, item in enumerate(items) if i not in active and item[0] == 0]
        tied = lax.optimization_barrier((got, [items[i][1] for i in waiting]))
        for i, value in zip(waiting, tied[1]):
            items[i][1] = value
        for i, value in zip(active, tied[0]):
            step, _, kept = items[i]
            joined = kept + value.astype(F32)
            if step + 1 < len(bits):
                items[i] = [step + 1, *halve(joined, bits[step + 1] // PAIR)]
            else:
                items[i] = [step + 1, None, joined.reshape(share, -1)]
        tick += 1
    ggn_mine = items[0][2]
    grad_mine = jnp.concatenate([items[1][2], items[2][2]], axis=1)

    first_row = vocab_index * share
    owner = first_row // tokens
    block = owner ^ seq_index

    def choose(options):
        result = options[0]
        for index in range(1, len(options)):
            result = jnp.where(block == index, options[index], result)
        return result

    def gather_rows(options):
        pieces = []
        for begin in range(0, share, size):
            inside = first_row % tokens + begin
            place = ((inside // quarter) ^ group) * quarter + inside % quarter
            pieces.append(
                choose([lax.dynamic_slice_in_dim(o, place, size, 0) for o in options])
            )
        return jnp.concatenate(pieces, axis=0)

    my_inputs = gather_rows(blocks).astype(F32) + steer_part
    my_denominator = gather_rows(denominators)
    my_radius = jnp.sqrt(my_denominator)

    scaled = [gain_part * upstream for upstream in (grad_mine, ggn_mine)]
    dotted = jnp.stack([jnp.sum(my_inputs * value, axis=1) for value in scaled])
    dotted = dotted + swap(dotted, "seq", 1, seq_size)
    dotted = dotted + swap(dotted, "seq", 2, seq_size)
    along = dotted / feature_count / my_denominator
    return tuple(
        (value - my_inputs * along[i][:, None]) / my_radius[:, None]
        for i, value in enumerate(scaled)
    )


def solution(mesh):
    return jax.shard_map(
        body,
        mesh=mesh,
        in_specs=(P("seq", None), P(), P(), P(), P("seq", "vocab"), P("seq", "vocab")),
        out_specs=(P("vocab", "seq"), P("vocab", "seq")),
        check_vma=False,
    )
```

```python
import functools

import jax
import jax.numpy as jnp
from jax import lax
from jax.experimental import pallas as pl
from jax.experimental.pallas import tpu as pltpu
from jax.sharding import PartitionSpec as P

EPSILON = 1e-06
NT = (((1,), (1,)), ((), ()))
QUARTERS = 4
PAIR = 2
LIGHT = pl.CostEstimate(flops=0, bytes_accessed=0, transcendentals=0)
F32, BF16 = jnp.float32, jnp.bfloat16


def params(mebibytes):
    return pltpu.CompilerParams(vmem_limit_bytes=mebibytes * 1024 * 1024)


def whole_spec():
    return pl.BlockSpec(memory_space=pltpu.VMEM)


def smem_spec():
    return pl.BlockSpec(memory_space=pltpu.SMEM)


def swap(value, axis, bit, size):
    return lax.ppermute(value, axis, [(i, i ^ bit) for i in range(size)])


def lanes(columns, rows):
    lane = lax.broadcasted_iota(jnp.int32, (rows, 128), 1)
    tile = jnp.zeros((rows, 128), F32)
    for index, column in enumerate(columns):
        tile = jnp.where(lane == index, column, tile)
    return tile


def turn(rows8):
    return jnp.concatenate([rows8, jnp.zeros((120, 128), F32)], axis=0).T


def cut_kernel(width, seq_size, at, hidden, vectors, *outs):
    own, mate, over_2, over_3, sums, parts, two = outs
    seq_index, group = at[0], at[1]
    rows = hidden.shape[0]
    size = rows // QUARTERS

    def quarter(place):
        return pl.ds(pl.multiple_of((place ^ group) * size, size), size)

    def features(bit):
        return pl.ds(pl.multiple_of((seq_index ^ bit) * width, width), width)

    for out, bit in ((over_2, 2), (over_3, 3)):
        out[0:size, :] = hidden[quarter(0), features(bit)]
        out[size:, :] = hidden[quarter(3), features(bit)]
    steer, tangent = vectors[0:1, :], vectors[1:2, :]
    columns = []
    for place in range(QUARTERS):
        spot = pl.ds(place * size, size)
        own[spot, :] = hidden[quarter(place), features(0)]
        mate[spot, :] = hidden[quarter(place), features(1)]
        inputs = hidden[quarter(place), :].astype(F32) + steer
        columns.append(
            lanes(
                [
                    jnp.sum(inputs * inputs, axis=1, keepdims=True),
                    jnp.sum(inputs * tangent, axis=1, keepdims=True),
                ],
                size,
            )
        )
    sums[...] = jnp.concatenate(columns, axis=0).T[:8]
    mine = vectors[:, features(0)]
    parts[...] = mine
    line = mine[1:2] * mine[2:3]
    high = line.astype(BF16).astype(F32)
    two[...] = jnp.concatenate(
        [high, line - high, jnp.zeros((14, width), F32)], axis=0
    ).astype(BF16)


def cut(at, hidden, vectors, width, seq_size):
    rows = hidden.shape[0]
    piece = jax.ShapeDtypeStruct((2 * (rows // QUARTERS), width), BF16)
    block = jax.ShapeDtypeStruct((rows, width), BF16)
    return pl.pallas_call(
        functools.partial(cut_kernel, width, seq_size),
        in_specs=[smem_spec(), whole_spec(), whole_spec()],
        out_specs=[whole_spec()] * 7,
        out_shape=[
            block,
            block,
            piece,
            piece,
            jax.ShapeDtypeStruct((8, rows), F32),
            jax.ShapeDtypeStruct((vectors.shape[0], width), F32),
            jax.ShapeDtypeStruct((16, width), BF16),
        ],
        compiler_params=params(12),
        cost_estimate=LIGHT,
    )(at, hidden, vectors)


def ahead_kernel(feature_count, first, second, sums_a, sums_b, parts, two, head, *outs):
    out_a, out_b, out_row, normed = outs
    tokens = first.shape[0]

    @pl.when(pl.program_id(0) == 0)
    def _():
        steer, gain = parts[0:1, :], parts[2:3, :]
        for index, (block, sums) in enumerate(((first, sums_a), (second, sums_b))):
            radius = jnp.sqrt(turn(sums[...])[:, 0:1] / feature_count + EPSILON)
            values = block[...].astype(F32) + steer
            normed[index * tokens : (index + 1) * tokens, :] = (
                gain * values / radius
            ).astype(BF16)
        normed[2 * tokens :, :] = two[...]

    product = jnp.dot(normed[...], head[...], preferred_element_type=F32)
    out_a[...] = product[:tokens]
    out_b[...] = product[tokens : 2 * tokens]
    out_row[...] = product[2 * tokens : 2 * tokens + 8]


def ahead(first, second, sums_a, sums_b, parts, two, head, feature_count):
    tokens, width = first.shape
    vocab = head.shape[1]
    tile = 256
    fixed = [
        pl.BlockSpec(value.shape, lambda i: (0, 0))
        for value in (first, second, sums_a, sums_b, parts, two)
    ]
    out = pl.BlockSpec((tokens, tile), lambda i: (0, i))
    return pl.pallas_call(
        functools.partial(ahead_kernel, feature_count),
        grid=(pl.cdiv(vocab, tile),),
        in_specs=fixed + [pl.BlockSpec((width, tile), lambda i: (0, i))],
        out_specs=[out, out, pl.BlockSpec((8, tile), lambda i: (0, i))],
        out_shape=[
            jax.ShapeDtypeStruct((tokens, vocab), F32),
            jax.ShapeDtypeStruct((tokens, vocab), F32),
            jax.ShapeDtypeStruct((8, vocab), F32),
        ],
        scratch_shapes=[pltpu.VMEM((2 * tokens + two.shape[0], width), BF16)],
        compiler_params=params(52),
        cost_estimate=LIGHT,
    )(first, second, sums_a, sums_b, parts, two, head)


def soften_kernel(feature_count, at, first, second, row, sums_a, sums_b, *outs):
    both_out, stats, tile = outs
    tokens = first.shape[0]
    count = at.shape[0]
    size = 2 * tokens // count
    line = row[0:1, :]
    for block, (source, sums) in enumerate(((first, sums_a), (second, sums_b))):
        turned = turn(sums[...])
        denominator = turned[:, 0:1] / feature_count + EPSILON
        inverse = 1.0 / jnp.sqrt(denominator)
        slope = turned[:, 1:2] / feature_count / denominator
        for piece in range(count // 2):
            begin = piece * size
            logits = source[begin : begin + size, :]
            spot = pl.ds(pl.multiple_of(at[block * (count // 2) + piece], size), size)
            peak = jnp.max(logits, axis=1, keepdims=True)
            exponent = jnp.exp(logits - peak)
            dlogits = line * inverse[begin : begin + size] - logits * slope[begin : begin + size]
            total = jnp.sum(exponent, axis=1, keepdims=True)
            mean = jnp.sum(exponent * dlogits, axis=1, keepdims=True) / total
            tilted = exponent * (dlogits - mean)
            both_out[0, spot, :] = exponent.astype(BF16)
            both_out[1, spot, :] = tilted.astype(BF16)
            tile[spot, :] = lanes([peak, total, mean], size)
    for begin in range(0, 2 * tokens, 128):
        stats[:, begin : begin + 128] = tile[begin : begin + 128, :].T[:8]


def soften(at, first, second, row, sums_a, sums_b, feature_count):
    tokens, width = first.shape
    rows = 2 * tokens
    return pl.pallas_call(
        functools.partial(soften_kernel, feature_count),
        in_specs=[smem_spec()] + [whole_spec()] * 5,
        out_specs=[whole_spec()] * 2,
        out_shape=[
            jax.ShapeDtypeStruct((2, rows, width), BF16),
            jax.ShapeDtypeStruct((8, rows), F32),
        ],
        scratch_shapes=[pltpu.VMEM((rows, 128), F32)],
        compiler_params=params(16),
        cost_estimate=LIGHT,
    )(at, first, second, row, sums_a, sums_b)


def order_kernel(at, *refs):
    blocks, totals, (ordered, columns) = refs[:4], refs[4:8], refs[8:]
    tokens = blocks[0].shape[0]
    count = at.shape[0]
    size = 4 * tokens // count
    half = 2 * tokens
    for block in range(4):
        inverse = 1.0 / turn(totals[block][...])
        for piece in range(count // 4):
            begin = piece * size
            place = at[block * (count // 4) + piece] + half * (block // 2)
            spot = pl.ds(pl.multiple_of(place, size), size)
            ordered[spot, :] = blocks[block][begin : begin + size, :]
            columns[spot, :] = inverse[begin : begin + size]


def order(at, blocks, totals):
    tokens, width = blocks[0].shape
    rows = 4 * tokens
    return pl.pallas_call(
        order_kernel,
        in_specs=[smem_spec()] + [whole_spec()] * 8,
        out_specs=[whole_spec()] * 2,
        out_shape=[
            jax.ShapeDtypeStruct((rows, width), BF16),
            jax.ShapeDtypeStruct((rows, 128), F32),
        ],
        compiler_params=params(12),
        cost_estimate=LIGHT,
    )(at, *blocks, *totals)


def back_kernel(deep, cotangent, head, out):
    width = head.shape[1]
    result = lax.dot_general(
        cotangent[:, :deep], head[:, :deep], NT, preferred_element_type=F32
    )
    if deep < width:
        result += lax.dot_general(
            cotangent[:, deep:], head[:, deep:], NT, preferred_element_type=F32
        )
    out[...] = result


def back(cotangent, head):
    rows, width = cotangent.shape
    features = head.shape[0]
    tile = 256 if features % 256 == 0 else features
    deep = width // 256 * 256 or width
    return pl.pallas_call(
        functools.partial(back_kernel, deep),
        grid=(features // tile,),
        in_specs=[
            pl.BlockSpec((rows, width), lambda i: (0, 0)),
            pl.BlockSpec((tile, width), lambda i: (i, 0)),
        ],
        out_specs=pl.BlockSpec((rows, tile), lambda i: (0, i)),
        out_shape=jax.ShapeDtypeStruct((rows, features), F32),
        compiler_params=params(52),
        cost_estimate=LIGHT,
    )(cotangent, head)


def merge(first, second):
    peak = jnp.maximum(first[0], second[0])
    one = jnp.exp(first[0] - peak) * first[1]
    two = jnp.exp(second[0] - peak) * second[1]
    total = one + two
    mean = (one * first[2] + two * second[2]) / total
    return jnp.stack([peak, total, mean] + [first[i] + second[i] for i in range(3, len(first))])


def exchange(value, size, beside):
    other, beside = lax.optimization_barrier((swap(value, "vocab", 1, size), beside))
    aligned = other[:3].reshape(3, 2, 2, -1)[:, :, ::-1].reshape(3, -1)
    value = merge(value, jnp.concatenate([aligned, other[3:]], axis=0))
    bit = PAIR
    while bit < size:
        value = merge(value, swap(value, "vocab", bit, size))
        bit *= 2
    return value, beside


def body(hidden, steer, tangent, gain, head, target):
    seq_size = lax.axis_size("seq")
    vocab_size = lax.axis_size("vocab")
    seq_index = lax.axis_index("seq")
    vocab_index = lax.axis_index("vocab")
    tokens, feature_count = hidden.shape
    width = head.shape[0]
    rows = seq_size * tokens
    share = rows // vocab_size
    quarter = tokens // QUARTERS
    size = min(share, quarter)
    y, z = vocab_index % PAIR, vocab_index // PAIR
    length = vocab_size // PAIR
    chip = seq_index // 2
    group = 2 * y + z % 2

    def destination(block, begin):
        row = (block % 2) * tokens + begin
        owner, inside = row // share, row % share
        return ((owner % PAIR) ^ y) * tokens + owner // PAIR * share + inside

    starts = jnp.arange(tokens // size) * size
    turned = ((starts // quarter) ^ group) * quarter + starts % quarter

    def places(bits, begins):
        return jnp.concatenate(
            [destination(seq_index ^ bit, begins) for bit in bits]
        ).astype(jnp.int32)

    own_places, other_places = places((0, 1), turned), places((2, 3), turned)
    target_places = places((0, 1, 2, 3), starts)

    at = jnp.stack([seq_index, group]).astype(jnp.int32)
    vectors = jnp.stack([steer, tangent, gain])
    own, mate, over_2, over_3, sums_0, parts, two = cut(
        at, hidden, vectors, width, seq_size
    )
    mate = swap(mate, "seq", 1, seq_size)
    sums_1 = swap(sums_0, "seq", 1, seq_size)
    over_2, over_3 = swap(over_2, "seq", 2, seq_size), swap(over_3, "seq", 3, seq_size)
    both = swap(jnp.stack([sums_0, sums_1]), "seq", 2, seq_size)
    near = jnp.stack([over_2[:quarter], over_3[:quarter]])
    by_y = swap(near, "vocab", 2, vocab_size)
    by_z = swap(near, "vocab", 1, vocab_size)
    steer_part, gain_part = parts[0], parts[2]

    kept, given, row = ahead(own, mate, sums_0, sums_1, parts, two, head, feature_count)
    row = row[0:1] + row[1:2]
    row = row + swap(row, "seq", 1, seq_size)
    tangent_row = row + swap(row, "seq", 2, seq_size)
    summed_0 = kept + swap(given, "seq", 1, seq_size)
    send_0, tangent_row = lax.optimization_barrier((summed_0.astype(jnp.float16), tangent_row))
    got_2 = swap(send_0, "seq", 2, seq_size)
    by_y, by_z, over_2, over_3, both, _ = lax.optimization_barrier(
        (by_y, by_z, over_2, over_3, both, send_0)
    )
    sums = [sums_0, sums_1, both[0], both[1]]
    denominators = [s[0] / feature_count + EPSILON for s in sums]

    blocks = [own, mate] + [
        jnp.concatenate([over[:quarter], by_y[i], by_z[i], over[quarter:]], axis=0)
        for i, over in enumerate((over_2, over_3))
    ]
    kept, given, _ = ahead(
        blocks[2], blocks[3], sums[2], sums[3], parts, two, head, feature_count
    )
    summed_2 = kept + swap(given, "seq", 1, seq_size)
    send_2, got_2 = lax.optimization_barrier((summed_2.astype(jnp.float16), got_2))
    got_0 = swap(send_2, "seq", 2, seq_size)

    half = rows // 2

    def half_of(base, summed, got, where):
        full = summed + got.astype(F32)
        mates = swap(full, "seq", 1, seq_size)
        both, stats = soften(
            where, full, mates, tangent_row, sums[base], sums[base + 1], feature_count
        )
        return back(both.reshape(2 * half, -1), head), stats[:3]

    raw_other, stats_other = half_of(2, summed_2, got_2, other_places)
    got_0, target, raw_other = lax.optimization_barrier((got_0, target, raw_other))
    target_2 = swap(target, "seq", 2, seq_size)
    raw_own, stats_own = half_of(0, summed_0, got_0, own_places)
    stats = jnp.concatenate([stats_own, stats_other], axis=1)
    own_total = jnp.sum(target.astype(F32), axis=1)
    joint, (raw_own,) = exchange(
        jnp.concatenate([stats, jnp.tile(own_total, seq_size)[None]]), vocab_size, (raw_own,)
    )
    scale = jnp.exp(stats[0] - joint[0]) / joint[1]
    lean = scale * (stats[2] - joint[2])

    form = (2, PAIR, length // 2, share)

    def spread(values):
        return values.reshape(*form, -1)

    scale_5, lean_5 = scale.reshape(*form, 1), lean.reshape(*form, 1)
    parted = ((0, width // 2), (width // 2, width))

    def plain_of(begin, end):
        return scale_5 * spread(
            jnp.concatenate([raw_own[:half, begin:end], raw_other[:half, begin:end]])
        )

    def ggn_of(begin, end):
        plain = jnp.concatenate([raw_own[:half, begin:end], raw_other[:half, begin:end]])
        tilted = jnp.concatenate([raw_own[half:, begin:end], raw_other[half:, begin:end]])
        return scale_5 * spread(tilted) + lean_5 * spread(plain)

    def halve(values, bit):
        if bit == 1:
            return values[:, 1:].astype(BF16), values[:, :1]
        step = bit // PAIR
        if step < length // 2:
            shape = values.shape
            values = values.reshape(*shape[:2], -1, 2, *shape[3:])
            place, axis = (z // step) % 2, 3
            sent = lax.dynamic_index_in_dim(values, 1 - place, axis, False)
            kept = lax.dynamic_index_in_dim(values, place, axis, False)
        else:
            place = (z // step) ^ chip
            sent = lax.dynamic_index_in_dim(values, 1 - place, 0, True)
            kept = lax.dynamic_index_in_dim(values, place, 0, True)
        return sent.astype(BF16), kept

    z_bits = []
    bit = PAIR
    while bit < vocab_size:
        z_bits.append(bit)
        bit *= 2
    y_first, z_first = [1] + z_bits, z_bits + [1]
    items = [
        [list(bits), 0, *halve(ggn_of(*part), bits[0])]
        for bits, part in ((y_first, parted[0]), (z_first, parted[1]))
    ]

    target_2, joint_total, items[0][2], items[1][2] = lax.optimization_barrier(
        (target_2, joint[3, :tokens], items[0][2], items[1][2])
    )
    target_1 = swap(target, "seq", 1, seq_size)
    target_3 = swap(target_2, "seq", 1, seq_size)
    total_0 = jnp.broadcast_to(joint_total, (8, tokens))
    total_1 = swap(total_0, "seq", 1, seq_size)
    both = swap(jnp.stack([total_0, total_1]), "seq", 2, seq_size)
    ordered, columns = order(
        target_places,
        [target, target_1, target_2, target_3],
        [total_0, total_1, both[0], both[1]],
    )
    weighed = back(ordered, head)
    inverse = columns[:, 0:1]
    for tick, (begin, end) in enumerate(parted):
        values = plain_of(begin, end) - spread(inverse * weighed[:, begin:end])
        items.append([list(y_first), tick + 1, *halve(values, 1)])

    tick = 0
    while any(item[0] for item in items):
        active = [item for item in items if item[0] and item[1] <= tick]
        waiting = [item for item in items if item[1] > tick]
        got = [swap(item[2], "vocab", item[0][0], vocab_size) for item in active]
        got, held = lax.optimization_barrier((got, [item[2] for item in waiting]))
        for item, value in zip(waiting, held):
            item[2] = value
        for item, value in zip(active, got):
            item[0].pop(0)
            item[3] = item[3] + value.astype(F32)
            if item[0]:
                item[2:] = halve(item[3], item[0][0])
        tick += 1
    summed = [item[3].reshape(share, -1) for item in items]
    ggn_mine = jnp.concatenate(summed[:2], axis=1)
    grad_mine = jnp.concatenate(summed[2:], axis=1)

    first_row = vocab_index * share
    owner = first_row // tokens
    block = owner ^ seq_index

    def choose(options):
        result = options[0]
        for index in range(1, len(options)):
            result = jnp.where(block == index, options[index], result)
        return result

    def gather_rows(options):
        pieces = []
        for begin in range(0, share, size):
            inside = first_row % tokens + begin
            place = ((inside // quarter) ^ group) * quarter + inside % quarter
            pieces.append(
                choose([lax.dynamic_slice_in_dim(o, place, size, 0) for o in options])
            )
        return jnp.concatenate(pieces, axis=0)

    my_inputs = gather_rows(blocks).astype(F32) + steer_part
    my_denominator = gather_rows(denominators)
    my_radius = jnp.sqrt(my_denominator)

    scaled = [gain_part * upstream for upstream in (grad_mine, ggn_mine)]
    dotted = jnp.stack([jnp.sum(my_inputs * value, axis=1) for value in scaled])
    dotted = dotted + swap(dotted, "seq", 1, seq_size)
    dotted = dotted + swap(dotted, "seq", 2, seq_size)
    along = dotted / feature_count / my_denominator
    return tuple(
        (value - my_inputs * along[i][:, None]) / my_radius[:, None]
        for i, value in enumerate(scaled)
    )


def solution(mesh):
    return jax.shard_map(
        body,
        mesh=mesh,
        in_specs=(P("seq", None), P(), P(), P(), P("seq", "vocab"), P("seq", "vocab")),
        out_specs=(P("vocab", "seq"), P("vocab", "seq")),
        check_vma=False,
    )
```

```python
import functools

import jax
import jax.numpy as jnp
from jax import lax
from jax.experimental import pallas as pl
from jax.experimental.pallas import tpu as pltpu
from jax.sharding import PartitionSpec as P

EPSILON = 1e-06
NT = (((1,), (1,)), ((), ()))
QUARTERS = 4
PAIR = 2
LIGHT = pl.CostEstimate(flops=0, bytes_accessed=0, transcendentals=0)
F32, BF16 = jnp.float32, jnp.bfloat16


def params(mebibytes):
    return pltpu.CompilerParams(vmem_limit_bytes=mebibytes * 1024 * 1024)


def whole_spec():
    return pl.BlockSpec(memory_space=pltpu.VMEM)


def smem_spec():
    return pl.BlockSpec(memory_space=pltpu.SMEM)


def swap(value, axis, bit, size):
    return lax.ppermute(value, axis, [(i, i ^ bit) for i in range(size)])


def lanes(columns, rows):
    lane = lax.broadcasted_iota(jnp.int32, (rows, 128), 1)
    tile = jnp.zeros((rows, 128), F32)
    for index, column in enumerate(columns):
        tile = jnp.where(lane == index, column, tile)
    return tile


def turn(rows8):
    return jnp.concatenate([rows8, jnp.zeros((120, 128), F32)], axis=0).T


def cut_kernel(width, seq_size, at, hidden, vectors, *outs):
    own, mate, over_2, over_3, sums, parts, two = outs
    seq_index, group = at[0], at[1]
    rows = hidden.shape[0]
    size = rows // QUARTERS

    def quarter(place):
        return pl.ds(pl.multiple_of((place ^ group) * size, size), size)

    def features(bit):
        return pl.ds(pl.multiple_of((seq_index ^ bit) * width, width), width)

    for out, bit in ((over_2, 2), (over_3, 3)):
        out[0:size, :] = hidden[quarter(0), features(bit)]
        out[size:, :] = hidden[quarter(3), features(bit)]
    steer, tangent = vectors[0:1, :], vectors[1:2, :]
    columns = []
    for place in range(QUARTERS):
        spot = pl.ds(place * size, size)
        own[spot, :] = hidden[quarter(place), features(0)]
        mate[spot, :] = hidden[quarter(place), features(1)]
        inputs = hidden[quarter(place), :].astype(F32) + steer
        columns.append(
            lanes(
                [
                    jnp.sum(inputs * inputs, axis=1, keepdims=True),
                    jnp.sum(inputs * tangent, axis=1, keepdims=True),
                ],
                size,
            )
        )
    sums[...] = jnp.concatenate(columns, axis=0).T[:8]
    mine = vectors[:, features(0)]
    parts[...] = mine
    line = mine[1:2] * mine[2:3]
    high = line.astype(BF16).astype(F32)
    two[...] = jnp.concatenate(
        [high, line - high, jnp.zeros((14, width), F32)], axis=0
    ).astype(BF16)


def cut(at, hidden, vectors, width, seq_size):
    rows = hidden.shape[0]
    piece = jax.ShapeDtypeStruct((2 * (rows // QUARTERS), width), BF16)
    block = jax.ShapeDtypeStruct((rows, width), BF16)
    return pl.pallas_call(
        functools.partial(cut_kernel, width, seq_size),
        in_specs=[smem_spec(), whole_spec(), whole_spec()],
        out_specs=[whole_spec()] * 7,
        out_shape=[
            block,
            block,
            piece,
            piece,
            jax.ShapeDtypeStruct((8, rows), F32),
            jax.ShapeDtypeStruct((vectors.shape[0], width), F32),
            jax.ShapeDtypeStruct((16, width), BF16),
        ],
        compiler_params=params(12),
        cost_estimate=LIGHT,
    )(at, hidden, vectors)


def soften_kernel(feature_count, at, first, second, row, sums_a, sums_b, *outs):
    both_out, stats, tile = outs
    tokens = first.shape[0]
    count = at.shape[0]
    size = 2 * tokens // count
    line = row[0:1, :]
    for block, (source, sums) in enumerate(((first, sums_a), (second, sums_b))):
        turned = turn(sums[...])
        denominator = turned[:, 0:1] / feature_count + EPSILON
        inverse = 1.0 / jnp.sqrt(denominator)
        slope = turned[:, 1:2] / feature_count / denominator
        for piece in range(count // 2):
            begin = piece * size
            logits = source[begin : begin + size, :]
            spot = pl.ds(pl.multiple_of(at[block * (count // 2) + piece], size), size)
            peak = jnp.max(logits, axis=1, keepdims=True)
            exponent = jnp.exp(logits - peak)
            dlogits = line * inverse[begin : begin + size] - logits * slope[begin : begin + size]
            total = jnp.sum(exponent, axis=1, keepdims=True)
            mean = jnp.sum(exponent * dlogits, axis=1, keepdims=True) / total
            tilted = exponent * (dlogits - mean)
            both_out[0, spot, :] = exponent.astype(BF16)
            both_out[1, spot, :] = tilted.astype(BF16)
            tile[spot, :] = lanes([peak, total, mean], size)
    for begin in range(0, 2 * tokens, 128):
        stats[:, begin : begin + 128] = tile[begin : begin + 128, :].T[:8]


def soften(at, first, second, row, sums_a, sums_b, feature_count):
    tokens, width = first.shape
    rows = 2 * tokens
    return pl.pallas_call(
        functools.partial(soften_kernel, feature_count),
        in_specs=[smem_spec()] + [whole_spec()] * 5,
        out_specs=[whole_spec()] * 2,
        out_shape=[
            jax.ShapeDtypeStruct((2, rows, width), BF16),
            jax.ShapeDtypeStruct((8, rows), F32),
        ],
        scratch_shapes=[pltpu.VMEM((rows, 128), F32)],
        compiler_params=params(16),
        cost_estimate=LIGHT,
    )(at, first, second, row, sums_a, sums_b)


def order_kernel(at, *refs):
    blocks, totals, (ordered, columns) = refs[:4], refs[4:8], refs[8:]
    tokens = blocks[0].shape[0]
    count = at.shape[0]
    size = 4 * tokens // count
    half = 2 * tokens
    for block in range(4):
        inverse = 1.0 / turn(totals[block][...])
        for piece in range(count // 4):
            begin = piece * size
            place = at[block * (count // 4) + piece] + half * (block // 2)
            spot = pl.ds(pl.multiple_of(place, size), size)
            ordered[spot, :] = blocks[block][begin : begin + size, :]
            columns[spot, :] = inverse[begin : begin + size]


def order(at, blocks, totals):
    tokens, width = blocks[0].shape
    rows = 4 * tokens
    return pl.pallas_call(
        order_kernel,
        in_specs=[smem_spec()] + [whole_spec()] * 8,
        out_specs=[whole_spec()] * 2,
        out_shape=[
            jax.ShapeDtypeStruct((rows, width), BF16),
            jax.ShapeDtypeStruct((rows, 128), F32),
        ],
        compiler_params=params(12),
        cost_estimate=LIGHT,
    )(at, *blocks, *totals)


STREAMS = 4


def back_kernel(deep, *refs):
    cotangents, heads = refs[:STREAMS], refs[STREAMS : 2 * STREAMS]
    out, left = refs[2 * STREAMS :]
    rows, part = cotangents[0].shape[0], heads[0].shape[0]
    width = left.shape[1]

    @pl.when(pl.program_id(0) == 0)
    def _():
        for index, source in enumerate(cotangents):
            left[index * rows : (index + 1) * rows, :] = source[...]

    head = jnp.concatenate([value[...] for value in heads], axis=0)
    result = lax.dot_general(left[:, :deep], head[:, :deep], NT, preferred_element_type=F32)
    if deep < width:
        result += lax.dot_general(
            left[:, deep:], head[:, deep:], NT, preferred_element_type=F32
        )
    out[...] = result


def back(cotangent, head):
    rows, width = cotangent.shape
    features = head.shape[0]
    tile = 256 if features % 256 == 0 else features
    deep = width // 256 * 256 or width

    def row_block(index):
        return pl.BlockSpec((rows // STREAMS, width), lambda i: (index, 0))

    def head_block(index):
        return pl.BlockSpec((tile // STREAMS, width), lambda i: (STREAMS * i + index, 0))

    return pl.pallas_call(
        functools.partial(back_kernel, deep),
        grid=(features // tile,),
        in_specs=[row_block(index) for index in range(STREAMS)]
        + [head_block(index) for index in range(STREAMS)],
        out_specs=pl.BlockSpec((rows, tile), lambda i: (0, i)),
        out_shape=jax.ShapeDtypeStruct((rows, features), F32),
        scratch_shapes=[pltpu.VMEM((rows, width), BF16)],
        compiler_params=params(52),
        cost_estimate=LIGHT,
    )(*([cotangent] * STREAMS), *([head] * STREAMS))


def merge(first, second):
    peak = jnp.maximum(first[0], second[0])
    one = jnp.exp(first[0] - peak) * first[1]
    two = jnp.exp(second[0] - peak) * second[1]
    total = one + two
    mean = (one * first[2] + two * second[2]) / total
    return jnp.stack([peak, total, mean] + [first[i] + second[i] for i in range(3, len(first))])


def exchange(value, size, beside):
    half = value.shape[1] // 2
    other, beside = lax.optimization_barrier((swap(value, "vocab", 1, size), beside))
    aligned = jnp.concatenate([other[:3, half:], other[:3, :half]], axis=1)
    value = merge(value, jnp.concatenate([aligned, other[3:]], axis=0))
    bit = PAIR
    while bit < size:
        value = merge(value, swap(value, "vocab", bit, size))
        bit *= 2
    return value, beside


def body(hidden, steer, tangent, gain, head, target):
    seq_size = lax.axis_size("seq")
    vocab_size = lax.axis_size("vocab")
    seq_index = lax.axis_index("seq")
    vocab_index = lax.axis_index("vocab")
    tokens, feature_count = hidden.shape
    width = head.shape[0]
    rows = seq_size * tokens
    share = rows // vocab_size
    quarter = tokens // QUARTERS
    size = min(share, quarter)
    y, z = vocab_index % PAIR, vocab_index // PAIR
    length = vocab_size // PAIR
    chip = seq_index // 2
    group = 2 * y + z % 2

    def destination(block, begin):
        row = (block % 2) * tokens + begin
        owner, inside = row // share, row % share
        return ((owner % PAIR) ^ y) * tokens + owner // PAIR * share + inside

    starts = jnp.arange(tokens // size) * size
    turned = ((starts // quarter) ^ group) * quarter + starts % quarter

    def places(bits, begins):
        return jnp.concatenate(
            [destination(seq_index ^ bit, begins) for bit in bits]
        ).astype(jnp.int32)

    own_places, other_places = places((0, 1), turned), places((2, 3), turned)
    target_places = places((0, 1, 2, 3), starts)

    at = jnp.stack([seq_index, group]).astype(jnp.int32)
    vectors = jnp.stack([steer, tangent, gain])
    own, mate, over_2, over_3, sums_0, parts, two = cut(
        at, hidden, vectors, width, seq_size
    )
    mate = swap(mate, "seq", 1, seq_size)
    sums_1 = swap(sums_0, "seq", 1, seq_size)
    over_2, over_3 = swap(over_2, "seq", 2, seq_size), swap(over_3, "seq", 3, seq_size)
    both = swap(jnp.stack([sums_0, sums_1]), "seq", 2, seq_size)
    near = jnp.stack([over_2[:quarter], over_3[:quarter]])
    by_y = swap(near, "vocab", 2, vocab_size)
    by_z = swap(near, "vocab", 1, vocab_size)
    steer_part, gain_part = parts[0], parts[2]

    def partial_logits(block, sums_of):
        radius = jnp.sqrt(sums_of[0] / feature_count + EPSILON)
        values = block.astype(F32) + steer_part
        normed = (gain_part * values / radius[:, None]).astype(BF16)
        return jnp.dot(normed, head, preferred_element_type=F32)

    given = partial_logits(mate, sums_1)
    two, given = lax.optimization_barrier((two, given))
    given = swap(given, "seq", 1, seq_size)
    row = jnp.sum(jnp.dot(two, head, preferred_element_type=F32), axis=0, keepdims=True)
    row = row + swap(row, "seq", 1, seq_size)
    tangent_row = row + swap(row, "seq", 2, seq_size)
    summed_0 = partial_logits(own, sums_0) + given
    send_0, tangent_row = lax.optimization_barrier((summed_0.astype(jnp.float16), tangent_row))
    got_2 = swap(send_0, "seq", 2, seq_size)
    by_y, by_z, over_2, over_3, both, _ = lax.optimization_barrier(
        (by_y, by_z, over_2, over_3, both, send_0)
    )
    sums = [sums_0, sums_1, both[0], both[1]]
    denominators = [s[0] / feature_count + EPSILON for s in sums]

    blocks = [own, mate] + [
        jnp.concatenate([over[:quarter], by_y[i], by_z[i], over[quarter:]], axis=0)
        for i, over in enumerate((over_2, over_3))
    ]
    given = swap(partial_logits(blocks[3], sums[3]), "seq", 1, seq_size)
    summed_2 = partial_logits(blocks[2], sums[2]) + given
    send_2, got_2 = lax.optimization_barrier((summed_2.astype(jnp.float16), got_2))
    got_0 = swap(send_2, "seq", 2, seq_size)

    half = rows // 2

    def soften_of(base, summed, got, where):
        full = summed + got.astype(F32)
        mates = swap(full, "seq", 1, seq_size)
        both, stats = soften(
            where, full, mates, tangent_row, sums[base], sums[base + 1], feature_count
        )
        return both.reshape(2 * half, -1), stats[:3]

    def scaled_of(raw, stats, joint):
        scale = jnp.exp(stats[0] - joint[0]) / joint[1]
        lean = scale * (stats[2] - joint[2])
        plain = scale[:, None] * raw[:half]
        ggn = scale[:, None] * raw[half:] + lean[:, None] * raw[:half]
        return plain, ggn[half // 2 :].astype(BF16), ggn[: half // 2]

    both_other, stats_other = soften_of(2, summed_2, got_2, other_places)
    raw_other = back(both_other, head)
    got_0, target, raw_other, stats_other = lax.optimization_barrier(
        (got_0, target, raw_other, stats_other)
    )
    target_2 = swap(target, "seq", 2, seq_size)
    joint_other, raw_other = exchange(stats_other, vocab_size, raw_other)
    plain_other, theirs_other, kept_other = scaled_of(raw_other, stats_other, joint_other)
    got_other = swap(theirs_other, "vocab", 1, vocab_size)

    both_own, stats_own = soften_of(0, summed_0, got_0, own_places)
    stats_own, theirs_other = lax.optimization_barrier((stats_own, theirs_other))
    own_total = jnp.sum(target.astype(F32), axis=1)
    joint, raw_own = exchange(
        jnp.concatenate([stats_own, jnp.concatenate([own_total, own_total])[None]]),
        vocab_size,
        back(both_own, head),
    )
    plain_own, theirs_own, kept_own = scaled_of(raw_own, stats_own, joint)
    got_own = swap(theirs_own, "vocab", 1, vocab_size)

    target_2, late_target, joint_total, _ = lax.optimization_barrier(
        (target_2, target, joint[3, :tokens], theirs_own)
    )
    target_1 = swap(late_target, "seq", 1, seq_size)
    target_3 = swap(target_2, "seq", 1, seq_size)
    total_0 = jnp.broadcast_to(joint_total, (8, tokens))
    total_1 = swap(total_0, "seq", 1, seq_size)
    both = swap(jnp.stack([total_0, total_1]), "seq", 2, seq_size)
    ordered, columns = order(
        target_places,
        [target, target_1, target_2, target_3],
        [total_0, total_1, both[0], both[1]],
    )
    weighed = back(ordered, head)
    inverse = columns[:, 0:1]
    gradients = [
        plain - inverse[begin : begin + half] * weighed[begin : begin + half]
        for plain, begin in ((plain_own, 0), (plain_other, half))
    ]

    def halve(joined, bit):
        if bit < length // 2:
            joined = joined.reshape(-1, 2, share, joined.shape[-1])
            place, axis = (z // bit) % 2, 1
        else:
            joined = joined.reshape(2, -1, share, joined.shape[-1])
            place, axis = (z // bit) ^ chip, 0
        sent = lax.dynamic_index_in_dim(joined, 1 - place, axis, False)
        kept = lax.dynamic_index_in_dim(joined, place, axis, False)
        return sent.astype(BF16), kept

    chunks = []
    for begin in (0, width // 2):
        part = [g[:, begin : begin + width // 2] for g in gradients]
        chunks.append(
            (
                jnp.concatenate([p[half // 2 :] for p in part]).astype(BF16),
                jnp.concatenate([p[: half // 2] for p in part]),
            )
        )
    got_own, got_other, *sends = lax.optimization_barrier(
        (got_own, got_other, chunks[0][0], chunks[1][0])
    )
    ggn = jnp.concatenate(
        [kept_own + got_own.astype(F32), kept_other + got_other.astype(F32)], axis=0
    )
    bits = [1]
    bit = 1
    while bit < length:
        bits.append(bit * PAIR)
        bit *= 2
    items = [[1, *halve(ggn, 1)]] + [[0, sent, chunk[1]] for sent, chunk in zip(sends, chunks)]
    tick = 0
    while any(item[0] < len(bits) for item in items):
        active = [
            i for i, item in enumerate(items) if item[0] < len(bits) and i <= tick + 1
        ]
        got = [swap(items[i][1], "vocab", bits[items[i][0]], vocab_size) for i in active]
        waiting = [i for i, item in enumerate(items) if i not in active and item[0] == 0]
        tied = lax.optimization_barrier((got, [items[i][1] for i in waiting]))
        for i, value in zip(waiting, tied[1]):
            items[i][1] = value
        for i, value in zip(active, tied[0]):
            step, _, kept = items[i]
            joined = kept + value.astype(F32)
            if step + 1 < len(bits):
                items[i] = [step + 1, *halve(joined, bits[step + 1] // PAIR)]
            else:
                items[i] = [step + 1, None, joined.reshape(share, -1)]
        tick += 1
    ggn_mine = items[0][2]
    grad_mine = jnp.concatenate([items[1][2], items[2][2]], axis=1)

    first_row = vocab_index * share
    owner = first_row // tokens
    block = owner ^ seq_index

    def choose(options):
        result = options[0]
        for index in range(1, len(options)):
            result = jnp.where(block == index, options[index], result)
        return result

    def gather_rows(options):
        pieces = []
        for begin in range(0, share, size):
            inside = first_row % tokens + begin
            place = ((inside // quarter) ^ group) * quarter + inside % quarter
            pieces.append(
                choose([lax.dynamic_slice_in_dim(o, place, size, 0) for o in options])
            )
        return jnp.concatenate(pieces, axis=0)

    my_inputs = gather_rows(blocks).astype(F32) + steer_part
    my_denominator = gather_rows(denominators)
    my_radius = jnp.sqrt(my_denominator)

    scaled = [gain_part * upstream for upstream in (grad_mine, ggn_mine)]
    dotted = jnp.stack([jnp.sum(my_inputs * value, axis=1) for value in scaled])
    dotted = dotted + swap(dotted, "seq", 1, seq_size)
    dotted = dotted + swap(dotted, "seq", 2, seq_size)
    along = dotted / feature_count / my_denominator
    return tuple(
        (value - my_inputs * along[i][:, None]) / my_radius[:, None]
        for i, value in enumerate(scaled)
    )


def solution(mesh):
    return jax.shard_map(
        body,
        mesh=mesh,
        in_specs=(P("seq", None), P(), P(), P(), P("seq", "vocab"), P("seq", "vocab")),
        out_specs=(P("vocab", "seq"), P("vocab", "seq")),
        check_vma=False,
    )
```

```python
import functools

import jax
import jax.numpy as jnp
from jax import lax
from jax.experimental import pallas as pl
from jax.experimental.pallas import tpu as pltpu
from jax.sharding import PartitionSpec as P

EPSILON = 1e-06
NT = (((1,), (1,)), ((), ()))
QUARTERS = 4
PAIR = 2
LIGHT = pl.CostEstimate(flops=0, bytes_accessed=0, transcendentals=0)
F32, BF16 = jnp.float32, jnp.bfloat16


def whole_spec():
    return pl.BlockSpec(memory_space=pltpu.VMEM)


def smem_spec():
    return pl.BlockSpec(memory_space=pltpu.SMEM)


def swap(value, axis, bit, size):
    return lax.ppermute(value, axis, [(i, i ^ bit) for i in range(size)])


def lanes(columns, rows):
    lane = lax.broadcasted_iota(jnp.int32, (rows, 128), 1)
    tile = jnp.zeros((rows, 128), F32)
    for index, column in enumerate(columns):
        tile = jnp.where(lane == index, column, tile)
    return tile


def turn(rows8):
    return jnp.concatenate([rows8, jnp.zeros((120, 128), F32)], axis=0).T


def cut_kernel(width, seq_size, at, hidden, vectors, *outs):
    own, mate, over_2, over_3, sums, parts, two = outs
    seq_index, group = at[0], at[1]
    rows = hidden.shape[0]
    size = rows // QUARTERS

    def quarter(place):
        return pl.ds(pl.multiple_of((place ^ group) * size, size), size)

    def features(bit):
        return pl.ds(pl.multiple_of((seq_index ^ bit) * width, width), width)

    for out, bit in ((over_2, 2), (over_3, 3)):
        out[0:size, :] = hidden[quarter(0), features(bit)]
        out[size:, :] = hidden[quarter(3), features(bit)]
    steer, tangent = vectors[0:1, :], vectors[1:2, :]
    columns = []
    for place in range(QUARTERS):
        spot = pl.ds(place * size, size)
        own[spot, :] = hidden[quarter(place), features(0)]
        mate[spot, :] = hidden[quarter(place), features(1)]
        inputs = hidden[quarter(place), :].astype(F32) + steer
        columns.append(
            lanes(
                [
                    jnp.sum(inputs * inputs, axis=1, keepdims=True),
                    jnp.sum(inputs * tangent, axis=1, keepdims=True),
                ],
                size,
            )
        )
    sums[...] = jnp.concatenate(columns, axis=0).T[:8]
    mine = vectors[:, features(0)]
    parts[...] = mine
    line = mine[1:2] * mine[2:3]
    high = line.astype(BF16).astype(F32)
    two[...] = jnp.concatenate(
        [high, line - high, jnp.zeros((14, width), F32)], axis=0
    ).astype(BF16)


def cut(at, hidden, vectors, width, seq_size):
    rows = hidden.shape[0]
    piece = jax.ShapeDtypeStruct((2 * (rows // QUARTERS), width), BF16)
    block = jax.ShapeDtypeStruct((rows, width), BF16)
    return pl.pallas_call(
        functools.partial(cut_kernel, width, seq_size),
        in_specs=[smem_spec(), whole_spec(), whole_spec()],
        out_specs=[whole_spec()] * 7,
        out_shape=[
            block,
            block,
            piece,
            piece,
            jax.ShapeDtypeStruct((8, rows), F32),
            jax.ShapeDtypeStruct((vectors.shape[0], width), F32),
            jax.ShapeDtypeStruct((16, width), BF16),
        ],
        cost_estimate=LIGHT,
    )(at, hidden, vectors)


def soften_kernel(feature_count, at, first, second, row, sums_a, sums_b, *outs):
    both_out, stats, tile = outs
    tokens = first.shape[0]
    count = at.shape[0]
    size = 2 * tokens // count
    line = row[0:1, :]
    for block, (source, sums) in enumerate(((first, sums_a), (second, sums_b))):
        turned = turn(sums[...])
        denominator = turned[:, 0:1] / feature_count + EPSILON
        inverse = 1.0 / jnp.sqrt(denominator)
        slope = turned[:, 1:2] / feature_count / denominator
        for piece in range(count // 2):
            begin = piece * size
            logits = source[begin : begin + size, :]
            spot = pl.ds(pl.multiple_of(at[block * (count // 2) + piece], size), size)
            peak = jnp.max(logits, axis=1, keepdims=True)
            exponent = jnp.exp(logits - peak)
            dlogits = line * inverse[begin : begin + size] - logits * slope[begin : begin + size]
            total = jnp.sum(exponent, axis=1, keepdims=True)
            mean = jnp.sum(exponent * dlogits, axis=1, keepdims=True) / total
            tilted = exponent * (dlogits - mean)
            both_out[0, spot, :] = exponent.astype(BF16)
            both_out[1, spot, :] = tilted.astype(BF16)
            tile[spot, :] = lanes([peak, total, mean], size)
    for begin in range(0, 2 * tokens, 128):
        stats[:, begin : begin + 128] = tile[begin : begin + 128, :].T[:8]


def soften(at, first, second, row, sums_a, sums_b, feature_count):
    tokens, width = first.shape
    rows = 2 * tokens
    return pl.pallas_call(
        functools.partial(soften_kernel, feature_count),
        in_specs=[smem_spec()] + [whole_spec()] * 5,
        out_specs=[whole_spec()] * 2,
        out_shape=[
            jax.ShapeDtypeStruct((2, rows, width), BF16),
            jax.ShapeDtypeStruct((8, rows), F32),
        ],
        scratch_shapes=[pltpu.VMEM((rows, 128), F32)],
        cost_estimate=LIGHT,
    )(at, first, second, row, sums_a, sums_b)


def order_kernel(at, *refs):
    blocks, totals, (ordered, columns) = refs[:4], refs[4:8], refs[8:]
    tokens = blocks[0].shape[0]
    count = at.shape[0]
    size = 4 * tokens // count
    half = 2 * tokens
    for block in range(4):
        inverse = 1.0 / turn(totals[block][...])
        for piece in range(count // 4):
            begin = piece * size
            place = at[block * (count // 4) + piece] + half * (block // 2)
            spot = pl.ds(pl.multiple_of(place, size), size)
            ordered[spot, :] = blocks[block][begin : begin + size, :]
            columns[spot, :] = inverse[begin : begin + size]


def order(at, blocks, totals):
    tokens, width = blocks[0].shape
    rows = 4 * tokens
    return pl.pallas_call(
        order_kernel,
        in_specs=[smem_spec()] + [whole_spec()] * 8,
        out_specs=[whole_spec()] * 2,
        out_shape=[
            jax.ShapeDtypeStruct((rows, width), BF16),
            jax.ShapeDtypeStruct((rows, 128), F32),
        ],
        cost_estimate=LIGHT,
    )(at, *blocks, *totals)


def back_kernel(deep, cotangent, head, out):
    width = head.shape[1]
    result = lax.dot_general(
        cotangent[:, :deep], head[:, :deep], NT, preferred_element_type=F32
    )
    if deep < width:
        result += lax.dot_general(
            cotangent[:, deep:], head[:, deep:], NT, preferred_element_type=F32
        )
    out[...] = result


def back(cotangent, head):
    rows, width = cotangent.shape
    features = head.shape[0]
    tile = 256 if features % 256 == 0 else features
    deep = width // 256 * 256 or width
    return pl.pallas_call(
        functools.partial(back_kernel, deep),
        grid=(features // tile,),
        in_specs=[
            pl.BlockSpec((rows, width), lambda i: (0, 0)),
            pl.BlockSpec((tile, width), lambda i: (i, 0)),
        ],
        out_specs=pl.BlockSpec((rows, tile), lambda i: (0, i)),
        out_shape=jax.ShapeDtypeStruct((rows, features), F32),
        cost_estimate=LIGHT,
    )(cotangent, head)


def merge(first, second):
    peak = jnp.maximum(first[0], second[0])
    one = jnp.exp(first[0] - peak) * first[1]
    two = jnp.exp(second[0] - peak) * second[1]
    total = one + two
    mean = (one * first[2] + two * second[2]) / total
    return jnp.stack([peak, total, mean] + [first[i] + second[i] for i in range(3, len(first))])


def exchange(value, size, beside):
    half = value.shape[1] // 2
    other, beside = lax.optimization_barrier((swap(value, "vocab", 1, size), beside))
    aligned = jnp.concatenate([other[:3, half:], other[:3, :half]], axis=1)
    value = merge(value, jnp.concatenate([aligned, other[3:]], axis=0))
    bit = PAIR
    while bit < size:
        value = merge(value, swap(value, "vocab", bit, size))
        bit *= 2
    return value, beside


def body(hidden, steer, tangent, gain, head, target):
    seq_size = lax.axis_size("seq")
    vocab_size = lax.axis_size("vocab")
    seq_index = lax.axis_index("seq")
    vocab_index = lax.axis_index("vocab")
    tokens, feature_count = hidden.shape
    width = head.shape[0]
    rows = seq_size * tokens
    share = rows // vocab_size
    quarter = tokens // QUARTERS
    size = min(share, quarter)
    y, z = vocab_index % PAIR, vocab_index // PAIR
    length = vocab_size // PAIR
    chip = seq_index // 2
    group = 2 * y + z % 2

    def destination(block, begin):
        row = (block % 2) * tokens + begin
        owner, inside = row // share, row % share
        return ((owner % PAIR) ^ y) * tokens + owner // PAIR * share + inside

    starts = jnp.arange(tokens // size) * size
    turned = ((starts // quarter) ^ group) * quarter + starts % quarter

    def places(bits, begins):
        return jnp.concatenate(
            [destination(seq_index ^ bit, begins) for bit in bits]
        ).astype(jnp.int32)

    own_places, other_places = places((0, 1), turned), places((2, 3), turned)
    target_places = places((0, 1, 2, 3), starts)

    at = jnp.stack([seq_index, group]).astype(jnp.int32)
    vectors = jnp.stack([steer, tangent, gain])
    own, mate, over_2, over_3, sums_0, parts, two = cut(
        at, hidden, vectors, width, seq_size
    )
    mate = swap(mate, "seq", 1, seq_size)
    sums_1 = swap(sums_0, "seq", 1, seq_size)
    over_2, over_3 = swap(over_2, "seq", 2, seq_size), swap(over_3, "seq", 3, seq_size)
    both = swap(jnp.stack([sums_0, sums_1]), "seq", 2, seq_size)
    steer_part, gain_part = parts[0], parts[2]

    def partial_logits(block, sums_of):
        radius = jnp.sqrt(sums_of[0] / feature_count + EPSILON)
        values = block.astype(F32) + steer_part
        normed = (gain_part * values / radius[:, None]).astype(BF16)
        return jnp.dot(normed, head, preferred_element_type=F32)

    given = partial_logits(mate, sums_1)
    two, given = lax.optimization_barrier((two, given))
    given = swap(given, "seq", 1, seq_size)
    row = jnp.sum(jnp.dot(two, head, preferred_element_type=F32), axis=0, keepdims=True)
    row = row + swap(row, "seq", 1, seq_size)
    tangent_row = row + swap(row, "seq", 2, seq_size)
    summed_0 = partial_logits(own, sums_0) + given
    send_0 = summed_0.astype(jnp.float16)
    over_2, over_3, both, send_0, tangent_row = lax.optimization_barrier(
        (over_2, over_3, both, send_0, tangent_row)
    )
    got_2 = swap(send_0, "seq", 2, seq_size)
    near = jnp.stack([over_2[:quarter], over_3[:quarter]])
    by_y = swap(near, "vocab", 2, vocab_size)
    by_z = swap(near, "vocab", 1, vocab_size)
    sums = [sums_0, sums_1, both[0], both[1]]
    denominators = [s[0] / feature_count + EPSILON for s in sums]

    blocks = [own, mate] + [
        jnp.concatenate([over[:quarter], by_y[i], by_z[i], over[quarter:]], axis=0)
        for i, over in enumerate((over_2, over_3))
    ]
    given = swap(partial_logits(blocks[3], sums[3]), "seq", 1, seq_size)
    summed_2 = partial_logits(blocks[2], sums[2]) + given
    send_2, got_2 = lax.optimization_barrier((summed_2.astype(jnp.float16), got_2))
    got_0 = swap(send_2, "seq", 2, seq_size)

    half = rows // 2

    def soften_of(base, summed, got, where):
        full = summed + got.astype(F32)
        mates = swap(full, "seq", 1, seq_size)
        both, stats = soften(
            where, full, mates, tangent_row, sums[base], sums[base + 1], feature_count
        )
        return both.reshape(2 * half, -1), stats[:3]

    def scaled_of(raw, stats, joint):
        scale = jnp.exp(stats[0] - joint[0]) / joint[1]
        lean = scale * (stats[2] - joint[2])
        plain = scale[:, None] * raw[:half]
        ggn = scale[:, None] * raw[half:] + lean[:, None] * raw[:half]
        return plain, ggn[half // 2 :].astype(BF16), ggn[: half // 2]

    both_other, stats_other = soften_of(2, summed_2, got_2, other_places)
    raw_other = back(both_other, head)
    got_0, target, raw_other, stats_other = lax.optimization_barrier(
        (got_0, target, raw_other, stats_other)
    )
    target_2 = swap(target, "seq", 2, seq_size)
    own_total = jnp.sum(target.astype(F32), axis=1)
    joint_other, raw_other = exchange(
        jnp.concatenate([stats_other, jnp.concatenate([own_total, own_total])[None]]),
        vocab_size,
        raw_other,
    )
    plain_other, theirs_other, kept_other = scaled_of(raw_other, stats_other, joint_other)
    got_other = swap(theirs_other, "vocab", 1, vocab_size)

    target_1 = swap(target, "seq", 1, seq_size)
    total_0 = jnp.broadcast_to(joint_other[3, :tokens], (8, tokens))
    total_1 = swap(total_0, "seq", 1, seq_size)
    both_totals = swap(jnp.stack([total_0, total_1]), "seq", 2, seq_size)

    both_own, stats_own = soften_of(0, summed_0, got_0, own_places)
    stats_own, theirs_other = lax.optimization_barrier((stats_own, theirs_other))
    joint, (raw_own, got_other, target_1, target_2, both_totals) = exchange(
        stats_own,
        vocab_size,
        (back(both_own, head), got_other, target_1, target_2, both_totals),
    )
    plain_own, theirs_own, kept_own = scaled_of(raw_own, stats_own, joint)
    got_own = swap(theirs_own, "vocab", 1, vocab_size)

    target_3 = swap(target_2, "seq", 1, seq_size)
    ordered, columns = order(
        target_places,
        [target, target_1, target_2, target_3],
        [total_0, total_1, both_totals[0], both_totals[1]],
    )
    ordered, _ = lax.optimization_barrier((ordered, theirs_own))
    weighed = back(ordered, head)
    inverse = columns[:, 0:1]
    gradients = [
        plain - inverse[begin : begin + half] * weighed[begin : begin + half]
        for plain, begin in ((plain_own, 0), (plain_other, half))
    ]

    def halve(joined, bit):
        if bit < length // 2:
            joined = joined.reshape(-1, 2, share, joined.shape[-1])
            place, axis = (z // bit) % 2, 1
        else:
            joined = joined.reshape(2, -1, share, joined.shape[-1])
            place, axis = (z // bit) ^ chip, 0
        sent = lax.dynamic_index_in_dim(joined, 1 - place, axis, False)
        kept = lax.dynamic_index_in_dim(joined, place, axis, False)
        return sent.astype(BF16), kept

    chunks = []
    for begin in (0, width // 2):
        part = [g[:, begin : begin + width // 2] for g in gradients]
        chunks.append(
            (
                jnp.concatenate([p[half // 2 :] for p in part]).astype(BF16),
                jnp.concatenate([p[: half // 2] for p in part]),
            )
        )
    got_own, got_other, *sends = lax.optimization_barrier(
        (got_own, got_other, chunks[0][0], chunks[1][0])
    )
    ggn = jnp.concatenate(
        [kept_own + got_own.astype(F32), kept_other + got_other.astype(F32)], axis=0
    )
    bits = [1]
    bit = 1
    while bit < length:
        bits.append(bit * PAIR)
        bit *= 2
    items = [[1, *halve(ggn, 1)]] + [[0, sent, chunk[1]] for sent, chunk in zip(sends, chunks)]
    tick = 0
    while any(item[0] < len(bits) for item in items):
        active = [
            i for i, item in enumerate(items) if item[0] < len(bits) and i <= tick + 1
        ]
        got = [swap(items[i][1], "vocab", bits[items[i][0]], vocab_size) for i in active]
        waiting = [i for i, item in enumerate(items) if i not in active and item[0] == 0]
        tied = lax.optimization_barrier((got, [items[i][1] for i in waiting]))
        for i, value in zip(waiting, tied[1]):
            items[i][1] = value
        for i, value in zip(active, tied[0]):
            step, _, kept = items[i]
            joined = kept + value.astype(F32)
            if step + 1 < len(bits):
                items[i] = [step + 1, *halve(joined, bits[step + 1] // PAIR)]
            else:
                items[i] = [step + 1, None, joined.reshape(share, -1)]
        tick += 1
    ggn_mine = items[0][2]
    grad_mine = jnp.concatenate([items[1][2], items[2][2]], axis=1)

    first_row = vocab_index * share
    owner = first_row // tokens
    block = owner ^ seq_index

    def choose(options):
        result = options[0]
        for index in range(1, len(options)):
            result = jnp.where(block == index, options[index], result)
        return result

    def gather_rows(options):
        pieces = []
        for begin in range(0, share, size):
            inside = first_row % tokens + begin
            place = ((inside // quarter) ^ group) * quarter + inside % quarter
            pieces.append(
                choose([lax.dynamic_slice_in_dim(o, place, size, 0) for o in options])
            )
        return jnp.concatenate(pieces, axis=0)

    my_inputs = gather_rows(blocks).astype(F32) + steer_part
    my_denominator = gather_rows(denominators)
    my_radius = jnp.sqrt(my_denominator)

    scaled = [gain_part * upstream for upstream in (grad_mine, ggn_mine)]
    dotted = jnp.stack([jnp.sum(my_inputs * value, axis=1) for value in scaled])
    dotted = dotted + swap(dotted, "seq", 1, seq_size)
    dotted = dotted + swap(dotted, "seq", 2, seq_size)
    along = dotted / feature_count / my_denominator
    return tuple(
        (value - my_inputs * along[i][:, None]) / my_radius[:, None]
        for i, value in enumerate(scaled)
    )


def solution(mesh):
    return jax.shard_map(
        body,
        mesh=mesh,
        in_specs=(P("seq", None), P(), P(), P(), P("seq", "vocab"), P("seq", "vocab")),
        out_specs=(P("vocab", "seq"), P("vocab", "seq")),
        check_vma=False,
    )
```

```python
import functools

import jax
import jax.numpy as jnp
from jax import lax
from jax.experimental import pallas as pl
from jax.experimental.pallas import tpu as pltpu
from jax.sharding import PartitionSpec as P

EPSILON = 1e-06
NT = (((1,), (1,)), ((), ()))
QUARTERS = 4
PAIR = 2
LIGHT = pl.CostEstimate(flops=0, bytes_accessed=0, transcendentals=0)
F32, BF16 = jnp.float32, jnp.bfloat16


def params(mebibytes):
    return pltpu.CompilerParams(vmem_limit_bytes=mebibytes * 1024 * 1024)


def whole_spec():
    return pl.BlockSpec(memory_space=pltpu.VMEM)


def smem_spec():
    return pl.BlockSpec(memory_space=pltpu.SMEM)


def swap(value, axis, bit, size):
    return lax.ppermute(value, axis, [(i, i ^ bit) for i in range(size)])


def lanes(columns, rows):
    lane = lax.broadcasted_iota(jnp.int32, (rows, 128), 1)
    tile = jnp.zeros((rows, 128), F32)
    for index, column in enumerate(columns):
        tile = jnp.where(lane == index, column, tile)
    return tile


def turn(rows8):
    return jnp.concatenate([rows8, jnp.zeros((120, 128), F32)], axis=0).T


def cut_kernel(width, at, hidden, vectors, *outs):
    blocks, (sums, parts, two) = outs[:4], outs[4:]
    seq_index = at[0]
    rows = hidden.shape[0]
    size = rows // QUARTERS

    def features(bit):
        return pl.ds(pl.multiple_of((seq_index ^ bit) * width, width), width)

    for bit, block in enumerate(blocks):
        block[...] = hidden[:, features(bit)]
    steer, tangent = vectors[0:1, :], vectors[1:2, :]
    columns = []
    for begin in range(0, rows, size):
        inputs = hidden[begin : begin + size, :].astype(F32) + steer
        columns.append(
            lanes(
                [
                    jnp.sum(inputs * inputs, axis=1, keepdims=True),
                    jnp.sum(inputs * tangent, axis=1, keepdims=True),
                ],
                size,
            )
        )
    sums[...] = jnp.concatenate(columns, axis=0).T[:8]
    mine = vectors[:, features(0)]
    parts[...] = mine
    line = mine[1:2] * mine[2:3]
    high = line.astype(BF16).astype(F32)
    two[...] = jnp.concatenate(
        [high, line - high, jnp.zeros((14, width), F32)], axis=0
    ).astype(BF16)


def cut(at, hidden, vectors, width):
    rows = hidden.shape[0]
    block = jax.ShapeDtypeStruct((rows, width), BF16)
    return pl.pallas_call(
        functools.partial(cut_kernel, width),
        in_specs=[smem_spec(), whole_spec(), whole_spec()],
        out_specs=[whole_spec()] * 7,
        out_shape=[
            block,
            block,
            block,
            block,
            jax.ShapeDtypeStruct((8, rows), F32),
            jax.ShapeDtypeStruct((vectors.shape[0], width), F32),
            jax.ShapeDtypeStruct((16, width), BF16),
        ],
        compiler_params=params(12),
        cost_estimate=LIGHT,
    )(at, hidden, vectors)


def soften_kernel(feature_count, at, first, second, row, sums_a, sums_b, *outs):
    both_out, stats, tile = outs
    tokens = first.shape[0]
    count = at.shape[0]
    size = 2 * tokens // count
    line = row[0:1, :]
    for block, (source, sums) in enumerate(((first, sums_a), (second, sums_b))):
        turned = turn(sums[...])
        denominator = turned[:, 0:1] / feature_count + EPSILON
        inverse = 1.0 / jnp.sqrt(denominator)
        slope = turned[:, 1:2] / feature_count / denominator
        for piece in range(count // 2):
            begin = piece * size
            logits = source[begin : begin + size, :]
            spot = pl.ds(pl.multiple_of(at[block * (count // 2) + piece], size), size)
            peak = jnp.max(logits, axis=1, keepdims=True)
            exponent = jnp.exp(logits - peak)
            dlogits = line * inverse[begin : begin + size] - logits * slope[begin : begin + size]
            total = jnp.sum(exponent, axis=1, keepdims=True)
            mean = jnp.sum(exponent * dlogits, axis=1, keepdims=True) / total
            tilted = exponent * (dlogits - mean)
            both_out[0, spot, :] = exponent.astype(BF16)
            both_out[1, spot, :] = tilted.astype(BF16)
            tile[spot, :] = lanes([peak, total, mean], size)
    for begin in range(0, 2 * tokens, 128):
        stats[:, begin : begin + 128] = tile[begin : begin + 128, :].T[:8]


def soften(at, first, second, row, sums_a, sums_b, feature_count):
    tokens, width = first.shape
    rows = 2 * tokens
    return pl.pallas_call(
        functools.partial(soften_kernel, feature_count),
        in_specs=[smem_spec()] + [whole_spec()] * 5,
        out_specs=[whole_spec()] * 2,
        out_shape=[
            jax.ShapeDtypeStruct((2, rows, width), BF16),
            jax.ShapeDtypeStruct((8, rows), F32),
        ],
        scratch_shapes=[pltpu.VMEM((rows, 128), F32)],
        compiler_params=params(16),
        cost_estimate=LIGHT,
    )(at, first, second, row, sums_a, sums_b)


def order_kernel(at, *refs):
    blocks, totals, (ordered, columns) = refs[:4], refs[4:8], refs[8:]
    tokens = blocks[0].shape[0]
    count = at.shape[0]
    size = 4 * tokens // count
    half = 2 * tokens
    for block in range(4):
        inverse = 1.0 / turn(totals[block][...])
        for piece in range(count // 4):
            begin = piece * size
            place = at[block * (count // 4) + piece] + half * (block // 2)
            spot = pl.ds(pl.multiple_of(place, size), size)
            ordered[spot, :] = blocks[block][begin : begin + size, :]
            columns[spot, :] = inverse[begin : begin + size]


def order(at, blocks, totals):
    tokens, width = blocks[0].shape
    rows = 4 * tokens
    return pl.pallas_call(
        order_kernel,
        in_specs=[smem_spec()] + [whole_spec()] * 8,
        out_specs=[whole_spec()] * 2,
        out_shape=[
            jax.ShapeDtypeStruct((rows, width), BF16),
            jax.ShapeDtypeStruct((rows, 128), F32),
        ],
        compiler_params=params(12),
        cost_estimate=LIGHT,
    )(at, *blocks, *totals)


def back_kernel(deep, cotangent, head, out):
    width = head.shape[1]
    result = lax.dot_general(
        cotangent[:, :deep], head[:, :deep], NT, preferred_element_type=F32
    )
    if deep < width:
        result += lax.dot_general(
            cotangent[:, deep:], head[:, deep:], NT, preferred_element_type=F32
        )
    out[...] = result


def back(cotangent, head):
    rows, width = cotangent.shape
    features = head.shape[0]
    tile = 256 if features % 256 == 0 else features
    deep = width // 256 * 256 or width
    return pl.pallas_call(
        functools.partial(back_kernel, deep),
        grid=(features // tile,),
        in_specs=[
            pl.BlockSpec((rows, width), lambda i: (0, 0)),
            pl.BlockSpec((tile, width), lambda i: (i, 0)),
        ],
        out_specs=pl.BlockSpec((rows, tile), lambda i: (0, i)),
        out_shape=jax.ShapeDtypeStruct((rows, features), F32),
        compiler_params=params(20),
        cost_estimate=LIGHT,
    )(cotangent, head)


def merge(first, second):
    peak = jnp.maximum(first[0], second[0])
    one = jnp.exp(first[0] - peak) * first[1]
    two = jnp.exp(second[0] - peak) * second[1]
    total = one + two
    mean = (one * first[2] + two * second[2]) / total
    return jnp.stack([peak, total, mean] + [first[i] + second[i] for i in range(3, len(first))])


def exchange(value, size, beside):
    other, beside = lax.optimization_barrier((swap(value, "vocab", 1, size), beside))
    part = value.shape[1] // 4
    aligned = jnp.concatenate(
        [other[:3, i * part : (i + 1) * part] for i in (1, 0, 3, 2)], axis=1
    )
    value = merge(value, jnp.concatenate([aligned, other[3:]], axis=0))
    bit = PAIR
    while bit < size:
        value = merge(value, swap(value, "vocab", bit, size))
        bit *= 2
    return value, beside


def body(hidden, steer, tangent, gain, head, target):
    seq_size = lax.axis_size("seq")
    vocab_size = lax.axis_size("vocab")
    seq_index = lax.axis_index("seq")
    vocab_index = lax.axis_index("vocab")
    tokens, feature_count = hidden.shape
    width = head.shape[0]
    rows = seq_size * tokens
    share = rows // vocab_size
    quarter = tokens // QUARTERS
    size = min(share, quarter)
    y, z = vocab_index % PAIR, vocab_index // PAIR
    length = vocab_size // PAIR
    chip = seq_index // 2

    def destination(block, begin):
        row = (block % 2) * tokens + begin
        owner, inside = row // share, row % share
        return ((owner % PAIR) ^ y) * tokens + owner // PAIR * share + inside

    starts = jnp.arange(tokens // size) * size

    def places(bits, begins):
        return jnp.concatenate(
            [destination(seq_index ^ bit, begins) for bit in bits]
        ).astype(jnp.int32)

    own_places, other_places = places((0, 1), starts), places((2, 3), starts)
    target_places = places((0, 1, 2, 3), starts)

    at = seq_index.astype(jnp.int32)[None]
    vectors = jnp.stack([steer, tangent, gain])
    own, mate, over_2, over_3, sums_0, parts, two = cut(
        at, hidden, vectors, width
    )
    mate = swap(mate, "seq", 1, seq_size)
    sums_1 = swap(sums_0, "seq", 1, seq_size)
    over_2, over_3 = swap(over_2, "seq", 2, seq_size), swap(over_3, "seq", 3, seq_size)
    both = swap(jnp.stack([sums_0, sums_1]), "seq", 2, seq_size)
    steer_part, gain_part = parts[0], parts[2]

    def partial_logits(block, sums_of):
        radius = jnp.sqrt(sums_of[0] / feature_count + EPSILON)
        values = block.astype(F32) + steer_part
        normed = (gain_part * values / radius[:, None]).astype(BF16)
        return jnp.dot(normed, head, preferred_element_type=F32)

    given = partial_logits(mate, sums_1)
    two, given = lax.optimization_barrier((two, given))
    given = swap(given, "seq", 1, seq_size)
    row = jnp.sum(jnp.dot(two, head, preferred_element_type=F32), axis=0, keepdims=True)
    row = row + swap(row, "seq", 1, seq_size)
    tangent_row = row + swap(row, "seq", 2, seq_size)
    summed_0 = partial_logits(own, sums_0) + given
    send_0 = summed_0.astype(jnp.float16)
    both, send_0, tangent_row = lax.optimization_barrier((both, send_0, tangent_row))
    got_2 = swap(send_0, "seq", 2, seq_size)
    sums = [sums_0, sums_1, both[0], both[1]]
    denominators = [s[0] / feature_count + EPSILON for s in sums]

    blocks = [own, mate, over_2, over_3]
    given = swap(partial_logits(blocks[3], sums[3]), "seq", 1, seq_size)
    summed_2 = partial_logits(blocks[2], sums[2]) + given
    send_2, got_2 = lax.optimization_barrier((summed_2.astype(jnp.float16), got_2))
    got_0 = swap(send_2, "seq", 2, seq_size)

    half = rows // 2

    def soften_of(base, summed, got, where):
        full = summed + got.astype(F32)
        mates = swap(full, "seq", 1, seq_size)
        both, stats = soften(
            where, full, mates, tangent_row, sums[base], sums[base + 1], feature_count
        )
        return both.reshape(2 * half, -1), stats[:3]

    def scaled_of(raw, stats, joint):
        scale = jnp.exp(stats[0] - joint[0]) / joint[1]
        lean = scale * (stats[2] - joint[2])
        plain = scale[:, None] * raw[:half]
        ggn = scale[:, None] * raw[half:] + lean[:, None] * raw[:half]
        return plain, ggn[half // 2 :].astype(BF16), ggn[: half // 2]

    both_other, stats_other = soften_of(2, summed_2, got_2, other_places)
    raw_other = back(both_other, head)
    got_0, target, raw_other, stats_other = lax.optimization_barrier(
        (got_0, target, raw_other, stats_other)
    )
    target_2 = swap(target, "seq", 2, seq_size)
    target_1 = swap(target, "seq", 1, seq_size)
    both_own, stats_own = soften_of(0, summed_0, got_0, own_places)
    own_total = jnp.sum(target.astype(F32), axis=1)
    stats = jnp.concatenate([stats_own, stats_other], axis=1)
    joint, (raw_own, target_1, target_2) = exchange(
        jnp.concatenate([stats, jnp.concatenate([own_total] * seq_size)[None]]),
        vocab_size,
        (back(both_own, head), target_1, target_2),
    )
    plain_own, theirs_own, kept_own = scaled_of(raw_own, stats_own, joint[:, :half])
    plain_other, theirs_other, kept_other = scaled_of(raw_other, stats_other, joint[:, half:])
    got_own = swap(theirs_own, "vocab", 1, vocab_size)
    got_other = swap(theirs_other, "vocab", 1, vocab_size)
    total_0 = jnp.broadcast_to(joint[3, :tokens], (8, tokens))
    total_1 = swap(total_0, "seq", 1, seq_size)
    both_totals = swap(jnp.stack([total_0, total_1]), "seq", 2, seq_size)

    target_3 = swap(target_2, "seq", 1, seq_size)
    ordered, columns = order(
        target_places,
        [target, target_1, target_2, target_3],
        [total_0, total_1, both_totals[0], both_totals[1]],
    )
    ordered, _, _ = lax.optimization_barrier((ordered, theirs_own, theirs_other))
    weighed = back(ordered, head)
    inverse = columns[:, 0:1]
    gradients = [
        plain - inverse[begin : begin + half] * weighed[begin : begin + half]
        for plain, begin in ((plain_own, 0), (plain_other, half))
    ]

    def halve(joined, bit):
        if bit < length // 2:
            joined = joined.reshape(-1, 2, share, joined.shape[-1])
            place, axis = (z // bit) % 2, 1
        else:
            joined = joined.reshape(2, -1, share, joined.shape[-1])
            place, axis = (z // bit) ^ chip, 0
        sent = lax.dynamic_index_in_dim(joined, 1 - place, axis, False)
        kept = lax.dynamic_index_in_dim(joined, place, axis, False)
        return sent.astype(BF16), kept

    chunks = []
    for begin in (0, width // 2):
        part = [g[:, begin : begin + width // 2] for g in gradients]
        chunks.append(
            (
                jnp.concatenate([p[half // 2 :] for p in part]).astype(BF16),
                jnp.concatenate([p[: half // 2] for p in part]),
            )
        )
    got_own, got_other, *sends = lax.optimization_barrier(
        (got_own, got_other, chunks[0][0], chunks[1][0])
    )
    ggn = jnp.concatenate(
        [kept_own + got_own.astype(F32), kept_other + got_other.astype(F32)], axis=0
    )
    bits = [1]
    bit = 1
    while bit < length:
        bits.append(bit * PAIR)
        bit *= 2
    items = [[1, *halve(ggn, 1)]] + [[0, sent, chunk[1]] for sent, chunk in zip(sends, chunks)]
    tick = 0
    while any(item[0] < len(bits) for item in items):
        active = [
            i for i, item in enumerate(items) if item[0] < len(bits) and i <= tick + 1
        ]
        got = [swap(items[i][1], "vocab", bits[items[i][0]], vocab_size) for i in active]
        waiting = [i for i, item in enumerate(items) if i not in active and item[0] == 0]
        tied = lax.optimization_barrier((got, [items[i][1] for i in waiting]))
        for i, value in zip(waiting, tied[1]):
            items[i][1] = value
        for i, value in zip(active, tied[0]):
            step, _, kept = items[i]
            joined = kept + value.astype(F32)
            if step + 1 < len(bits):
                items[i] = [step + 1, *halve(joined, bits[step + 1] // PAIR)]
            else:
                items[i] = [step + 1, None, joined.reshape(share, -1)]
        tick += 1
    ggn_mine = items[0][2]
    grad_mine = jnp.concatenate([items[1][2], items[2][2]], axis=1)

    first_row = vocab_index * share
    owner = first_row // tokens
    block = owner ^ seq_index

    def choose(options):
        result = options[0]
        for index in range(1, len(options)):
            result = jnp.where(block == index, options[index], result)
        return result

    def gather_rows(options):
        pieces = []
        for begin in range(0, share, size):
            inside = first_row % tokens + begin
            pieces.append(
                choose([lax.dynamic_slice_in_dim(o, inside, size, 0) for o in options])
            )
        return jnp.concatenate(pieces, axis=0)

    my_inputs = gather_rows(blocks).astype(F32) + steer_part
    my_denominator = gather_rows(denominators)
    my_radius = jnp.sqrt(my_denominator)

    scaled = [gain_part * upstream for upstream in (grad_mine, ggn_mine)]
    dotted = jnp.stack([jnp.sum(my_inputs * value, axis=1) for value in scaled])
    dotted = dotted + swap(dotted, "seq", 1, seq_size)
    dotted = dotted + swap(dotted, "seq", 2, seq_size)
    along = dotted / feature_count / my_denominator
    return tuple(
        (value - my_inputs * along[i][:, None]) / my_radius[:, None]
        for i, value in enumerate(scaled)
    )


def solution(mesh):
    return jax.shard_map(
        body,
        mesh=mesh,
        in_specs=(P("seq", None), P(), P(), P(), P("seq", "vocab"), P("seq", "vocab")),
        out_specs=(P("vocab", "seq"), P("vocab", "seq")),
        check_vma=False,
    )
```

```python
import functools

import jax
import jax.numpy as jnp
from jax import lax
from jax.experimental import pallas as pl
from jax.experimental.pallas import tpu as pltpu
from jax.sharding import PartitionSpec as P

EPSILON = 1e-06
NT = (((1,), (1,)), ((), ()))
QUARTERS = 4
PAIR = 2
LIGHT = pl.CostEstimate(flops=0, bytes_accessed=0, transcendentals=0)
F32, BF16 = jnp.float32, jnp.bfloat16


def params(mebibytes):
    return pltpu.CompilerParams(vmem_limit_bytes=mebibytes * 1024 * 1024)


def whole_spec():
    return pl.BlockSpec(memory_space=pltpu.VMEM)


def smem_spec():
    return pl.BlockSpec(memory_space=pltpu.SMEM)


def swap(value, axis, bit, size):
    return lax.ppermute(value, axis, [(i, i ^ bit) for i in range(size)])


def lanes(columns, rows):
    lane = lax.broadcasted_iota(jnp.int32, (rows, 128), 1)
    tile = jnp.zeros((rows, 128), F32)
    for index, column in enumerate(columns):
        tile = jnp.where(lane == index, column, tile)
    return tile


def turn(rows8):
    return jnp.concatenate([rows8, jnp.zeros((120, 128), F32)], axis=0).T


def cut_kernel(width, at, hidden, vectors, *outs):
    own, mate, over, sums, parts, two = outs
    seq_index = at[0]
    rows = hidden.shape[0]
    size = rows // QUARTERS

    def features(bit):
        return pl.ds(pl.multiple_of((seq_index ^ bit) * width, width), width)

    own[...] = hidden[:, features(0)]
    mate[...] = hidden[:, features(1)]
    over[0] = hidden[:, features(2)]
    over[1] = hidden[:, features(3)]
    steer, tangent = vectors[0:1, :], vectors[1:2, :]
    columns = []
    for begin in range(0, rows, size):
        inputs = hidden[begin : begin + size, :].astype(F32) + steer
        columns.append(
            lanes(
                [
                    jnp.sum(inputs * inputs, axis=1, keepdims=True),
                    jnp.sum(inputs * tangent, axis=1, keepdims=True),
                ],
                size,
            )
        )
    sums[...] = jnp.concatenate(columns, axis=0).T[:8]
    mine = vectors[:, features(0)]
    parts[...] = mine
    line = mine[1:2] * mine[2:3]
    high = line.astype(BF16).astype(F32)
    two[...] = jnp.concatenate(
        [high, line - high, jnp.zeros((14, width), F32)], axis=0
    ).astype(BF16)


def cut(at, hidden, vectors, width):
    rows = hidden.shape[0]
    block = jax.ShapeDtypeStruct((rows, width), BF16)
    return pl.pallas_call(
        functools.partial(cut_kernel, width),
        in_specs=[smem_spec(), whole_spec(), whole_spec()],
        out_specs=[whole_spec()] * 6,
        out_shape=[
            block,
            block,
            jax.ShapeDtypeStruct((2, rows, width), BF16),
            jax.ShapeDtypeStruct((8, rows), F32),
            jax.ShapeDtypeStruct((vectors.shape[0], width), F32),
            jax.ShapeDtypeStruct((16, width), BF16),
        ],
        compiler_params=params(12),
        cost_estimate=LIGHT,
    )(at, hidden, vectors)


def soften_kernel(feature_count, at, first, second, row, sums_a, sums_b, *outs):
    both_out, stats, tile = outs
    tokens = first.shape[0]
    count = at.shape[0]
    size = 2 * tokens // count
    line = row[0:1, :]
    for block, (source, sums) in enumerate(((first, sums_a), (second, sums_b))):
        turned = turn(sums[...])
        denominator = turned[:, 0:1] / feature_count + EPSILON
        inverse = 1.0 / jnp.sqrt(denominator)
        slope = turned[:, 1:2] / feature_count / denominator
        for piece in range(count // 2):
            begin = piece * size
            logits = source[begin : begin + size, :]
            spot = pl.ds(pl.multiple_of(at[block * (count // 2) + piece], size), size)
            peak = jnp.max(logits, axis=1, keepdims=True)
            exponent = jnp.exp(logits - peak)
            dlogits = line * inverse[begin : begin + size] - logits * slope[begin : begin + size]
            total = jnp.sum(exponent, axis=1, keepdims=True)
            mean = jnp.sum(exponent * dlogits, axis=1, keepdims=True) / total
            tilted = exponent * (dlogits - mean)
            both_out[0, spot, :] = exponent.astype(BF16)
            both_out[1, spot, :] = tilted.astype(BF16)
            tile[spot, :] = lanes([peak, total, mean], size)
    for begin in range(0, 2 * tokens, 128):
        stats[:, begin : begin + 128] = tile[begin : begin + 128, :].T[:8]


def soften(at, first, second, row, sums_a, sums_b, feature_count):
    tokens, width = first.shape
    rows = 2 * tokens
    return pl.pallas_call(
        functools.partial(soften_kernel, feature_count),
        in_specs=[smem_spec()] + [whole_spec()] * 5,
        out_specs=[whole_spec()] * 2,
        out_shape=[
            jax.ShapeDtypeStruct((2, rows, width), BF16),
            jax.ShapeDtypeStruct((8, rows), F32),
        ],
        scratch_shapes=[pltpu.VMEM((rows, 128), F32)],
        compiler_params=params(16),
        cost_estimate=LIGHT,
    )(at, first, second, row, sums_a, sums_b)


def order_kernel(at, *refs):
    blocks, totals, (ordered, columns) = refs[:4], refs[4:8], refs[8:]
    tokens = blocks[0].shape[0]
    count = at.shape[0]
    size = 4 * tokens // count
    half = 2 * tokens
    for block in range(4):
        inverse = 1.0 / turn(totals[block][...])
        for piece in range(count // 4):
            begin = piece * size
            place = at[block * (count // 4) + piece] + half * (block // 2)
            spot = pl.ds(pl.multiple_of(place, size), size)
            ordered[spot, :] = blocks[block][begin : begin + size, :]
            columns[spot, :] = inverse[begin : begin + size]


def order(at, blocks, totals):
    tokens, width = blocks[0].shape
    rows = 4 * tokens
    return pl.pallas_call(
        order_kernel,
        in_specs=[smem_spec()] + [whole_spec()] * 8,
        out_specs=[whole_spec()] * 2,
        out_shape=[
            jax.ShapeDtypeStruct((rows, width), BF16),
            jax.ShapeDtypeStruct((rows, 128), F32),
        ],
        compiler_params=params(12),
        cost_estimate=LIGHT,
    )(at, *blocks, *totals)


def back_kernel(deep, cotangent, head, out):
    width = head.shape[1]
    result = lax.dot_general(
        cotangent[:, :deep], head[:, :deep], NT, preferred_element_type=F32
    )
    if deep < width:
        result += lax.dot_general(
            cotangent[:, deep:], head[:, deep:], NT, preferred_element_type=F32
        )
    out[...] = result


def back(cotangent, head):
    rows, width = cotangent.shape
    features = head.shape[0]
    tile = 256 if features % 256 == 0 else features
    deep = width // 256 * 256 or width
    return pl.pallas_call(
        functools.partial(back_kernel, deep),
        grid=(features // tile,),
        in_specs=[
            pl.BlockSpec((rows, width), lambda i: (0, 0)),
            pl.BlockSpec((tile, width), lambda i: (i, 0)),
        ],
        out_specs=pl.BlockSpec((rows, tile), lambda i: (0, i)),
        out_shape=jax.ShapeDtypeStruct((rows, features), F32),
        compiler_params=params(20),
        cost_estimate=LIGHT,
    )(cotangent, head)


def merge(first, second):
    peak = jnp.maximum(first[0], second[0])
    one = jnp.exp(first[0] - peak) * first[1]
    two = jnp.exp(second[0] - peak) * second[1]
    total = one + two
    mean = (one * first[2] + two * second[2]) / total
    return jnp.stack([peak, total, mean] + [first[i] + second[i] for i in range(3, len(first))])


def exchange(value, size, beside):
    other, beside = lax.optimization_barrier((swap(value, "vocab", 1, size), beside))
    part = value.shape[1] // 4
    aligned = jnp.concatenate(
        [other[:3, i * part : (i + 1) * part] for i in (1, 0, 3, 2)], axis=1
    )
    value = merge(value, jnp.concatenate([aligned, other[3:]], axis=0))
    bit = PAIR
    while bit < size:
        value = merge(value, swap(value, "vocab", bit, size))
        bit *= 2
    return value, beside


def body(hidden, steer, tangent, gain, head, target):
    seq_size = lax.axis_size("seq")
    vocab_size = lax.axis_size("vocab")
    seq_index = lax.axis_index("seq")
    vocab_index = lax.axis_index("vocab")
    tokens, feature_count = hidden.shape
    width = head.shape[0]
    rows = seq_size * tokens
    share = rows // vocab_size
    quarter = tokens // QUARTERS
    size = min(share, quarter)
    y, z = vocab_index % PAIR, vocab_index // PAIR
    length = vocab_size // PAIR
    chip = seq_index // 2

    def destination(block, begin):
        row = (block % 2) * tokens + begin
        owner, inside = row // share, row % share
        return ((owner % PAIR) ^ y) * tokens + owner // PAIR * share + inside

    starts = jnp.arange(tokens // size) * size

    def places(bits, begins):
        return jnp.concatenate(
            [destination(seq_index ^ bit, begins) for bit in bits]
        ).astype(jnp.int32)

    own_places, other_places = places((0, 1), starts), places((2, 3), starts)
    target_places = places((0, 1, 2, 3), starts)

    at = seq_index.astype(jnp.int32)[None]
    vectors = jnp.stack([steer, tangent, gain])
    own, mate, over, sums_0, parts, two = cut(
        at, hidden, vectors, width
    )
    mate = swap(mate, "seq", 1, seq_size)
    sums_1 = swap(sums_0, "seq", 1, seq_size)
    over = swap(over, "seq", 2, seq_size)
    over_2, over_3 = over[0], swap(over[1], "seq", 1, seq_size)
    both = swap(jnp.stack([sums_0, sums_1]), "seq", 2, seq_size)
    steer_part, gain_part = parts[0], parts[2]

    def partial_logits(block, sums_of):
        radius = jnp.sqrt(sums_of[0] / feature_count + EPSILON)
        values = block.astype(F32) + steer_part
        normed = (gain_part * values / radius[:, None]).astype(BF16)
        return jnp.dot(normed, head, preferred_element_type=F32)

    given = partial_logits(mate, sums_1)
    two, given = lax.optimization_barrier((two, given))
    given = swap(given, "seq", 1, seq_size)
    row = jnp.sum(jnp.dot(two, head, preferred_element_type=F32), axis=0, keepdims=True)
    row = row + swap(row, "seq", 1, seq_size)
    tangent_row = row + swap(row, "seq", 2, seq_size)
    summed_0 = partial_logits(own, sums_0) + given
    send_0 = summed_0.astype(jnp.float16)
    both, send_0, tangent_row = lax.optimization_barrier((both, send_0, tangent_row))
    got_2 = swap(send_0, "seq", 2, seq_size)
    sums = [sums_0, sums_1, both[0], both[1]]
    denominators = [s[0] / feature_count + EPSILON for s in sums]

    blocks = [own, mate, over_2, over_3]
    given = swap(partial_logits(blocks[3], sums[3]), "seq", 1, seq_size)
    summed_2 = partial_logits(blocks[2], sums[2]) + given
    send_2, got_2 = lax.optimization_barrier((summed_2.astype(jnp.float16), got_2))
    got_0 = swap(send_2, "seq", 2, seq_size)

    half = rows // 2

    def soften_of(base, summed, got, where):
        full = summed + got.astype(F32)
        mates = swap(full, "seq", 1, seq_size)
        both, stats = soften(
            where, full, mates, tangent_row, sums[base], sums[base + 1], feature_count
        )
        return both.reshape(2 * half, -1), stats[:3]

    def scaled_of(raw, stats, joint):
        scale = jnp.exp(stats[0] - joint[0]) / joint[1]
        lean = scale * (stats[2] - joint[2])
        plain = scale[:, None] * raw[:half]
        ggn = scale[:, None] * raw[half:] + lean[:, None] * raw[:half]
        return plain, ggn[half // 2 :].astype(BF16), ggn[: half // 2]

    both_other, stats_other = soften_of(2, summed_2, got_2, other_places)
    raw_other = back(both_other, head)
    got_0, target, raw_other, stats_other = lax.optimization_barrier(
        (got_0, target, raw_other, stats_other)
    )
    target_2 = swap(target, "seq", 2, seq_size)
    target_1 = swap(target, "seq", 1, seq_size)
    both_own, stats_own = soften_of(0, summed_0, got_0, own_places)
    own_total = jnp.sum(target.astype(F32), axis=1)
    stats = jnp.concatenate([stats_own, stats_other], axis=1)
    joint, (raw_own, target_1, target_2) = exchange(
        jnp.concatenate([stats, jnp.concatenate([own_total] * seq_size)[None]]),
        vocab_size,
        (back(both_own, head), target_1, target_2),
    )
    plain_own, theirs_own, kept_own = scaled_of(raw_own, stats_own, joint[:, :half])
    plain_other, theirs_other, kept_other = scaled_of(raw_other, stats_other, joint[:, half:])
    got_own = swap(theirs_own, "vocab", 1, vocab_size)
    got_other = swap(theirs_other, "vocab", 1, vocab_size)
    total_0 = jnp.broadcast_to(joint[3, :tokens], (8, tokens))
    total_1 = swap(total_0, "seq", 1, seq_size)
    both_totals = swap(jnp.stack([total_0, total_1]), "seq", 2, seq_size)

    target_3 = swap(target_2, "seq", 1, seq_size)
    ordered, columns = order(
        target_places,
        [target, target_1, target_2, target_3],
        [total_0, total_1, both_totals[0], both_totals[1]],
    )
    ordered, _, _ = lax.optimization_barrier((ordered, theirs_own, theirs_other))
    weighed = back(ordered, head)
    inverse = columns[:, 0:1]
    gradients = [
        plain - inverse[begin : begin + half] * weighed[begin : begin + half]
        for plain, begin in ((plain_own, 0), (plain_other, half))
    ]

    def halve(joined, bit):
        if bit < length // 2:
            joined = joined.reshape(-1, 2, share, joined.shape[-1])
            place, axis = (z // bit) % 2, 1
        else:
            joined = joined.reshape(2, -1, share, joined.shape[-1])
            place, axis = (z // bit) ^ chip, 0
        sent = lax.dynamic_index_in_dim(joined, 1 - place, axis, False)
        kept = lax.dynamic_index_in_dim(joined, place, axis, False)
        return sent.astype(BF16), kept

    chunks = []
    for begin in (0, width // 2):
        part = [g[:, begin : begin + width // 2] for g in gradients]
        chunks.append(
            (
                jnp.concatenate([p[half // 2 :] for p in part]).astype(BF16),
                jnp.concatenate([p[: half // 2] for p in part]),
            )
        )
    got_own, got_other, *sends = lax.optimization_barrier(
        (got_own, got_other, chunks[0][0], chunks[1][0])
    )
    ggn = jnp.concatenate(
        [kept_own + got_own.astype(F32), kept_other + got_other.astype(F32)], axis=0
    )
    bits = [1]
    bit = 1
    while bit < length:
        bits.append(bit * PAIR)
        bit *= 2
    items = [[1, *halve(ggn, 1)]] + [[0, sent, chunk[1]] for sent, chunk in zip(sends, chunks)]
    tick = 0
    while any(item[0] < len(bits) for item in items):
        active = [
            i for i, item in enumerate(items) if item[0] < len(bits) and i <= tick + 1
        ]
        got = [swap(items[i][1], "vocab", bits[items[i][0]], vocab_size) for i in active]
        waiting = [i for i, item in enumerate(items) if i not in active and item[0] == 0]
        tied = lax.optimization_barrier((got, [items[i][1] for i in waiting]))
        for i, value in zip(waiting, tied[1]):
            items[i][1] = value
        for i, value in zip(active, tied[0]):
            step, _, kept = items[i]
            joined = kept + value.astype(F32)
            if step + 1 < len(bits):
                items[i] = [step + 1, *halve(joined, bits[step + 1] // PAIR)]
            else:
                items[i] = [step + 1, None, joined.reshape(share, -1)]
        tick += 1
    ggn_mine = items[0][2]
    grad_mine = jnp.concatenate([items[1][2], items[2][2]], axis=1)

    first_row = vocab_index * share
    owner = first_row // tokens
    block = owner ^ seq_index

    def choose(options):
        result = options[0]
        for index in range(1, len(options)):
            result = jnp.where(block == index, options[index], result)
        return result

    def gather_rows(options):
        pieces = []
        for begin in range(0, share, size):
            inside = first_row % tokens + begin
            pieces.append(
                choose([lax.dynamic_slice_in_dim(o, inside, size, 0) for o in options])
            )
        return jnp.concatenate(pieces, axis=0)

    my_inputs = gather_rows(blocks).astype(F32) + steer_part
    my_denominator = gather_rows(denominators)
    my_radius = jnp.sqrt(my_denominator)

    scaled = [gain_part * upstream for upstream in (grad_mine, ggn_mine)]
    dotted = jnp.stack([jnp.sum(my_inputs * value, axis=1) for value in scaled])
    dotted = dotted + swap(dotted, "seq", 1, seq_size)
    dotted = dotted + swap(dotted, "seq", 2, seq_size)
    along = dotted / feature_count / my_denominator
    return tuple(
        (value - my_inputs * along[i][:, None]) / my_radius[:, None]
        for i, value in enumerate(scaled)
    )


def solution(mesh):
    return jax.shard_map(
        body,
        mesh=mesh,
        in_specs=(P("seq", None), P(), P(), P(), P("seq", "vocab"), P("seq", "vocab")),
        out_specs=(P("vocab", "seq"), P("vocab", "seq")),
        check_vma=False,
    )
```

```python
import functools

import jax
import jax.numpy as jnp
from jax import lax
from jax.experimental import pallas as pl
from jax.experimental.pallas import tpu as pltpu
from jax.sharding import PartitionSpec as P

EPSILON = 1e-06
NT = (((1,), (1,)), ((), ()))
QUARTERS = 4
PAIR = 2
LIGHT = pl.CostEstimate(flops=0, bytes_accessed=0, transcendentals=0)
F32, BF16 = jnp.float32, jnp.bfloat16


def params(mebibytes):
    return pltpu.CompilerParams(vmem_limit_bytes=mebibytes * 1024 * 1024)


def whole_spec():
    return pl.BlockSpec(memory_space=pltpu.VMEM)


def smem_spec():
    return pl.BlockSpec(memory_space=pltpu.SMEM)


def swap(value, axis, bit, size):
    return lax.ppermute(value, axis, [(i, i ^ bit) for i in range(size)])


def lanes(columns, rows):
    lane = lax.broadcasted_iota(jnp.int32, (rows, 128), 1)
    tile = jnp.zeros((rows, 128), F32)
    for index, column in enumerate(columns):
        tile = jnp.where(lane == index, column, tile)
    return tile


def turn(rows8):
    return jnp.concatenate([rows8, jnp.zeros((120, 128), F32)], axis=0).T


def cut_kernel(width, at, hidden, vectors, *outs):
    own, mate, over, sums, parts, two = outs
    seq_index = at[0]
    rows = hidden.shape[0]
    size = rows // QUARTERS

    def features(bit):
        return pl.ds(pl.multiple_of((seq_index ^ bit) * width, width), width)

    own[...] = hidden[:, features(0)]
    mate[...] = hidden[:, features(1)]
    over[0] = hidden[:, features(2)]
    over[1] = hidden[:, features(3)]
    steer, tangent = vectors[0:1, :], vectors[1:2, :]
    columns = []
    for begin in range(0, rows, size):
        inputs = hidden[begin : begin + size, :].astype(F32) + steer
        columns.append(
            lanes(
                [
                    jnp.sum(inputs * inputs, axis=1, keepdims=True),
                    jnp.sum(inputs * tangent, axis=1, keepdims=True),
                ],
                size,
            )
        )
    sums[...] = jnp.concatenate(columns, axis=0).T[:8]
    mine = vectors[:, features(0)]
    parts[...] = mine
    line = mine[1:2] * mine[2:3]
    high = line.astype(BF16).astype(F32)
    two[...] = jnp.concatenate(
        [high, line - high, jnp.zeros((14, width), F32)], axis=0
    ).astype(BF16)


def cut(at, hidden, vectors, width):
    rows = hidden.shape[0]
    block = jax.ShapeDtypeStruct((rows, width), BF16)
    return pl.pallas_call(
        functools.partial(cut_kernel, width),
        in_specs=[smem_spec(), whole_spec(), whole_spec()],
        out_specs=[whole_spec()] * 6,
        out_shape=[
            block,
            block,
            jax.ShapeDtypeStruct((2, rows, width), BF16),
            jax.ShapeDtypeStruct((8, rows), F32),
            jax.ShapeDtypeStruct((vectors.shape[0], width), F32),
            jax.ShapeDtypeStruct((16, width), BF16),
        ],
        compiler_params=params(12),
        cost_estimate=LIGHT,
    )(at, hidden, vectors)


def soften_kernel(feature_count, at, first, second, row, sums_a, sums_b, *outs):
    both_out, stats, tile = outs
    tokens = first.shape[0]
    count = at.shape[0]
    size = 2 * tokens // count
    line = row[0:1, :]
    for block, (source, sums) in enumerate(((first, sums_a), (second, sums_b))):
        turned = turn(sums[...])
        denominator = turned[:, 0:1] / feature_count + EPSILON
        inverse = 1.0 / jnp.sqrt(denominator)
        slope = turned[:, 1:2] / feature_count / denominator
        for piece in range(count // 2):
            begin = piece * size
            logits = source[begin : begin + size, :]
            spot = pl.ds(pl.multiple_of(at[block * (count // 2) + piece], size), size)
            peak = jnp.max(logits, axis=1, keepdims=True)
            exponent = jnp.exp(logits - peak)
            dlogits = line * inverse[begin : begin + size] - logits * slope[begin : begin + size]
            total = jnp.sum(exponent, axis=1, keepdims=True)
            mean = jnp.sum(exponent * dlogits, axis=1, keepdims=True) / total
            tilted = exponent * (dlogits - mean)
            both_out[0, spot, :] = exponent.astype(BF16)
            both_out[1, spot, :] = tilted.astype(BF16)
            tile[spot, :] = lanes([peak, total, mean], size)
    for begin in range(0, 2 * tokens, 128):
        stats[:, begin : begin + 128] = tile[begin : begin + 128, :].T[:8]


def soften(at, first, second, row, sums_a, sums_b, feature_count):
    tokens, width = first.shape
    rows = 2 * tokens
    return pl.pallas_call(
        functools.partial(soften_kernel, feature_count),
        in_specs=[smem_spec()] + [whole_spec()] * 5,
        out_specs=[whole_spec()] * 2,
        out_shape=[
            jax.ShapeDtypeStruct((2, rows, width), BF16),
            jax.ShapeDtypeStruct((8, rows), F32),
        ],
        scratch_shapes=[pltpu.VMEM((rows, 128), F32)],
        compiler_params=params(16),
        cost_estimate=LIGHT,
    )(at, first, second, row, sums_a, sums_b)


def order_kernel(at, *refs):
    blocks, totals, (ordered, columns) = refs[:4], refs[4:8], refs[8:]
    tokens = blocks[0].shape[0]
    count = at.shape[0]
    size = 4 * tokens // count
    half = 2 * tokens
    for block in range(4):
        inverse = 1.0 / turn(totals[block][...])
        for piece in range(count // 4):
            begin = piece * size
            place = at[block * (count // 4) + piece] + half * (block // 2)
            spot = pl.ds(pl.multiple_of(place, size), size)
            ordered[spot, :] = blocks[block][begin : begin + size, :]
            columns[spot, :] = inverse[begin : begin + size]


def order(at, blocks, totals):
    tokens, width = blocks[0].shape
    rows = 4 * tokens
    return pl.pallas_call(
        order_kernel,
        in_specs=[smem_spec()] + [whole_spec()] * 8,
        out_specs=[whole_spec()] * 2,
        out_shape=[
            jax.ShapeDtypeStruct((rows, width), BF16),
            jax.ShapeDtypeStruct((rows, 128), F32),
        ],
        compiler_params=params(12),
        cost_estimate=LIGHT,
    )(at, *blocks, *totals)


def back_kernel(deep, cotangent, head, out):
    width = head.shape[1]
    result = lax.dot_general(
        cotangent[:, :deep], head[:, :deep], NT, preferred_element_type=F32
    )
    if deep < width:
        result += lax.dot_general(
            cotangent[:, deep:], head[:, deep:], NT, preferred_element_type=F32
        )
    out[...] = result


def back(cotangent, head):
    rows, width = cotangent.shape
    features = head.shape[0]
    tile = 256 if features % 256 == 0 else features
    deep = width // 256 * 256 or width
    return pl.pallas_call(
        functools.partial(back_kernel, deep),
        grid=(features // tile,),
        in_specs=[
            pl.BlockSpec((rows, width), lambda i: (0, 0)),
            pl.BlockSpec((tile, width), lambda i: (i, 0)),
        ],
        out_specs=pl.BlockSpec((rows, tile), lambda i: (0, i)),
        out_shape=jax.ShapeDtypeStruct((rows, features), F32),
        compiler_params=params(20),
        cost_estimate=LIGHT,
    )(cotangent, head)


def merge(first, second):
    peak = jnp.maximum(first[0], second[0])
    one = jnp.exp(first[0] - peak) * first[1]
    two = jnp.exp(second[0] - peak) * second[1]
    total = one + two
    mean = (one * first[2] + two * second[2]) / total
    return jnp.stack([peak, total, mean] + [first[i] + second[i] for i in range(3, len(first))])


def exchange(value, size, beside):
    other, beside = lax.optimization_barrier((swap(value, "vocab", 1, size), beside))
    part = value.shape[1] // 4
    aligned = jnp.concatenate(
        [other[:3, i * part : (i + 1) * part] for i in (1, 0, 3, 2)], axis=1
    )
    value = merge(value, jnp.concatenate([aligned, other[3:]], axis=0))
    bit = PAIR
    while bit < size:
        value = merge(value, swap(value, "vocab", bit, size))
        bit *= 2
    return value, beside


def body(hidden, steer, tangent, gain, head, target):
    seq_size = lax.axis_size("seq")
    vocab_size = lax.axis_size("vocab")
    seq_index = lax.axis_index("seq")
    vocab_index = lax.axis_index("vocab")
    tokens, feature_count = hidden.shape
    width = head.shape[0]
    rows = seq_size * tokens
    share = rows // vocab_size
    quarter = tokens // QUARTERS
    size = min(share, quarter)
    y, z = vocab_index % PAIR, vocab_index // PAIR
    length = vocab_size // PAIR
    chip = seq_index // 2

    def destination(block, begin):
        row = (block % 2) * tokens + begin
        owner, inside = row // share, row % share
        return ((owner % PAIR) ^ y) * tokens + owner // PAIR * share + inside

    starts = jnp.arange(tokens // size) * size

    def places(bits, begins):
        return jnp.concatenate(
            [destination(seq_index ^ bit, begins) for bit in bits]
        ).astype(jnp.int32)

    own_places, other_places = places((0, 1), starts), places((2, 3), starts)
    target_places = places((0, 1, 2, 3), starts)

    at = seq_index.astype(jnp.int32)[None]
    vectors = jnp.stack([steer, tangent, gain])
    own, mate, over, sums_0, parts, two = cut(
        at, hidden, vectors, width
    )
    mate = swap(mate, "seq", 1, seq_size)
    sums_1 = swap(sums_0, "seq", 1, seq_size)
    over = swap(over, "seq", 2, seq_size)
    over_2, over_3 = over[0], swap(over[1], "seq", 1, seq_size)
    both = swap(jnp.stack([sums_0, sums_1]), "seq", 2, seq_size)
    steer_part, gain_part = parts[0], parts[2]

    def partial_logits(block, sums_of):
        radius = jnp.sqrt(sums_of[0] / feature_count + EPSILON)
        values = block.astype(F32) + steer_part
        normed = (gain_part * values / radius[:, None]).astype(BF16)
        return jnp.dot(normed, head, preferred_element_type=F32)

    given = partial_logits(mate, sums_1)
    two, given = lax.optimization_barrier((two, given))
    given = swap(given, "seq", 1, seq_size)
    row = jnp.sum(jnp.dot(two, head, preferred_element_type=F32), axis=0, keepdims=True)
    row = row + swap(row, "seq", 1, seq_size)
    summed_0 = partial_logits(own, sums_0) + given
    send_0 = summed_0.astype(jnp.float16)
    both, send_0, row = lax.optimization_barrier((both, send_0, row))
    tangent_row = row + swap(row, "seq", 2, seq_size)
    got_2 = swap(send_0, "seq", 2, seq_size)
    sums = [sums_0, sums_1, both[0], both[1]]
    denominators = [s[0] / feature_count + EPSILON for s in sums]

    blocks = [own, mate, over_2, over_3]
    given = swap(partial_logits(blocks[3], sums[3]), "seq", 1, seq_size)
    summed_2 = partial_logits(blocks[2], sums[2]) + given
    send_2, got_2, tangent_row = lax.optimization_barrier(
        (summed_2.astype(jnp.float16), got_2, tangent_row)
    )
    got_0 = swap(send_2, "seq", 2, seq_size)

    half = rows // 2

    def soften_of(base, summed, got, where):
        full = summed + got.astype(F32)
        mates = swap(full, "seq", 1, seq_size)
        both, stats = soften(
            where, full, mates, tangent_row, sums[base], sums[base + 1], feature_count
        )
        return both.reshape(2 * half, -1), stats[:3]

    def scaled_of(raw, stats, joint):
        scale = jnp.exp(stats[0] - joint[0]) / joint[1]
        lean = scale * (stats[2] - joint[2])
        plain = scale[:, None] * raw[:half]
        ggn = scale[:, None] * raw[half:] + lean[:, None] * raw[:half]
        return plain, ggn[half // 2 :].astype(BF16), ggn[: half // 2]

    both_other, stats_other = soften_of(2, summed_2, got_2, other_places)
    raw_other = back(both_other, head)
    got_0, target, raw_other, stats_other = lax.optimization_barrier(
        (got_0, target, raw_other, stats_other)
    )
    target_2 = swap(target, "seq", 2, seq_size)
    target_1 = swap(target, "seq", 1, seq_size)
    both_own, stats_own = soften_of(0, summed_0, got_0, own_places)
    own_total = jnp.sum(target.astype(F32), axis=1)
    stats = jnp.concatenate([stats_own, stats_other], axis=1)
    joint, (raw_own, target_1, target_2) = exchange(
        jnp.concatenate([stats, jnp.concatenate([own_total] * seq_size)[None]]),
        vocab_size,
        (back(both_own, head), target_1, target_2),
    )
    plain_own, theirs_own, kept_own = scaled_of(raw_own, stats_own, joint[:, :half])
    plain_other, theirs_other, kept_other = scaled_of(raw_other, stats_other, joint[:, half:])
    got_own = swap(theirs_own, "vocab", 1, vocab_size)
    got_other = swap(theirs_other, "vocab", 1, vocab_size)
    total_0 = jnp.broadcast_to(joint[3, :tokens], (8, tokens))
    total_1 = swap(total_0, "seq", 1, seq_size)
    both_totals = swap(jnp.stack([total_0, total_1]), "seq", 2, seq_size)

    target_3 = swap(target_2, "seq", 1, seq_size)
    ordered, columns = order(
        target_places,
        [target, target_1, target_2, target_3],
        [total_0, total_1, both_totals[0], both_totals[1]],
    )
    ordered, _, _ = lax.optimization_barrier((ordered, theirs_own, theirs_other))
    weighed = back(ordered, head)
    inverse = columns[:, 0:1]
    gradients = [
        plain - inverse[begin : begin + half] * weighed[begin : begin + half]
        for plain, begin in ((plain_own, 0), (plain_other, half))
    ]

    def halve(joined, bit):
        if bit < length // 2:
            joined = joined.reshape(-1, 2, share, joined.shape[-1])
            place, axis = (z // bit) % 2, 1
        else:
            joined = joined.reshape(2, -1, share, joined.shape[-1])
            place, axis = (z // bit) ^ chip, 0
        sent = lax.dynamic_index_in_dim(joined, 1 - place, axis, False)
        kept = lax.dynamic_index_in_dim(joined, place, axis, False)
        return sent.astype(BF16), kept

    chunks = []
    for begin in (0, width // 2):
        part = [g[:, begin : begin + width // 2] for g in gradients]
        chunks.append(
            (
                jnp.concatenate([p[half // 2 :] for p in part]).astype(BF16),
                jnp.concatenate([p[: half // 2] for p in part]),
            )
        )
    got_own, got_other, *sends = lax.optimization_barrier(
        (got_own, got_other, chunks[0][0], chunks[1][0])
    )
    ggn = jnp.concatenate(
        [kept_own + got_own.astype(F32), kept_other + got_other.astype(F32)], axis=0
    )
    bits = [1]
    bit = 1
    while bit < length:
        bits.append(bit * PAIR)
        bit *= 2
    items = [[1, *halve(ggn, 1)]] + [[0, sent, chunk[1]] for sent, chunk in zip(sends, chunks)]
    tick = 0
    while any(item[0] < len(bits) for item in items):
        active = [
            i for i, item in enumerate(items) if item[0] < len(bits) and i <= tick + 1
        ]
        got = [swap(items[i][1], "vocab", bits[items[i][0]], vocab_size) for i in active]
        waiting = [i for i, item in enumerate(items) if i not in active and item[0] == 0]
        tied = lax.optimization_barrier((got, [items[i][1] for i in waiting]))
        for i, value in zip(waiting, tied[1]):
            items[i][1] = value
        for i, value in zip(active, tied[0]):
            step, _, kept = items[i]
            joined = kept + value.astype(F32)
            if step + 1 < len(bits):
                items[i] = [step + 1, *halve(joined, bits[step + 1] // PAIR)]
            else:
                items[i] = [step + 1, None, joined.reshape(share, -1)]
        tick += 1
    ggn_mine = items[0][2]
    grad_mine = jnp.concatenate([items[1][2], items[2][2]], axis=1)

    first_row = vocab_index * share
    owner = first_row // tokens
    block = owner ^ seq_index

    def choose(options):
        result = options[0]
        for index in range(1, len(options)):
            result = jnp.where(block == index, options[index], result)
        return result

    def gather_rows(options):
        pieces = []
        for begin in range(0, share, size):
            inside = first_row % tokens + begin
            pieces.append(
                choose([lax.dynamic_slice_in_dim(o, inside, size, 0) for o in options])
            )
        return jnp.concatenate(pieces, axis=0)

    my_inputs = gather_rows(blocks).astype(F32) + steer_part
    my_denominator = gather_rows(denominators)
    my_radius = jnp.sqrt(my_denominator)

    scaled = [gain_part * upstream for upstream in (grad_mine, ggn_mine)]
    dotted = jnp.stack([jnp.sum(my_inputs * value, axis=1) for value in scaled])
    dotted = dotted + swap(dotted, "seq", 1, seq_size)
    dotted = dotted + swap(dotted, "seq", 2, seq_size)
    along = dotted / feature_count / my_denominator
    return tuple(
        (value - my_inputs * along[i][:, None]) / my_radius[:, None]
        for i, value in enumerate(scaled)
    )


def solution(mesh):
    return jax.shard_map(
        body,
        mesh=mesh,
        in_specs=(P("seq", None), P(), P(), P(), P("seq", "vocab"), P("seq", "vocab")),
        out_specs=(P("vocab", "seq"), P("vocab", "seq")),
        check_vma=False,
    )
```

```python
import functools

import jax
import jax.numpy as jnp
from jax import lax
from jax.experimental import pallas as pl
from jax.experimental.pallas import tpu as pltpu
from jax.sharding import PartitionSpec as P

EPSILON = 1e-06
NT = (((1,), (1,)), ((), ()))
QUARTERS = 4
PAIR = 2
LIGHT = pl.CostEstimate(flops=0, bytes_accessed=0, transcendentals=0)
F32, BF16 = jnp.float32, jnp.bfloat16


def params(mebibytes):
    return pltpu.CompilerParams(vmem_limit_bytes=mebibytes * 1024 * 1024)


def whole_spec():
    return pl.BlockSpec(memory_space=pltpu.VMEM)


def smem_spec():
    return pl.BlockSpec(memory_space=pltpu.SMEM)


def swap(value, axis, bit, size):
    return lax.ppermute(value, axis, [(i, i ^ bit) for i in range(size)])


def lanes(columns, rows):
    lane = lax.broadcasted_iota(jnp.int32, (rows, 128), 1)
    tile = jnp.zeros((rows, 128), F32)
    for index, column in enumerate(columns):
        tile = jnp.where(lane == index, column, tile)
    return tile


def turn(rows8):
    return jnp.concatenate([rows8, jnp.zeros((120, 128), F32)], axis=0).T


def cut_kernel(width, at, hidden, vectors, *outs):
    blocks, (sums, parts, two) = outs[:4], outs[4:]
    seq_index = at[0]
    rows = hidden.shape[0]
    size = rows // QUARTERS

    def features(bit):
        return pl.ds(pl.multiple_of((seq_index ^ bit) * width, width), width)

    for bit, block in enumerate(blocks):
        block[...] = hidden[:, features(bit)]
    steer, tangent = vectors[0:1, :], vectors[1:2, :]
    columns = []
    for begin in range(0, rows, size):
        inputs = hidden[begin : begin + size, :].astype(F32) + steer
        columns.append(
            lanes(
                [
                    jnp.sum(inputs * inputs, axis=1, keepdims=True),
                    jnp.sum(inputs * tangent, axis=1, keepdims=True),
                ],
                size,
            )
        )
    sums[...] = jnp.concatenate(columns, axis=0).T[:8]
    mine = vectors[:, features(0)]
    parts[...] = mine
    line = mine[1:2] * mine[2:3]
    high = line.astype(BF16).astype(F32)
    two[...] = jnp.concatenate(
        [high, line - high, jnp.zeros((14, width), F32)], axis=0
    ).astype(BF16)


def cut(at, hidden, vectors, width):
    rows = hidden.shape[0]
    block = jax.ShapeDtypeStruct((rows, width), BF16)
    return pl.pallas_call(
        functools.partial(cut_kernel, width),
        in_specs=[smem_spec(), whole_spec(), whole_spec()],
        out_specs=[whole_spec()] * 7,
        out_shape=[
            block,
            block,
            block,
            block,
            jax.ShapeDtypeStruct((8, rows), F32),
            jax.ShapeDtypeStruct((vectors.shape[0], width), F32),
            jax.ShapeDtypeStruct((16, width), BF16),
        ],
        compiler_params=params(12),
        cost_estimate=LIGHT,
    )(at, hidden, vectors)


def soften_kernel(feature_count, at, first, second, row, sums_a, sums_b, *outs):
    both_out, stats, tile = outs
    tokens = first.shape[0]
    count = at.shape[0]
    size = 2 * tokens // count
    line = row[0:1, :]
    for block, (source, sums) in enumerate(((first, sums_a), (second, sums_b))):
        turned = turn(sums[...])
        denominator = turned[:, 0:1] / feature_count + EPSILON
        inverse = 1.0 / jnp.sqrt(denominator)
        slope = turned[:, 1:2] / feature_count / denominator
        for piece in range(count // 2):
            begin = piece * size
            logits = source[begin : begin + size, :]
            spot = pl.ds(pl.multiple_of(at[block * (count // 2) + piece], size), size)
            peak = jnp.max(logits, axis=1, keepdims=True)
            exponent = jnp.exp(logits - peak)
            dlogits = line * inverse[begin : begin + size] - logits * slope[begin : begin + size]
            total = jnp.sum(exponent, axis=1, keepdims=True)
            mean = jnp.sum(exponent * dlogits, axis=1, keepdims=True) / total
            tilted = exponent * (dlogits - mean)
            both_out[0, spot, :] = exponent.astype(BF16)
            both_out[1, spot, :] = tilted.astype(BF16)
            tile[spot, :] = lanes([peak, total, mean], size)
    for begin in range(0, 2 * tokens, 128):
        stats[:, begin : begin + 128] = tile[begin : begin + 128, :].T[:8]


def soften(at, first, second, row, sums_a, sums_b, feature_count):
    tokens, width = first.shape
    rows = 2 * tokens
    return pl.pallas_call(
        functools.partial(soften_kernel, feature_count),
        in_specs=[smem_spec()] + [whole_spec()] * 5,
        out_specs=[whole_spec()] * 2,
        out_shape=[
            jax.ShapeDtypeStruct((2, rows, width), BF16),
            jax.ShapeDtypeStruct((8, rows), F32),
        ],
        scratch_shapes=[pltpu.VMEM((rows, 128), F32)],
        compiler_params=params(16),
        cost_estimate=LIGHT,
    )(at, first, second, row, sums_a, sums_b)


def order_kernel(at, *refs):
    blocks, totals, (ordered, columns) = refs[:4], refs[4:8], refs[8:]
    tokens = blocks[0].shape[0]
    count = at.shape[0]
    size = 4 * tokens // count
    half = 2 * tokens
    for block in range(4):
        inverse = 1.0 / turn(totals[block][...])
        for piece in range(count // 4):
            begin = piece * size
            place = at[block * (count // 4) + piece] + half * (block // 2)
            spot = pl.ds(pl.multiple_of(place, size), size)
            ordered[spot, :] = blocks[block][begin : begin + size, :]
            columns[spot, :] = inverse[begin : begin + size]


def order(at, blocks, totals):
    tokens, width = blocks[0].shape
    rows = 4 * tokens
    return pl.pallas_call(
        order_kernel,
        in_specs=[smem_spec()] + [whole_spec()] * 8,
        out_specs=[whole_spec()] * 2,
        out_shape=[
            jax.ShapeDtypeStruct((rows, width), BF16),
            jax.ShapeDtypeStruct((rows, 128), F32),
        ],
        compiler_params=params(12),
        cost_estimate=LIGHT,
    )(at, *blocks, *totals)


def back_kernel(deep, cotangent, head, out):
    width = head.shape[1]
    result = lax.dot_general(
        cotangent[:, :deep], head[:, :deep], NT, preferred_element_type=F32
    )
    if deep < width:
        result += lax.dot_general(
            cotangent[:, deep:], head[:, deep:], NT, preferred_element_type=F32
        )
    out[...] = result


def back(cotangent, head):
    rows, width = cotangent.shape
    features = head.shape[0]
    tile = 256 if features % 256 == 0 else features
    deep = width // 256 * 256 or width
    return pl.pallas_call(
        functools.partial(back_kernel, deep),
        grid=(features // tile,),
        in_specs=[
            pl.BlockSpec((rows, width), lambda i: (0, 0)),
            pl.BlockSpec((tile, width), lambda i: (i, 0)),
        ],
        out_specs=pl.BlockSpec((rows, tile), lambda i: (0, i)),
        out_shape=jax.ShapeDtypeStruct((rows, features), F32),
        compiler_params=params(20),
        cost_estimate=LIGHT,
    )(cotangent, head)


def merge(first, second):
    peak = jnp.maximum(first[0], second[0])
    one = jnp.exp(first[0] - peak) * first[1]
    two = jnp.exp(second[0] - peak) * second[1]
    total = one + two
    mean = (one * first[2] + two * second[2]) / total
    return jnp.stack([peak, total, mean] + [first[i] + second[i] for i in range(3, len(first))])


def exchange(value, size, beside):
    other, beside = lax.optimization_barrier((swap(value, "vocab", 1, size), beside))
    part = value.shape[1] // 4
    aligned = jnp.concatenate(
        [other[:3, i * part : (i + 1) * part] for i in (1, 0, 3, 2)], axis=1
    )
    value = merge(value, jnp.concatenate([aligned, other[3:]], axis=0))
    bit = PAIR
    while bit < size:
        value = merge(value, swap(value, "vocab", bit, size))
        bit *= 2
    return value, beside


def body(hidden, steer, tangent, gain, head, target):
    seq_size = lax.axis_size("seq")
    vocab_size = lax.axis_size("vocab")
    seq_index = lax.axis_index("seq")
    vocab_index = lax.axis_index("vocab")
    tokens, feature_count = hidden.shape
    width = head.shape[0]
    rows = seq_size * tokens
    share = rows // vocab_size
    quarter = tokens // QUARTERS
    size = min(share, quarter)
    y, z = vocab_index % PAIR, vocab_index // PAIR
    length = vocab_size // PAIR
    chip = seq_index // 2

    def destination(block, begin):
        row = (block % 2) * tokens + begin
        owner, inside = row // share, row % share
        return ((owner % PAIR) ^ y) * tokens + owner // PAIR * share + inside

    starts = jnp.arange(tokens // size) * size

    def places(bits, begins):
        return jnp.concatenate(
            [destination(seq_index ^ bit, begins) for bit in bits]
        ).astype(jnp.int32)

    own_places, other_places = places((0, 1), starts), places((2, 3), starts)
    target_places = places((0, 1, 2, 3), starts)

    at = seq_index.astype(jnp.int32)[None]
    vectors = jnp.stack([steer, tangent, gain])
    own, mate, over_2, over_3, sums_0, parts, two = cut(
        at, hidden, vectors, width
    )
    mate = swap(mate, "seq", 1, seq_size)
    sums_1 = swap(sums_0, "seq", 1, seq_size)
    over_2, over_3 = swap(over_2, "seq", 2, seq_size), swap(over_3, "seq", 3, seq_size)
    both = swap(jnp.stack([sums_0, sums_1]), "seq", 2, seq_size)
    steer_part, gain_part = parts[0], parts[2]

    def partial_logits(block, sums_of):
        radius = jnp.sqrt(sums_of[0] / feature_count + EPSILON)
        values = block.astype(F32) + steer_part
        normed = (gain_part * values / radius[:, None]).astype(BF16)
        return jnp.dot(normed, head, preferred_element_type=F32)

    given = partial_logits(mate, sums_1)
    two, given = lax.optimization_barrier((two, given))
    given = swap(given, "seq", 1, seq_size)
    row = jnp.sum(jnp.dot(two, head, preferred_element_type=F32), axis=0, keepdims=True)
    row = row + swap(row, "seq", 1, seq_size)
    tangent_row = row + swap(row, "seq", 2, seq_size)
    summed_0 = partial_logits(own, sums_0) + given
    send_0 = summed_0.astype(jnp.float16)
    both, send_0, tangent_row = lax.optimization_barrier((both, send_0, tangent_row))
    got_2 = swap(send_0, "seq", 2, seq_size)
    sums = [sums_0, sums_1, both[0], both[1]]
    denominators = [s[0] / feature_count + EPSILON for s in sums]

    blocks = [own, mate, over_2, over_3]
    given = swap(partial_logits(blocks[3], sums[3]), "seq", 1, seq_size)
    summed_2 = partial_logits(blocks[2], sums[2]) + given
    send_2, got_2 = lax.optimization_barrier((summed_2.astype(jnp.float16), got_2))
    got_0 = swap(send_2, "seq", 2, seq_size)

    half = rows // 2

    def soften_of(base, summed, got, where):
        full = summed + got.astype(F32)
        mates = swap(full, "seq", 1, seq_size)
        both, stats = soften(
            where, full, mates, tangent_row, sums[base], sums[base + 1], feature_count
        )
        return both.reshape(2 * half, -1), stats[:3]

    def scaled_of(raw, stats, joint):
        scale = jnp.exp(stats[0] - joint[0]) / joint[1]
        lean = scale * (stats[2] - joint[2])
        plain = scale[:, None] * raw[:half]
        ggn = scale[:, None] * raw[half:] + lean[:, None] * raw[:half]
        return plain, ggn[half // 2 :].astype(BF16), ggn[: half // 2]

    both_other, stats_other = soften_of(2, summed_2, got_2, other_places)
    raw_other = back(both_other, head)
    got_0, target, raw_other, stats_other = lax.optimization_barrier(
        (got_0, target, raw_other, stats_other)
    )
    target_2 = swap(target, "seq", 2, seq_size)
    target_1 = swap(target, "seq", 1, seq_size)
    both_own, stats_own = soften_of(0, summed_0, got_0, own_places)
    own_total = jnp.sum(target.astype(F32), axis=1)
    stats = jnp.concatenate([stats_own, stats_other], axis=1)
    joint, (raw_own, target_1, target_2) = exchange(
        jnp.concatenate([stats, jnp.concatenate([own_total] * seq_size)[None]]),
        vocab_size,
        (
            lax.dot_general(both_own, head, NT, preferred_element_type=F32),
            target_1,
            target_2,
        ),
    )
    plain_own, theirs_own, kept_own = scaled_of(raw_own, stats_own, joint[:, :half])
    plain_other, theirs_other, kept_other = scaled_of(raw_other, stats_other, joint[:, half:])
    got_own = swap(theirs_own, "vocab", 1, vocab_size)
    got_other = swap(theirs_other, "vocab", 1, vocab_size)
    total_0 = jnp.broadcast_to(joint[3, :tokens], (8, tokens))
    total_1 = swap(total_0, "seq", 1, seq_size)
    both_totals = swap(jnp.stack([total_0, total_1]), "seq", 2, seq_size)

    target_3 = swap(target_2, "seq", 1, seq_size)
    ordered, columns = order(
        target_places,
        [target, target_1, target_2, target_3],
        [total_0, total_1, both_totals[0], both_totals[1]],
    )
    ordered, _, _ = lax.optimization_barrier((ordered, theirs_own, theirs_other))
    weighed = back(ordered, head)
    inverse = columns[:, 0:1]
    gradients = [
        plain - inverse[begin : begin + half] * weighed[begin : begin + half]
        for plain, begin in ((plain_own, 0), (plain_other, half))
    ]

    def halve(joined, bit):
        if bit < length // 2:
            joined = joined.reshape(-1, 2, share, joined.shape[-1])
            place, axis = (z // bit) % 2, 1
        else:
            joined = joined.reshape(2, -1, share, joined.shape[-1])
            place, axis = (z // bit) ^ chip, 0
        sent = lax.dynamic_index_in_dim(joined, 1 - place, axis, False)
        kept = lax.dynamic_index_in_dim(joined, place, axis, False)
        return sent.astype(BF16), kept

    chunks = []
    for begin in (0, width // 2):
        part = [g[:, begin : begin + width // 2] for g in gradients]
        chunks.append(
            (
                jnp.concatenate([p[half // 2 :] for p in part]).astype(BF16),
                jnp.concatenate([p[: half // 2] for p in part]),
            )
        )
    got_own, got_other, *sends = lax.optimization_barrier(
        (got_own, got_other, chunks[0][0], chunks[1][0])
    )
    ggn = jnp.concatenate(
        [kept_own + got_own.astype(F32), kept_other + got_other.astype(F32)], axis=0
    )
    bits = [1]
    bit = 1
    while bit < length:
        bits.append(bit * PAIR)
        bit *= 2
    items = [[1, *halve(ggn, 1)]] + [[0, sent, chunk[1]] for sent, chunk in zip(sends, chunks)]
    tick = 0
    while any(item[0] < len(bits) for item in items):
        active = [
            i for i, item in enumerate(items) if item[0] < len(bits) and i <= tick + 1
        ]
        got = [swap(items[i][1], "vocab", bits[items[i][0]], vocab_size) for i in active]
        waiting = [i for i, item in enumerate(items) if i not in active and item[0] == 0]
        tied = lax.optimization_barrier((got, [items[i][1] for i in waiting]))
        for i, value in zip(waiting, tied[1]):
            items[i][1] = value
        for i, value in zip(active, tied[0]):
            step, _, kept = items[i]
            joined = kept + value.astype(F32)
            if step + 1 < len(bits):
                items[i] = [step + 1, *halve(joined, bits[step + 1] // PAIR)]
            else:
                items[i] = [step + 1, None, joined.reshape(share, -1)]
        tick += 1
    ggn_mine = items[0][2]
    grad_mine = jnp.concatenate([items[1][2], items[2][2]], axis=1)

    first_row = vocab_index * share
    owner = first_row // tokens
    block = owner ^ seq_index

    def choose(options):
        result = options[0]
        for index in range(1, len(options)):
            result = jnp.where(block == index, options[index], result)
        return result

    def gather_rows(options):
        pieces = []
        for begin in range(0, share, size):
            inside = first_row % tokens + begin
            pieces.append(
                choose([lax.dynamic_slice_in_dim(o, inside, size, 0) for o in options])
            )
        return jnp.concatenate(pieces, axis=0)

    my_inputs = gather_rows(blocks).astype(F32) + steer_part
    my_denominator = gather_rows(denominators)
    my_radius = jnp.sqrt(my_denominator)

    scaled = [gain_part * upstream for upstream in (grad_mine, ggn_mine)]
    dotted = jnp.stack([jnp.sum(my_inputs * value, axis=1) for value in scaled])
    dotted = dotted + swap(dotted, "seq", 1, seq_size)
    dotted = dotted + swap(dotted, "seq", 2, seq_size)
    along = dotted / feature_count / my_denominator
    return tuple(
        (value - my_inputs * along[i][:, None]) / my_radius[:, None]
        for i, value in enumerate(scaled)
    )


def solution(mesh):
    return jax.shard_map(
        body,
        mesh=mesh,
        in_specs=(P("seq", None), P(), P(), P(), P("seq", "vocab"), P("seq", "vocab")),
        out_specs=(P("vocab", "seq"), P("vocab", "seq")),
        check_vma=False,
    )
```

```python
import functools

import jax
import jax.numpy as jnp
from jax import lax
from jax.experimental import pallas as pl
from jax.experimental.pallas import tpu as pltpu
from jax.sharding import PartitionSpec as P

EPSILON = 1e-06
NT = (((1,), (1,)), ((), ()))
QUARTERS = 4
PAIR = 2
LIGHT = pl.CostEstimate(flops=0, bytes_accessed=0, transcendentals=0)
F32, BF16 = jnp.float32, jnp.bfloat16


def params(mebibytes):
    return pltpu.CompilerParams(vmem_limit_bytes=mebibytes * 1024 * 1024)


def whole_spec():
    return pl.BlockSpec(memory_space=pltpu.VMEM)


def smem_spec():
    return pl.BlockSpec(memory_space=pltpu.SMEM)


def swap(value, axis, bit, size):
    return lax.ppermute(value, axis, [(i, i ^ bit) for i in range(size)])


def lanes(columns, rows):
    lane = lax.broadcasted_iota(jnp.int32, (rows, 128), 1)
    tile = jnp.zeros((rows, 128), F32)
    for index, column in enumerate(columns):
        tile = jnp.where(lane == index, column, tile)
    return tile


def turn(rows8):
    return jnp.concatenate([rows8, jnp.zeros((120, 128), F32)], axis=0).T


def cut_kernel(width, at, hidden, vectors, *outs):
    blocks, (sums, parts, two) = outs[:4], outs[4:]
    seq_index = at[0]
    rows = hidden.shape[0]
    size = rows // QUARTERS

    def features(bit):
        return pl.ds(pl.multiple_of((seq_index ^ bit) * width, width), width)

    for bit, block in enumerate(blocks):
        block[...] = hidden[:, features(bit)]
    steer, tangent = vectors[0:1, :], vectors[1:2, :]
    columns = []
    for begin in range(0, rows, size):
        inputs = hidden[begin : begin + size, :].astype(F32) + steer
        columns.append(
            lanes(
                [
                    jnp.sum(inputs * inputs, axis=1, keepdims=True),
                    jnp.sum(inputs * tangent, axis=1, keepdims=True),
                ],
                size,
            )
        )
    sums[...] = jnp.concatenate(columns, axis=0).T[:8]
    mine = vectors[:, features(0)]
    parts[...] = mine
    line = mine[1:2] * mine[2:3]
    high = line.astype(BF16).astype(F32)
    two[...] = jnp.concatenate(
        [high, line - high, jnp.zeros((14, width), F32)], axis=0
    ).astype(BF16)


def cut(at, hidden, vectors, width):
    rows = hidden.shape[0]
    block = jax.ShapeDtypeStruct((rows, width), BF16)
    return pl.pallas_call(
        functools.partial(cut_kernel, width),
        in_specs=[smem_spec(), whole_spec(), whole_spec()],
        out_specs=[whole_spec()] * 7,
        out_shape=[
            block,
            block,
            block,
            block,
            jax.ShapeDtypeStruct((8, rows), F32),
            jax.ShapeDtypeStruct((vectors.shape[0], width), F32),
            jax.ShapeDtypeStruct((16, width), BF16),
        ],
        compiler_params=params(12),
        cost_estimate=LIGHT,
    )(at, hidden, vectors)


def soften_kernel(feature_count, at, first, second, row, sums_a, sums_b, *outs):
    both_out, stats, tile = outs
    tokens = first.shape[0]
    count = at.shape[0]
    size = 2 * tokens // count
    line = row[0:1, :]
    for block, (source, sums) in enumerate(((first, sums_a), (second, sums_b))):
        turned = turn(sums[...])
        denominator = turned[:, 0:1] / feature_count + EPSILON
        inverse = 1.0 / jnp.sqrt(denominator)
        slope = turned[:, 1:2] / feature_count / denominator
        for piece in range(count // 2):
            begin = piece * size
            logits = source[begin : begin + size, :]
            spot = pl.ds(pl.multiple_of(at[block * (count // 2) + piece], size), size)
            peak = jnp.max(logits, axis=1, keepdims=True)
            exponent = jnp.exp(logits - peak)
            dlogits = line * inverse[begin : begin + size] - logits * slope[begin : begin + size]
            total = jnp.sum(exponent, axis=1, keepdims=True)
            mean = jnp.sum(exponent * dlogits, axis=1, keepdims=True) / total
            tilted = exponent * (dlogits - mean)
            both_out[0, spot, :] = exponent.astype(BF16)
            both_out[1, spot, :] = tilted.astype(BF16)
            tile[spot, :] = lanes([peak, total, mean], size)
    for begin in range(0, 2 * tokens, 128):
        stats[:, begin : begin + 128] = tile[begin : begin + 128, :].T[:8]


def soften(at, first, second, row, sums_a, sums_b, feature_count):
    tokens, width = first.shape
    rows = 2 * tokens
    return pl.pallas_call(
        functools.partial(soften_kernel, feature_count),
        in_specs=[smem_spec()] + [whole_spec()] * 5,
        out_specs=[whole_spec()] * 2,
        out_shape=[
            jax.ShapeDtypeStruct((2, rows, width), BF16),
            jax.ShapeDtypeStruct((8, rows), F32),
        ],
        scratch_shapes=[pltpu.VMEM((rows, 128), F32)],
        compiler_params=params(16),
        cost_estimate=LIGHT,
    )(at, first, second, row, sums_a, sums_b)


def order_kernel(at, *refs):
    blocks, totals, (ordered, columns) = refs[:4], refs[4:8], refs[8:]
    tokens = blocks[0].shape[0]
    count = at.shape[0]
    size = 4 * tokens // count
    half = 2 * tokens
    for block in range(4):
        inverse = 1.0 / turn(totals[block][...])
        for piece in range(count // 4):
            begin = piece * size
            place = at[block * (count // 4) + piece] + half * (block // 2)
            spot = pl.ds(pl.multiple_of(place, size), size)
            ordered[spot, :] = blocks[block][begin : begin + size, :]
            columns[spot, :] = inverse[begin : begin + size]


def order(at, blocks, totals):
    tokens, width = blocks[0].shape
    rows = 4 * tokens
    return pl.pallas_call(
        order_kernel,
        in_specs=[smem_spec()] + [whole_spec()] * 8,
        out_specs=[whole_spec()] * 2,
        out_shape=[
            jax.ShapeDtypeStruct((rows, width), BF16),
            jax.ShapeDtypeStruct((rows, 128), F32),
        ],
        compiler_params=params(12),
        cost_estimate=LIGHT,
    )(at, *blocks, *totals)


def back_kernel(deep, cotangent, head, out):
    width = head.shape[1]
    result = lax.dot_general(
        cotangent[:, :deep], head[:, :deep], NT, preferred_element_type=F32
    )
    if deep < width:
        result += lax.dot_general(
            cotangent[:, deep:], head[:, deep:], NT, preferred_element_type=F32
        )
    out[...] = result


def back(cotangent, head):
    rows, width = cotangent.shape
    features = head.shape[0]
    tile = 256 if features % 256 == 0 else features
    deep = width // 256 * 256 or width
    return pl.pallas_call(
        functools.partial(back_kernel, deep),
        grid=(features // tile,),
        in_specs=[
            pl.BlockSpec((rows, width), lambda i: (0, 0)),
            pl.BlockSpec((tile, width), lambda i: (i, 0)),
        ],
        out_specs=pl.BlockSpec((rows, tile), lambda i: (0, i)),
        out_shape=jax.ShapeDtypeStruct((rows, features), F32),
        compiler_params=params(20),
        cost_estimate=LIGHT,
    )(cotangent, head)


def merge(first, second):
    peak = jnp.maximum(first[0], second[0])
    one = jnp.exp(first[0] - peak) * first[1]
    two = jnp.exp(second[0] - peak) * second[1]
    total = one + two
    mean = (one * first[2] + two * second[2]) / total
    return jnp.stack([peak, total, mean] + [first[i] + second[i] for i in range(3, len(first))])


def exchange(value, size, beside):
    other, beside = lax.optimization_barrier((swap(value, "vocab", 1, size), beside))
    part = value.shape[1] // 4
    aligned = jnp.concatenate(
        [other[:3, i * part : (i + 1) * part] for i in (1, 0, 3, 2)], axis=1
    )
    value = merge(value, jnp.concatenate([aligned, other[3:]], axis=0))
    bit = PAIR
    while bit < size:
        value = merge(value, swap(value, "vocab", bit, size))
        bit *= 2
    return value, beside


def body(hidden, steer, tangent, gain, head, target):
    seq_size = lax.axis_size("seq")
    vocab_size = lax.axis_size("vocab")
    seq_index = lax.axis_index("seq")
    vocab_index = lax.axis_index("vocab")
    tokens, feature_count = hidden.shape
    width = head.shape[0]
    rows = seq_size * tokens
    share = rows // vocab_size
    quarter = tokens // QUARTERS
    size = min(share, quarter)
    y, z = vocab_index % PAIR, vocab_index // PAIR
    length = vocab_size // PAIR
    chip = seq_index // 2

    def destination(block, begin):
        row = (block % 2) * tokens + begin
        owner, inside = row // share, row % share
        return ((owner % PAIR) ^ y) * tokens + owner // PAIR * share + inside

    starts = jnp.arange(tokens // size) * size

    def places(bits, begins):
        return jnp.concatenate(
            [destination(seq_index ^ bit, begins) for bit in bits]
        ).astype(jnp.int32)

    own_places, other_places = places((0, 1), starts), places((2, 3), starts)
    target_places = places((0, 1, 2, 3), starts)

    at = seq_index.astype(jnp.int32)[None]
    vectors = jnp.stack([steer, tangent, gain])
    own, mate, over_2, over_3, sums_0, parts, two = cut(
        at, hidden, vectors, width
    )
    mate = swap(mate, "seq", 1, seq_size)
    sums_1 = swap(sums_0, "seq", 1, seq_size)
    over_2, over_3 = swap(over_2, "seq", 2, seq_size), swap(over_3, "seq", 3, seq_size)
    both = swap(jnp.stack([sums_0, sums_1]), "seq", 2, seq_size)
    steer_part, gain_part = parts[0], parts[2]

    def partial_logits(block, sums_of):
        radius = jnp.sqrt(sums_of[0] / feature_count + EPSILON)
        values = block.astype(F32) + steer_part
        normed = (gain_part * values / radius[:, None]).astype(BF16)
        return jnp.dot(normed, head, preferred_element_type=F32)

    given = partial_logits(mate, sums_1)
    two, given = lax.optimization_barrier((two, given))
    given = swap(given, "seq", 1, seq_size)
    row = jnp.sum(jnp.dot(two, head, preferred_element_type=F32), axis=0, keepdims=True)
    row = row + swap(row, "seq", 1, seq_size)
    tangent_row = row + swap(row, "seq", 2, seq_size)
    summed_0 = partial_logits(own, sums_0) + given
    send_0 = summed_0.astype(jnp.float16)
    both, send_0, tangent_row = lax.optimization_barrier((both, send_0, tangent_row))
    got_2 = swap(send_0, "seq", 2, seq_size)
    sums = [sums_0, sums_1, both[0], both[1]]
    denominators = [s[0] / feature_count + EPSILON for s in sums]

    blocks = [own, mate, over_2, over_3]
    given = swap(partial_logits(blocks[3], sums[3]), "seq", 1, seq_size)
    summed_2 = partial_logits(blocks[2], sums[2]) + given
    send_2, got_2 = lax.optimization_barrier((summed_2.astype(jnp.float16), got_2))
    got_0 = swap(send_2, "seq", 2, seq_size)

    half = rows // 2

    def soften_of(base, summed, got, where):
        full = summed + got.astype(F32)
        mates = swap(full, "seq", 1, seq_size)
        both, stats = soften(
            where, full, mates, tangent_row, sums[base], sums[base + 1], feature_count
        )
        return both.reshape(2 * half, -1), stats[:3]

    def scaled_of(raw, stats, joint):
        scale = jnp.exp(stats[0] - joint[0]) / joint[1]
        lean = scale * (stats[2] - joint[2])
        plain = scale[:, None] * raw[:half]
        ggn = scale[:, None] * raw[half:] + lean[:, None] * raw[:half]
        return plain, ggn[half // 2 :].astype(BF16), ggn[: half // 2]

    both_other, stats_other = soften_of(2, summed_2, got_2, other_places)
    raw_other = back(both_other, head)
    got_0, target, raw_other, stats_other = lax.optimization_barrier(
        (got_0, target, raw_other, stats_other)
    )
    target_2 = swap(target, "seq", 2, seq_size)
    target_1 = swap(target, "seq", 1, seq_size)
    both_own, stats_own = soften_of(0, summed_0, got_0, own_places)
    own_total = jnp.sum(target.astype(F32), axis=1)
    stats = jnp.concatenate([stats_own, stats_other], axis=1)
    joint, (raw_own, target_1, target_2) = exchange(
        jnp.concatenate([stats, jnp.concatenate([own_total] * seq_size)[None]]),
        vocab_size,
        (
            lax.dot_general(both_own, head, NT, preferred_element_type=F32),
            target_1,
            target_2,
        ),
    )
    plain_own, theirs_own, kept_own = scaled_of(raw_own, stats_own, joint[:, :half])
    plain_other, theirs_other, kept_other = scaled_of(raw_other, stats_other, joint[:, half:])
    got_own = swap(theirs_own, "vocab", 1, vocab_size)
    got_other = swap(theirs_other, "vocab", 1, vocab_size)
    total_0 = jnp.broadcast_to(joint[3, :tokens], (8, tokens))
    total_1 = swap(total_0, "seq", 1, seq_size)
    both_totals = swap(jnp.stack([total_0, total_1]), "seq", 2, seq_size)

    target_3 = swap(target_2, "seq", 1, seq_size)
    ordered, columns = order(
        target_places,
        [target, target_1, target_2, target_3],
        [total_0, total_1, both_totals[0], both_totals[1]],
    )
    ordered, _, _ = lax.optimization_barrier((ordered, theirs_own, theirs_other))
    weighed = back(ordered, head)
    inverse = columns[:, 0:1]
    gradients = [
        plain - inverse[begin : begin + half] * weighed[begin : begin + half]
        for plain, begin in ((plain_own, 0), (plain_other, half))
    ]

    def halve(joined, bit):
        if bit < length // 2:
            joined = joined.reshape(-1, 2, share, joined.shape[-1])
            place, axis = (z // bit) % 2, 1
        else:
            joined = joined.reshape(2, -1, share, joined.shape[-1])
            place, axis = (z // bit) ^ chip, 0
        sent = lax.dynamic_index_in_dim(joined, 1 - place, axis, False)
        kept = lax.dynamic_index_in_dim(joined, place, axis, False)
        return sent.astype(BF16), kept

    chunks = []
    for begin in (0, width // 2):
        part = [g[:, begin : begin + width // 2] for g in gradients]
        chunks.append(
            (
                jnp.concatenate([p[half // 2 :] for p in part]).astype(BF16),
                jnp.concatenate([p[: half // 2] for p in part]),
            )
        )
    got_own, got_other, *sends = lax.optimization_barrier(
        (got_own, got_other, chunks[0][0], chunks[1][0])
    )
    ggn = jnp.concatenate(
        [kept_own + got_own.astype(F32), kept_other + got_other.astype(F32)], axis=0
    )
    bits = [1]
    bit = 1
    while bit < length:
        bits.append(bit * PAIR)
        bit *= 2
    items = [[1, *halve(ggn, 1)]] + [[0, sent, chunk[1]] for sent, chunk in zip(sends, chunks)]
    tick = 0
    while any(item[0] < len(bits) for item in items):
        active = [
            i for i, item in enumerate(items) if item[0] < len(bits) and i <= tick + 1
        ]
        got = [swap(items[i][1], "vocab", bits[items[i][0]], vocab_size) for i in active]
        waiting = [i for i, item in enumerate(items) if i not in active and item[0] == 0]
        tied = (got, [])
        if waiting:
            tied = lax.optimization_barrier((got, [items[i][1] for i in waiting]))
        for i, value in zip(waiting, tied[1]):
            items[i][1] = value
        for i, value in zip(active, tied[0]):
            step, _, kept = items[i]
            joined = kept + value.astype(F32)
            if step + 1 < len(bits):
                items[i] = [step + 1, *halve(joined, bits[step + 1] // PAIR)]
            else:
                items[i] = [step + 1, None, joined.reshape(share, -1)]
        tick += 1
    ggn_mine = items[0][2]
    grad_mine = jnp.concatenate([items[1][2], items[2][2]], axis=1)

    first_row = vocab_index * share
    owner = first_row // tokens
    block = owner ^ seq_index

    def choose(options):
        result = options[0]
        for index in range(1, len(options)):
            result = jnp.where(block == index, options[index], result)
        return result

    def gather_rows(options):
        pieces = []
        for begin in range(0, share, size):
            inside = first_row % tokens + begin
            pieces.append(
                choose([lax.dynamic_slice_in_dim(o, inside, size, 0) for o in options])
            )
        return jnp.concatenate(pieces, axis=0)

    my_inputs = gather_rows(blocks).astype(F32) + steer_part
    my_denominator = gather_rows(denominators)
    my_radius = jnp.sqrt(my_denominator)

    scaled = [gain_part * upstream for upstream in (grad_mine, ggn_mine)]
    dotted = jnp.stack([jnp.sum(my_inputs * value, axis=1) for value in scaled])
    dotted = dotted + swap(dotted, "seq", 1, seq_size)
    dotted = dotted + swap(dotted, "seq", 2, seq_size)
    along = dotted / feature_count / my_denominator
    return tuple(
        (value - my_inputs * along[i][:, None]) / my_radius[:, None]
        for i, value in enumerate(scaled)
    )


def solution(mesh):
    return jax.shard_map(
        body,
        mesh=mesh,
        in_specs=(P("seq", None), P(), P(), P(), P("seq", "vocab"), P("seq", "vocab")),
        out_specs=(P("vocab", "seq"), P("vocab", "seq")),
        check_vma=False,
    )
```
